32 devices in a mesh: clip: 2 (over x), row: 16 (over z, y, core).
Axes of the slice: x: 2, y: 2, z: 4, core: 2. Of those that a mesh axis runs over, the one named last changes fastest.
Arguments:
- source: bfloat16 [32768, 256], P(('clip', 'row')), parts along dimension 0, may hold values from -6 to 6
- near_blocks: bfloat16 [128, 16, 256, 256], P(('clip', 'row')), parts along dimension 0, may hold values from -0.125 to 0.125
- near_list: int32 [128, 16], P(('clip', 'row')), parts along dimension 0, may hold values from 0 to 63, as said below
- near_count: int32 [128], P(('clip', 'row')), parts along dimension 0, may hold values from 1 to 16
- col_basis: bfloat16 [128, 256, 128], P(('clip', 'row')), parts along dimension 0, may hold values from -0.375 to 0.375
- row_basis: bfloat16 [128, 256, 128], P(('clip', 'row')), parts along dimension 0, may hold values from -0.5 to 0.5
- transfer: bfloat16 [128, 128, 128], P(('clip', 'row')), parts along dimension 0, may hold values from -0.25 to 0.25
- far_list: int32 [128, 16], P(('clip', 'row')), parts along dimension 0, may hold values from 0 to 63, as said below
- far_coupling: bfloat16 [128, 16, 128, 128], P(('clip', 'row')), parts along dimension 0, may hold values from -0.125 to 0.125
- coarse_list: int32 [32, 8], P(('clip', 'row')), parts along dimension 0, may hold values from 0 to 15, as said below
- coarse_coupling: bfloat16 [32, 8, 128, 128], P(('clip', 'row')), parts along dimension 0, may hold values from -0.375 to 0.375
Outputs:
- product: bfloat16 [32768, 256], P(('clip', 'row')), parts along dimension 0
The draws below stay inside these ranges and needn't reach their ends.
There are 2 independent parts, one for each index of `clip`. The reference program is written for one: setup_inputs(seed, part) draws one part's arguments, and reference() takes and returns one part's arrays. A program takes and returns all parts, laid end to end along the dimension named above; each array names one. Nothing has to cross between parts.
Inputs may be any that keep to these rules, and one draw needn't show every extreme that they name: near_list[i, 0] = i; the other entries lie within 4 leaves of i. far_list[i, f] lies in a coarse cluster one or two clusters away from that of leaf i. coarse_list[d, m] lies in the same aligned group of 16 coarse clusters as d, and its position in the group differs from that of d by three or more modulo 16.
All inputs are finite; a program needn't handle non-finite values.
Results may differ from the reference program's by a relative error of at most 0.0057.
Values may be sent and summed in bfloat16 or wider, within the bound.
No kernel may reach another device: no remote copies, remote signals or barrier semaphores. Data moves between devices by JAX's collectives and lax.ppermute only.
A program may use at most 128 MiB of HBM per device.

```python
import jax
import jax.numpy as jnp
from jax import lax

LEAF = 256
RANK = 128
RHS = 256
LEAF_DEV = 4
NEAR_SLOTS = 16
FAR_SLOTS = 16
COARSE_SLOTS = 8
LEAF_CLUSTERS = 64
ROWS = 16384
N_ROW = 16


def draw_near_list(key, part):
    key = jax.random.fold_in(key, 11)
    first, second = jax.random.split(key)
    rows = jnp.arange(LEAF_CLUSTERS, dtype=jnp.int32)[:, None]
    magnitude = jax.random.randint(first, (LEAF_CLUSTERS, NEAR_SLOTS - 1), 1, LEAF_DEV + 1)
    sign = 2 * jax.random.randint(second, (LEAF_CLUSTERS, NEAR_SLOTS - 1), 0, 2) - 1
    offset = magnitude * sign
    target = rows + offset
    target = jnp.where((target < 0) | (target >= LEAF_CLUSTERS), rows - offset, target)
    return jnp.concatenate([rows, target], axis=1).astype(jnp.int32)


def draw_far_list(key, part):
    key = jax.random.fold_in(key, 23)
    first, second = jax.random.split(key)
    cluster_index = (jnp.arange(LEAF_CLUSTERS, dtype=jnp.int32) // LEAF_DEV)[:, None]
    pick = jax.random.randint(first, (LEAF_CLUSTERS, FAR_SLOTS), 0, 4)
    offset = jnp.array([-2, -1, 1, 2], dtype=jnp.int32)[pick]
    other = cluster_index + offset
    other = jnp.where((other < 0) | (other >= N_ROW), cluster_index - offset, other)
    cluster_member = jax.random.randint(second, (LEAF_CLUSTERS, FAR_SLOTS), 0, LEAF_DEV)
    return (other * LEAF_DEV + cluster_member).astype(jnp.int32)


def draw_coarse_list(key, part):
    key = jax.random.fold_in(key, 37)
    cluster_index = jnp.arange(N_ROW, dtype=jnp.int32)[:, None]
    base = cluster_index - cluster_index % 16
    step = jax.random.randint(key, (N_ROW, COARSE_SLOTS), 0, 11)
    return (base + (cluster_index % 16 + 3 + step) % 16).astype(jnp.int32)


def set_ends(values, key, low, largest):
    spot = [jax.random.randint(jax.random.fold_in(key, axis), (), 0, length) for axis, length in enumerate(values.shape)]
    widest = values.shape.index(max(values.shape))
    beside = spot[:widest] + [(spot[widest] + 1) % values.shape[widest]] + spot[widest + 1:]
    return values.at[tuple(spot)].set(low).at[tuple(beside)].set(largest)


def steps_of(key, shape, cuts, low, high):
    def one(dim, blocks):
        draws = jax.random.uniform(jax.random.fold_in(jax.random.fold_in(key, 6), dim), (blocks,), jnp.float32, low / len(cuts), high / len(cuts))
        return jnp.repeat(jnp.exp(draws), shape[dim] // blocks).reshape((-1,) + (1,) * (len(shape) - dim - 1))

    factor_of = one(*cuts[0])
    for cut in cuts[1:]:
        factor_of = factor_of * one(*cut)
    return factor_of


def bell_draw(own_key, extent, scale, most, shards=(), kind=jnp.bfloat16):
    values = jax.random.normal(own_key, extent, jnp.float32) * scale
    if len(shards) > 0:
        values = steps_of(own_key, extent, shards, -0.22, 0.18) * values
    return jnp.clip(values, min=-most, max=most).astype(kind)


def setup_inputs(seed: int = 0, part: int = 0) -> dict:
    streams_of = jax.random.split(jax.random.key(seed), 12)
    own_keys = jax.random.split(jax.random.fold_in(streams_of[11], part), 12)
    source = bell_draw(own_keys[0], (ROWS, RHS), 1.0, 6.0, ((0, 16),))
    near_blocks = bell_draw(own_keys[1], (LEAF_CLUSTERS, NEAR_SLOTS, LEAF, LEAF), (LEAF * NEAR_SLOTS // 2) ** -0.5, 0.125, ((0, 16),))
    near_list = draw_near_list(jax.random.fold_in(jax.random.fold_in(streams_of[11], part), 71), part)
    near_count = set_ends(jax.random.randint(own_keys[3], (LEAF_CLUSTERS,), 1, NEAR_SLOTS + 1), jax.random.fold_in(own_keys[3], 1), 1, NEAR_SLOTS).astype(jnp.int32)
    col_basis = bell_draw(own_keys[4], (LEAF_CLUSTERS, LEAF, RANK), LEAF ** -0.5, 0.375, ((0, 16),))
    row_basis = bell_draw(own_keys[5], (LEAF_CLUSTERS, LEAF, RANK), RANK ** -0.5, 0.5, ((0, 16),))
    transfer = bell_draw(own_keys[6], (LEAF_CLUSTERS, RANK, RANK), (RANK * LEAF_DEV) ** -0.5, 0.25, ((0, 16),))
    far_list = draw_far_list(jax.random.fold_in(jax.random.fold_in(streams_of[11], part), 71), part)
    far_coupling = bell_draw(own_keys[8], (LEAF_CLUSTERS, FAR_SLOTS, RANK, RANK), (RANK * FAR_SLOTS) ** -0.5, 0.125, ((0, 16),))
    coarse_list = draw_coarse_list(jax.random.fold_in(jax.random.fold_in(streams_of[11], part), 71), part)
    coarse_coupling = bell_draw(own_keys[10], (N_ROW, COARSE_SLOTS, RANK, RANK), (RANK * COARSE_SLOTS // 4) ** -0.5, 0.375, ((0, 16),))
    return dict(source=source, near_blocks=near_blocks, near_list=near_list, near_count=near_count, col_basis=col_basis, row_basis=row_basis, transfer=transfer, far_list=far_list, far_coupling=far_coupling, coarse_list=coarse_list, coarse_coupling=coarse_coupling)


def reference(source, near_blocks, near_list, near_count, col_basis, row_basis, transfer, far_list, far_coupling, coarse_list, coarse_coupling):
    panels = source.reshape(LEAF_CLUSTERS, LEAF, RHS)

    def near_one(items):
        block_list, column_count, count = items
        selected_entries = panels[column_count]
        live = jnp.arange(NEAR_SLOTS, dtype=jnp.int32) < count
        selected_entries = jnp.where(live[:, None, None], selected_entries, jnp.zeros_like(selected_entries))
        return jnp.einsum('nhd,ndu->hu', block_list.astype(jnp.float32), selected_entries.astype(jnp.float32))

    near = lax.map(near_one, (near_blocks, near_list, near_count))
    coef = jnp.einsum('lak,lar->lkr', col_basis.astype(jnp.float32), panels.astype(jnp.float32)).astype(jnp.bfloat16)
    grouped = transfer.reshape(N_ROW, LEAF_DEV, RANK, RANK).astype(jnp.float32)
    parent = jnp.einsum('dlab,dlar->dbr', grouped, coef.reshape(N_ROW, LEAF_DEV, RANK, RHS).astype(jnp.float32)).astype(jnp.bfloat16)

    def single_far_block(items):
        coupling, sources = items
        return jnp.einsum('fab,fbr->ar', coupling.astype(jnp.float32), coef[sources].astype(jnp.float32))

    leaf_far = lax.map(single_far_block, (far_coupling, far_list))
    coarse = jnp.einsum('dmab,dmbr->dar', coarse_coupling.astype(jnp.float32), parent[coarse_list].astype(jnp.float32))
    spread = jnp.einsum('dlab,dbr->dlar', grouped, coarse, precision=lax.Precision.HIGHEST).reshape(LEAF_CLUSTERS, RANK, RHS)
    down = (leaf_far + spread).astype(jnp.bfloat16)
    result = near + jnp.einsum('lka,lar->lkr', row_basis.astype(jnp.float32), down.astype(jnp.float32))
    return result.reshape(ROWS, RHS).astype(jnp.bfloat16)
```

```python
import jax
import jax.numpy as jnp
from jax import lax
from jax.experimental import pallas as pl
from jax.experimental.pallas import tpu as pltpu
from jax.sharding import PartitionSpec as P

GROUP = 16
CHUNK = 4


def dot(a, b):
    return jnp.dot(a, b, preferred_element_type=jnp.float32)


def dot_t(a, b):
    return lax.dot_general(
        a, b, (((0,), (0,)), ((), ())), preferred_element_type=jnp.float32
    )


def up_kernel(source_ref, col_ref, transfer_ref, coef_ref, parent_ref):
    leaves, rows, rank = col_ref.shape
    total = None
    for leaf in range(leaves):
        coef = dot_t(col_ref[leaf], source_ref[pl.ds(leaf * rows, rows), :]).astype(jnp.bfloat16)
        coef_ref[leaf] = coef
        term = dot_t(transfer_ref[leaf], coef)
        total = term if total is None else total + term
    parent_ref[...] = total.astype(jnp.bfloat16)


def near_kernel(
    list_ref, count_ref, blocks_hbm, own_hbm, other_hbm, across_hbm, near_ref,
    blocks, panels, block_sems, panel_sems,
):
    leaves, slots, rows, _ = blocks.shape
    chunks = slots // CHUNK
    place = list_ref[0, 0] // leaves
    pairs = [
        pltpu.make_async_copy(
            ref, panels.at[pl.ds(which * leaves, leaves)], panel_sems.at[which]
        )
        for which, ref in enumerate((own_hbm, other_hbm, across_hbm))
    ]
    for copy in pairs:
        copy.start()

    def block_copy(leaf, chunk):
        where = pl.ds(chunk * CHUNK, CHUNK)
        return pltpu.make_async_copy(
            blocks_hbm.at[leaf, where], blocks.at[leaf, where], block_sems.at[leaf, chunk]
        )

    for leaf in range(leaves):
        for chunk in range(chunks):
            @pl.when(chunk * CHUNK < count_ref[leaf])
            def _():
                block_copy(leaf, chunk).start()

    panels[3 * leaves] = jnp.zeros(panels.shape[1:], panels.dtype)
    for copy in pairs:
        copy.wait()

    def panel_of(leaf, slot):
        column = list_ref[leaf, slot]
        cluster = column // leaves
        which = jnp.where(cluster == place, 0, jnp.where(cluster == (place ^ 1), 1, 2))
        index = which * leaves + column - cluster * leaves
        return panels[jnp.where(slot < count_ref[leaf], index, 3 * leaves)]

    for leaf in range(leaves):
        for chunk in range(chunks):
            @pl.when(chunk * CHUNK < count_ref[leaf])
            def _():
                block_copy(leaf, chunk).wait()
                total = None if chunk == 0 else near_ref[leaf]
                for slot in range(chunk * CHUNK, (chunk + 1) * CHUNK):
                    term = dot(blocks[leaf, slot], panel_of(leaf, slot))
                    total = term if total is None else total + term
                near_ref[leaf] = total


def down_kernel(
    near_list_ref, far_list_ref, coarse_list_ref,
    near_hbm, row_ref, transfer_ref, coupling_hbm, coarse_coupling_ref,
    skip_hbm, across_hbm, other_hbm, passed_hbm, mine_hbm, theirs_hbm,
    out_ref,
    near, coupling, coefs, parents, sems,
):
    leaves, slots, rank, _ = coupling.shape
    place = near_list_ref[0, 0] // leaves
    copies = [
        pltpu.make_async_copy(ref, coefs.at[pl.ds(n * leaves, leaves)], sems.at[n])
        for n, ref in enumerate((skip_hbm, across_hbm, other_hbm, passed_hbm))
    ]
    half = GROUP // 2
    copies += [
        pltpu.make_async_copy(ref, parents.at[pl.ds(n * half, half)], sems.at[4 + n])
        for n, ref in enumerate((mine_hbm, theirs_hbm))
    ]
    copies.append(pltpu.make_async_copy(coupling_hbm, coupling, sems.at[6]))
    near_copy = pltpu.make_async_copy(near_hbm, near, sems.at[7])
    for copy in copies:
        copy.start()
    near_copy.start()
    for copy in copies:
        copy.wait()

    local = place % GROUP
    total = None
    for slot in range(coarse_list_ref.shape[1]):
        step = (coarse_list_ref[0, slot] % GROUP) ^ local
        index = (step & 1) * half + (step >> 1)
        term = dot(coarse_coupling_ref[0, slot], parents[index])
        total = term if total is None else total + term
    high = total.astype(jnp.bfloat16)
    low = (total - high.astype(jnp.float32)).astype(jnp.bfloat16)
    coarse = jnp.concatenate([high, low], axis=0)

    odd = place % 2 == 1
    near_copy.wait()
    for leaf in range(leaves):
        matrix = transfer_ref[leaf]
        total = dot(jnp.concatenate([matrix, matrix], axis=1), coarse)
        for slot in range(slots):
            column = far_list_ref[leaf, slot]
            cluster = column // leaves
            away = jnp.where(odd, place - cluster, cluster - place)
            which = jnp.where(away < 0, away + 2, away + 1)
            index = which * leaves + column - cluster * leaves
            total = total + dot(coupling[leaf, slot], coefs[index])
        down = total.astype(jnp.bfloat16)
        result = near[leaf] + dot(row_ref[leaf], down)
        out_ref[leaf] = result.astype(jnp.bfloat16)


VMEM = pl.BlockSpec(memory_space=pltpu.VMEM)
SMEM = pl.BlockSpec(memory_space=pltpu.SMEM)
ANY = pl.BlockSpec(memory_space=pl.ANY)


def body(
    source,
    near_blocks,
    near_list,
    near_count,
    col_basis,
    row_basis,
    transfer,
    far_list,
    far_coupling,
    coarse_list,
    coarse_coupling,
):
    leaves, slots, rows, _ = near_blocks.shape
    rank = col_basis.shape[2]
    width = source.shape[1]
    count = lax.axis_size("row")
    far_slots = far_coupling.shape[1]
    coarse_slots = coarse_coupling.shape[1]

    def pairs_of(target):
        return [(d, target(d)) for d in range(count) if 0 <= target(d) < count]

    across = pairs_of(lambda d: d + 1 if d % 2 else d - 1)
    skip = pairs_of(lambda d: d - 2 if d % 2 else d + 2)

    def flip(bit):
        return pairs_of(lambda d: d ^ bit)

    def send(value, pairs):
        return lax.ppermute(value, "row", pairs)

    panels = source.reshape(leaves, rows, width)
    source_across = send(panels, across)
    source_other = send(panels, flip(1))

    coef, parent = pl.pallas_call(
        up_kernel,
        out_shape=(
            jax.ShapeDtypeStruct((leaves, rank, width), jnp.bfloat16),
            jax.ShapeDtypeStruct((rank, width), jnp.bfloat16),
        ),
        in_specs=[VMEM] * 3,
        out_specs=(VMEM, VMEM),
        cost_estimate=pl.CostEstimate(
            flops=2 * leaves * rank * width * (rows + rank),
            bytes_accessed=2 * leaves * rows * (width + rank),
            transcendentals=0,
        ),
        name="up",
    )(source, col_basis, transfer)

    parent = parent[None]
    pair = jnp.concatenate([parent, send(parent, flip(2))], axis=0)
    mine = jnp.concatenate([pair] + [send(pair, flip(bit)) for bit in (4, 8, 12)], axis=0)
    theirs = send(mine, flip(1))

    coef_across = send(coef, across)
    coef_other = send(coef, flip(1))
    coef_passed = send(coef_across, flip(1))
    coef_skip = send(coef, skip)

    near = pl.pallas_call(
        near_kernel,
        out_shape=jax.ShapeDtypeStruct((leaves, rows, width), jnp.float32),
        in_specs=[SMEM, SMEM, ANY, ANY, ANY, ANY],
        out_specs=VMEM,
        scratch_shapes=[
            pltpu.VMEM((leaves, slots, rows, rows), jnp.bfloat16),
            pltpu.VMEM((3 * leaves + 1, rows, width), jnp.bfloat16),
            pltpu.SemaphoreType.DMA((leaves, slots // CHUNK)),
            pltpu.SemaphoreType.DMA((3,)),
        ],
        cost_estimate=pl.CostEstimate(
            flops=2 * leaves * slots * rows * rows * width,
            bytes_accessed=2 * leaves * slots * rows * rows,
            transcendentals=0,
        ),
        compiler_params=pltpu.CompilerParams(vmem_limit_bytes=24 * 2**20),
        name="near",
    )(near_list, near_count, near_blocks, panels, source_other, source_across)

    result = pl.pallas_call(
        down_kernel,
        out_shape=jax.ShapeDtypeStruct((leaves, rows, width), jnp.bfloat16),
        in_specs=[SMEM] * 3 + [ANY, VMEM, VMEM, ANY, VMEM] + [ANY] * 6,
        out_specs=VMEM,
        scratch_shapes=[
            pltpu.VMEM((leaves, rows, width), jnp.float32),
            pltpu.VMEM((leaves, far_slots, rank, rank), jnp.bfloat16),
            pltpu.VMEM((4 * leaves, rank, width), jnp.bfloat16),
            pltpu.VMEM((GROUP, rank, width), jnp.bfloat16),
            pltpu.SemaphoreType.DMA((8,)),
        ],
        cost_estimate=pl.CostEstimate(
            flops=2 * leaves * (far_slots + 4) * rank * rank * width,
            bytes_accessed=2 * leaves * far_slots * rank * rank,
            transcendentals=0,
        ),
        compiler_params=pltpu.CompilerParams(vmem_limit_bytes=16 * 2**20),
        name="down",
    )(
        near_list, far_list, coarse_list, near, row_basis, transfer, far_coupling,
        coarse_coupling, coef_skip, coef_across, coef_other, coef_passed, mine, theirs,
    )
    return result.reshape(source.shape)


def solution(mesh):
    placed = (
        P(("clip", "row"), None),
        P(("clip", "row"), None, None, None),
        P(("clip", "row"), None),
        P(("clip", "row")),
        P(("clip", "row"), None, None),
        P(("clip", "row"), None, None),
        P(("clip", "row"), None, None),
        P(("clip", "row"), None),
        P(("clip", "row"), None, None, None),
        P(("clip", "row"), None),
        P(("clip", "row"), None, None, None),
    )
    return jax.shard_map(
        body, mesh=mesh, in_specs=placed, out_specs=P(("clip", "row"), None), check_vma=False
    )
```

```python
import jax
import jax.numpy as jnp
from jax import lax
from jax.experimental import pallas as pl
from jax.experimental.pallas import tpu as pltpu
from jax.sharding import PartitionSpec as P

GROUP = 16
CHUNK = 4


def dot(a, b):
    return jnp.dot(a, b, preferred_element_type=jnp.float32)


def dot_t(a, b):
    return lax.dot_general(
        a, b, (((0,), (0,)), ((), ())), preferred_element_type=jnp.float32
    )


def up_kernel(source_ref, col_ref, transfer_ref, share_ref, coef_ref, parent_ref):
    leaves, rows, rank = col_ref.shape
    total = None
    for leaf in range(leaves):
        panel = source_ref[pl.ds(leaf * rows, rows), :]
        share_ref[pl.ds(leaf * rows, rows), :] = panel
        coef = dot_t(col_ref[leaf], panel).astype(jnp.bfloat16)
        coef_ref[pl.ds(leaf * rank, rank), :] = coef
        share_ref[pl.ds(leaves * rows + leaf * rank, rank), :] = coef
        term = dot_t(transfer_ref[leaf], coef)
        total = term if total is None else total + term
    parent_ref[...] = total.astype(jnp.bfloat16)


def near_kernel(
    list_ref, count_ref, blocks_hbm, own_ref, share_ref, across_ref, near_ref,
    blocks, panels, block_sems, panel_sems,
):
    leaves, slots, rows, _ = blocks.shape
    chunks = slots // CHUNK
    size = leaves * rows
    place = list_ref[0, 0] // leaves
    pairs = [
        pltpu.make_async_copy(
            ref.at[pl.ds(0, size)], panels.at[pl.ds(which * size, size)], panel_sems.at[which]
        )
        for which, ref in enumerate((own_ref, share_ref, across_ref))
    ]
    for copy in pairs:
        copy.start()

    def block_copy(leaf, chunk):
        where = pl.ds(chunk * CHUNK, CHUNK)
        return pltpu.make_async_copy(
            blocks_hbm.at[leaf, where], blocks.at[leaf, where], block_sems.at[leaf, chunk]
        )

    for leaf in range(leaves):
        for chunk in range(chunks):
            @pl.when(chunk * CHUNK < count_ref[leaf])
            def _():
                block_copy(leaf, chunk).start()

    panels[pl.ds(3 * size, rows), :] = jnp.zeros((rows, panels.shape[1]), panels.dtype)
    for copy in pairs:
        copy.wait()

    def panel_of(leaf, slot):
        column = list_ref[leaf, slot]
        cluster = column // leaves
        which = jnp.where(cluster == place, 0, jnp.where(cluster == (place ^ 1), 1, 2))
        index = which * leaves + column - cluster * leaves
        index = jnp.where(slot < count_ref[leaf], index, 3 * leaves)
        return panels[pl.ds(pl.multiple_of(index * rows, rows), rows), :]

    for leaf in range(leaves):
        for chunk in range(chunks):
            @pl.when(chunk * CHUNK < count_ref[leaf])
            def _():
                block_copy(leaf, chunk).wait()
                total = None if chunk == 0 else near_ref[leaf]
                for slot in range(chunk * CHUNK, (chunk + 1) * CHUNK):
                    term = dot(blocks[leaf, slot], panel_of(leaf, slot))
                    total = term if total is None else total + term
                near_ref[leaf] = total


def down_kernel(
    near_list_ref, far_list_ref, coarse_list_ref,
    near_ref, row_ref, transfer_ref, coupling_ref, coarse_coupling_ref,
    skip_ref, across_ref, share_ref, passed_ref, mine_ref, theirs_ref,
    out_ref,
    coefs, sems,
):
    leaves, slots, rank, _ = coupling_ref.shape
    rows = row_ref.shape[1]
    size = leaves * rank
    place = near_list_ref[0, 0] // leaves
    copies = [
        pltpu.make_async_copy(
            ref.at[pl.ds(start, size)], coefs.at[pl.ds(n * size, size)], sems.at[n]
        )
        for n, (ref, start) in enumerate(
            ((skip_ref, 0), (across_ref, 0), (share_ref, leaves * rows), (passed_ref, 0))
        )
    ]
    for copy in copies:
        copy.start()

    local = place % GROUP
    total = None
    for slot in range(coarse_list_ref.shape[1]):
        cluster = coarse_list_ref[0, slot] % GROUP
        flip = cluster ^ local
        index = (cluster >> 2) * 2 + ((flip >> 1) & 1)
        panel = jnp.where((flip & 1) == 0, mine_ref[index], theirs_ref[index])
        term = dot(coarse_coupling_ref[0, slot], panel)
        total = term if total is None else total + term
    high = total.astype(jnp.bfloat16)
    low = (total - high.astype(jnp.float32)).astype(jnp.bfloat16)
    coarse = jnp.concatenate([high, low], axis=0)

    odd = place % 2 == 1
    for copy in copies:
        copy.wait()
    for leaf in range(leaves):
        matrix = transfer_ref[leaf]
        total = dot(jnp.concatenate([matrix, matrix], axis=1), coarse)
        for slot in range(slots):
            column = far_list_ref[leaf, slot]
            cluster = column // leaves
            away = jnp.where(odd, place - cluster, cluster - place)
            which = jnp.where(away < 0, away + 2, away + 1)
            index = which * leaves + column - cluster * leaves
            panel = coefs[pl.ds(pl.multiple_of(index * rank, rank), rank), :]
            total = total + dot(coupling_ref[leaf, slot], panel)
        down = total.astype(jnp.bfloat16)
        result = near_ref[leaf] + dot(row_ref[leaf], down)
        out_ref[pl.ds(leaf * rows, rows), :] = result.astype(jnp.bfloat16)


VMEM = pl.BlockSpec(memory_space=pltpu.VMEM)
SMEM = pl.BlockSpec(memory_space=pltpu.SMEM)
ANY = pl.BlockSpec(memory_space=pl.ANY)
HBM = pl.BlockSpec(memory_space=pltpu.HBM)


def body(
    source,
    near_blocks,
    near_list,
    near_count,
    col_basis,
    row_basis,
    transfer,
    far_list,
    far_coupling,
    coarse_list,
    coarse_coupling,
):
    leaves, slots, rows, _ = near_blocks.shape
    rank = col_basis.shape[2]
    width = source.shape[1]
    count = lax.axis_size("row")
    far_slots = far_coupling.shape[1]

    def pairs_of(target):
        return [(d, target(d)) for d in range(count) if 0 <= target(d) < count]

    across = pairs_of(lambda d: d + 1 if d % 2 else d - 1)
    skip = pairs_of(lambda d: d - 2 if d % 2 else d + 2)

    def flip(bit):
        return pairs_of(lambda d: d ^ bit)

    def send(value, pairs):
        return lax.ppermute(value, "row", pairs)

    across_source = send(source, across)

    share, coef, parent = pl.pallas_call(
        up_kernel,
        out_shape=(
            jax.ShapeDtypeStruct((leaves * (rows + rank), width), jnp.bfloat16),
            jax.ShapeDtypeStruct((leaves * rank, width), jnp.bfloat16),
            jax.ShapeDtypeStruct((rank, width), jnp.bfloat16),
        ),
        in_specs=[VMEM] * 3,
        out_specs=(VMEM,) * 3,
        cost_estimate=pl.CostEstimate(
            flops=2 * leaves * rank * width * (rows + rank),
            bytes_accessed=2 * leaves * rows * (width + rank),
            transcendentals=0,
        ),
        name="up",
    )(source, col_basis, transfer)

    parent = parent[None]
    pair = jnp.concatenate([parent, send(parent, flip(2))], axis=0)
    layers = [
        [base + step * 4 for step in range(GROUP // 4)]
        for start in range(0, count, GROUP)
        for base in range(start, start + 4)
    ]
    copies = jnp.broadcast_to(pair[None], (GROUP // 4,) + pair.shape)
    mine = lax.all_to_all(
        copies, "row", split_axis=0, concat_axis=0, axis_index_groups=layers
    ).reshape(GROUP // 2, rank, width)
    theirs = send(mine, flip(1))

    share_other = send(share, flip(1))
    coef_across = send(coef, across)
    coef_passed = send(coef_across, flip(1))
    coef_skip = send(coef, skip)

    near = pl.pallas_call(
        near_kernel,
        out_shape=jax.ShapeDtypeStruct((leaves, rows, width), jnp.float32),
        in_specs=[SMEM, SMEM, HBM, ANY, ANY, ANY],
        out_specs=VMEM,
        scratch_shapes=[
            pltpu.VMEM((leaves, slots, rows, rows), jnp.bfloat16),
            pltpu.VMEM(((3 * leaves + 1) * rows, width), jnp.bfloat16),
            pltpu.SemaphoreType.DMA((leaves, slots // CHUNK)),
            pltpu.SemaphoreType.DMA((3,)),
        ],
        cost_estimate=pl.CostEstimate(
            flops=2 * leaves * slots * rows * rows * width,
            bytes_accessed=2 * leaves * slots * rows * rows,
            transcendentals=0,
        ),
        compiler_params=pltpu.CompilerParams(vmem_limit_bytes=50 * 2**20),
        name="near",
    )(near_list, near_count, near_blocks, share, share_other, across_source)

    return pl.pallas_call(
        down_kernel,
        out_shape=jax.ShapeDtypeStruct(source.shape, jnp.bfloat16),
        in_specs=[SMEM] * 3 + [VMEM] * 5 + [ANY] * 4 + [VMEM] * 2,
        out_specs=VMEM,
        scratch_shapes=[
            pltpu.VMEM((4 * leaves * rank, width), jnp.bfloat16),
            pltpu.SemaphoreType.DMA((4,)),
        ],
        cost_estimate=pl.CostEstimate(
            flops=2 * leaves * (far_slots + 4) * rank * rank * width,
            bytes_accessed=2 * leaves * far_slots * rank * rank,
            transcendentals=0,
        ),
        compiler_params=pltpu.CompilerParams(vmem_limit_bytes=16 * 2**20),
        name="down",
    )(
        near_list, far_list, coarse_list, near, row_basis, transfer, far_coupling,
        coarse_coupling, coef_skip, coef_across, share_other, coef_passed, mine, theirs,
    )


def solution(mesh):
    placed = (
        P(("clip", "row"), None),
        P(("clip", "row"), None, None, None),
        P(("clip", "row"), None),
        P(("clip", "row")),
        P(("clip", "row"), None, None),
        P(("clip", "row"), None, None),
        P(("clip", "row"), None, None),
        P(("clip", "row"), None),
        P(("clip", "row"), None, None, None),
        P(("clip", "row"), None),
        P(("clip", "row"), None, None, None),
    )
    return jax.shard_map(
        body, mesh=mesh, in_specs=placed, out_specs=P(("clip", "row"), None), check_vma=False
    )
```

```python
import jax
import jax.numpy as jnp
from jax import lax
from jax.experimental import pallas as pl
from jax.experimental.pallas import tpu as pltpu
from jax.sharding import PartitionSpec as P

GROUP = 16
CHUNK = 4
AHEAD = 4


def dot(a, b):
    return jnp.dot(a, b, preferred_element_type=jnp.float32)


def dot_t(a, b):
    return lax.dot_general(
        a, b, (((0,), (0,)), ((), ())), preferred_element_type=jnp.float32
    )


def up_kernel(source_ref, col_ref, transfer_ref, share_ref, coef_ref, parent_ref):
    leaves, rows, rank = col_ref.shape
    total = None
    for leaf in range(leaves):
        panel = source_ref[pl.ds(leaf * rows, rows), :]
        share_ref[pl.ds(leaf * rows, rows), :] = panel
        coef = dot_t(col_ref[leaf], panel).astype(jnp.bfloat16)
        coef_ref[pl.ds(leaf * rank, rank), :] = coef
        share_ref[pl.ds(leaves * rows + leaf * rank, rank), :] = coef
        term = dot_t(transfer_ref[leaf], coef)
        total = term if total is None else total + term
    parent_ref[...] = total.astype(jnp.bfloat16)


def join(pieces, starts):
    sizes = [piece.shape[0] - start for piece, start in zip(pieces, starts)]

    def join_kernel(*refs):
        at = 0
        for ref, start, size in zip(refs, starts, sizes):
            refs[-1][pl.ds(at, size), :] = ref[pl.ds(start, size), :]
            at += size

    return pl.pallas_call(
        join_kernel,
        out_shape=jax.ShapeDtypeStruct((sum(sizes), pieces[0].shape[1]), pieces[0].dtype),
        in_specs=[VMEM] * len(pieces),
        out_specs=VMEM,
        name="join",
    )(*pieces)


def near_kernel(
    list_ref, count_ref, blocks_hbm, own_ref, share_ref, across_ref,
    near_ref,
    blocks, panels, block_sems, panel_sems,
):
    leaves, slots, rows, _ = blocks.shape
    chunks = slots // CHUNK
    size = leaves * rows
    place = list_ref[0, 0] // leaves

    def live(step):
        return step % chunks * CHUNK < count_ref[step // chunks]

    def block_copy(step):
        leaf, chunk = step // chunks, step % chunks
        where = pl.ds(chunk * CHUNK, CHUNK)
        return pltpu.make_async_copy(
            blocks_hbm.at[leaf, where], blocks.at[leaf, where], block_sems.at[leaf, chunk]
        )

    def start(step):
        if step < leaves * chunks:
            @pl.when(live(step))
            def _():
                block_copy(step).start()

    for step in range(AHEAD):
        start(step)
    pairs = [
        pltpu.make_async_copy(
            ref.at[pl.ds(0, size)], panels.at[pl.ds(which * size, size)], panel_sems.at[which]
        )
        for which, ref in enumerate((own_ref, share_ref, across_ref))
    ]
    for copy in pairs:
        copy.start()

    panels[pl.ds(3 * size, rows), :] = jnp.zeros((rows, panels.shape[1]), panels.dtype)
    for copy in pairs:
        copy.wait()

    def panel_of(leaf, slot):
        column = list_ref[leaf, slot]
        cluster = column // leaves
        which = jnp.where(cluster == place, 0, jnp.where(cluster == (place ^ 1), 1, 2))
        index = which * leaves + column - cluster * leaves
        index = jnp.where(slot < count_ref[leaf], index, 3 * leaves)
        return panels[pl.ds(pl.multiple_of(index * rows, rows), rows), :]

    for step in range(leaves * chunks):
        leaf, chunk = step // chunks, step % chunks
        start(step + AHEAD)

        @pl.when(live(step))
        def _():
            block_copy(step).wait()
            total = None if chunk == 0 else near_ref[leaf]
            for slot in range(chunk * CHUNK, (chunk + 1) * CHUNK):
                term = dot(blocks[leaf, slot], panel_of(leaf, slot))
                total = term if total is None else total + term
            near_ref[leaf] = total


def down_kernel(
    near_list_ref, far_list_ref, coarse_list_ref,
    near_ref, row_ref, transfer_ref, coupling_ref, coarse_coupling_ref,
    skip_ref, across_ref, share_ref, mine_ref, theirs_ref,
    out_ref,
    coefs, sems,
):
    leaves, slots, rank, _ = coupling_ref.shape
    rows = row_ref.shape[1]
    size = leaves * rank
    place = near_list_ref[0, 0] // leaves
    copies = [
        pltpu.make_async_copy(
            ref.at[pl.ds(start, size)], coefs.at[pl.ds(n * size, size)], sems.at[n]
        )
        for n, (ref, start) in enumerate(
            ((skip_ref, 0), (across_ref, leaves * rows), (share_ref, leaves * rows), (theirs_ref, GROUP // 2 * rank))
        )
    ]
    for copy in copies:
        copy.start()

    local = place % GROUP
    total = None
    for slot in range(coarse_list_ref.shape[1]):
        flip = coarse_list_ref[0, slot] % GROUP ^ local
        where = pl.ds(pl.multiple_of((flip >> 1) * rank, rank), rank)
        panel = jnp.where((flip & 1) == 0, mine_ref[where, :], theirs_ref[where, :])
        term = dot(coarse_coupling_ref[0, slot], panel)
        total = term if total is None else total + term
    high = total.astype(jnp.bfloat16)
    low = (total - high.astype(jnp.float32)).astype(jnp.bfloat16)
    coarse = jnp.concatenate([high, low], axis=0)

    odd = place % 2 == 1
    for copy in copies:
        copy.wait()
    for leaf in range(leaves):
        matrix = transfer_ref[leaf]
        total = dot(jnp.concatenate([matrix, matrix], axis=1), coarse)
        for slot in range(slots):
            column = far_list_ref[leaf, slot]
            cluster = column // leaves
            away = jnp.where(odd, place - cluster, cluster - place)
            which = jnp.where(away < 0, away + 2, away + 1)
            index = which * leaves + column - cluster * leaves
            panel = coefs[pl.ds(pl.multiple_of(index * rank, rank), rank), :]
            total = total + dot(coupling_ref[leaf, slot], panel)
        down = total.astype(jnp.bfloat16)
        result = near_ref[leaf] + dot(row_ref[leaf], down)
        out_ref[pl.ds(leaf * rows, rows), :] = result.astype(jnp.bfloat16)


VMEM = pl.BlockSpec(memory_space=pltpu.VMEM)
SMEM = pl.BlockSpec(memory_space=pltpu.SMEM)
ANY = pl.BlockSpec(memory_space=pl.ANY)
HBM = pl.BlockSpec(memory_space=pltpu.HBM)


def body(
    source,
    near_blocks,
    near_list,
    near_count,
    col_basis,
    row_basis,
    transfer,
    far_list,
    far_coupling,
    coarse_list,
    coarse_coupling,
):
    leaves, slots, rows, _ = near_blocks.shape
    rank = col_basis.shape[2]
    width = source.shape[1]
    count = lax.axis_size("row")
    far_slots = far_coupling.shape[1]

    def pairs_of(target):
        return [(d, target(d)) for d in range(count) if 0 <= target(d) < count]

    across = pairs_of(lambda d: d + 1 if d % 2 else d - 1)
    skip = pairs_of(lambda d: d - 2 if d % 2 else d + 2)

    def flip(bit):
        return pairs_of(lambda d: d ^ bit)

    def send(value, pairs):
        return lax.ppermute(value, "row", pairs)

    share, coef, parent = pl.pallas_call(
        up_kernel,
        out_shape=(
            jax.ShapeDtypeStruct((leaves * (rows + rank), width), jnp.bfloat16),
            jax.ShapeDtypeStruct((leaves * rank, width), jnp.bfloat16),
            jax.ShapeDtypeStruct((rank, width), jnp.bfloat16),
        ),
        in_specs=[VMEM] * 3,
        out_specs=(VMEM,) * 3,
        cost_estimate=pl.CostEstimate(
            flops=2 * leaves * rank * width * (rows + rank),
            bytes_accessed=2 * leaves * rows * (width + rank),
            transcendentals=0,
        ),
        name="up",
    )(source, col_basis, transfer)

    share_across = send(share, across)
    share_other = send(share, flip(1))
    coef_skip = send(coef, skip)
    pair = join([parent, send(parent, flip(2))], [0, 0])
    layers = [send(pair, flip(bit)) for bit in (4, 8, 12)]
    passed = join([pair, *layers, share_across], [0] * 4 + [leaves * rows])
    passed_other = send(passed, flip(1))

    near = pl.pallas_call(
        near_kernel,
        out_shape=jax.ShapeDtypeStruct((leaves, rows, width), jnp.float32),
        in_specs=[SMEM, SMEM, HBM] + [ANY] * 3,
        out_specs=VMEM,
        scratch_shapes=[
            pltpu.VMEM((leaves, slots, rows, rows), jnp.bfloat16),
            pltpu.VMEM(((3 * leaves + 1) * rows, width), jnp.bfloat16),
            pltpu.SemaphoreType.DMA((leaves, slots // CHUNK)),
            pltpu.SemaphoreType.DMA((3,)),
        ],
        cost_estimate=pl.CostEstimate(
            flops=2 * leaves * slots * rows * rows * width,
            bytes_accessed=2 * leaves * slots * rows * rows,
            transcendentals=0,
        ),
        compiler_params=pltpu.CompilerParams(vmem_limit_bytes=48 * 2**20),
        name="near",
    )(near_list, near_count, near_blocks, share, share_other, share_across)

    return pl.pallas_call(
        down_kernel,
        out_shape=jax.ShapeDtypeStruct(source.shape, jnp.bfloat16),
        in_specs=[SMEM] * 3 + [VMEM] * 5 + [ANY] * 3 + [VMEM] * 2,
        out_specs=VMEM,
        scratch_shapes=[
            pltpu.VMEM((4 * leaves * rank, width), jnp.bfloat16),
            pltpu.SemaphoreType.DMA((4,)),
        ],
        cost_estimate=pl.CostEstimate(
            flops=2 * leaves * (far_slots + 4) * rank * rank * width,
            bytes_accessed=2 * leaves * far_slots * rank * rank,
            transcendentals=0,
        ),
        compiler_params=pltpu.CompilerParams(vmem_limit_bytes=16 * 2**20),
        name="down",
    )(
        near_list, far_list, coarse_list, near, row_basis, transfer, far_coupling,
        coarse_coupling, coef_skip, share_across, share_other, passed, passed_other,
    )


def solution(mesh):
    placed = (
        P(("clip", "row"), None),
        P(("clip", "row"), None, None, None),
        P(("clip", "row"), None),
        P(("clip", "row")),
        P(("clip", "row"), None, None),
        P(("clip", "row"), None, None),
        P(("clip", "row"), None, None),
        P(("clip", "row"), None),
        P(("clip", "row"), None, None, None),
        P(("clip", "row"), None),
        P(("clip", "row"), None, None, None),
    )
    return jax.shard_map(
        body, mesh=mesh, in_specs=placed, out_specs=P(("clip", "row"), None), check_vma=False
    )
```

```python
import jax
import jax.numpy as jnp
from jax import lax
from jax.experimental import pallas as pl
from jax.experimental.pallas import tpu as pltpu
from jax.sharding import PartitionSpec as P

GROUP = 16
MIB = 2**20

VMEM = pl.BlockSpec(memory_space=pltpu.VMEM)
SMEM = pl.BlockSpec(memory_space=pltpu.SMEM)
ANY = pl.BlockSpec(memory_space=pl.ANY)


def dot(a, b):
    return jnp.dot(a, b, preferred_element_type=jnp.float32)


def dot_t(a, b):
    return lax.dot_general(
        a, b, (((0,), (0,)), ((), ())), preferred_element_type=jnp.float32
    )


def rows_at(index, rows):
    return pl.ds(pl.multiple_of(index * rows, rows), rows)


def up_kernel(source_ref, col_ref, transfer_ref, share_ref, lift_ref):
    leaves, rows, rank = col_ref.shape
    total = None
    for leaf in range(leaves):
        panel = source_ref[pl.ds(leaf * rows, rows), :]
        share_ref[pl.ds(leaf * rows, rows), :] = panel
        coef = dot_t(col_ref[leaf], panel).astype(jnp.bfloat16)
        lift_ref[pl.ds(leaf * rank, rank), :] = coef
        share_ref[pl.ds(leaves * rows + leaf * rank, rank), :] = coef
        term = dot_t(transfer_ref[leaf], coef)
        total = term if total is None else total + term
    lift_ref[pl.ds(leaves * rank, rank), :] = total.astype(jnp.bfloat16)


def pair_kernel(own_ref, lift_ref, _, level_ref, pair_ref):
    size = level_ref.shape[0]
    rank = own_ref.shape[0] - size
    level_ref[...] = lift_ref[pl.ds(0, size), :]
    pair_ref[pl.ds(0, rank), :] = own_ref[pl.ds(size, rank), :]
    pair_ref[pl.ds(rank, rank), :] = lift_ref[pl.ds(size, rank), :]


def pass_kernel(list_ref, *refs):
    *layers, level_ref, layer_ref, out_ref = refs
    at = 0
    for ref in layers:
        out_ref[pl.ds(at, ref.shape[0]), :] = ref[...]
        at += ref.shape[0]
    place = lax.div(list_ref[0, 0], list_ref.shape[0])
    corner = place & 3
    level = (corner == 0) | (corner == 3)
    out_ref[pl.ds(at, level_ref.shape[0]), :] = jnp.where(level, level_ref[...], layer_ref[...])


def pick_slots(list_ref, count_ref, blocks_hbm, blocks, sems, order_ref, leaf, keep):
    leaves, _ = list_ref.shape

    def step(slot, found):
        column = list_ref[leaf, slot]
        kept = keep(lax.div(column, leaves))

        @pl.when(kept)
        def _():
            order_ref[leaf, found] = column
            pltpu.make_async_copy(
                blocks_hbm.at[leaf, slot], blocks.at[leaf, found], sems.at[leaf, found]
            ).start()

        return found + kept.astype(jnp.int32)

    return lax.fori_loop(0, count_ref[leaf], step, 0)


def add_slots(total_ref, blocks_hbm, blocks, sems, order_ref, leaf, found, panel_of):
    def term(n):
        pltpu.make_async_copy(blocks_hbm.at[leaf, 0], blocks.at[leaf, n], sems.at[leaf, n]).wait()
        return dot(blocks[leaf, n], panel_of(order_ref[leaf, n]))

    def pair(n, _):
        total_ref[leaf] = total_ref[leaf] + term(2 * n) + term(2 * n + 1)
        return 0

    lax.fori_loop(0, found >> 1, pair, 0)

    @pl.when((found & 1) == 1)
    def _():
        total_ref[leaf] = total_ref[leaf] + term(found - 1)


def near_kernel(
    list_ref, count_ref, blocks_hbm, own_ref, share_ref,
    near_ref,
    blocks, panels, order, block_sems, panel_sems,
):
    leaves, _, rows, _ = blocks.shape
    size = leaves * rows
    place = lax.div(list_ref[0, 0], leaves)
    pairs = [
        pltpu.make_async_copy(
            ref.at[pl.ds(0, size)], panels.at[pl.ds(which * size, size)], panel_sems.at[which]
        )
        for which, ref in enumerate((own_ref, share_ref))
    ]
    for copy in pairs:
        copy.start()
    found = [
        pick_slots(
            list_ref, count_ref, blocks_hbm, blocks, block_sems, order, leaf,
            lambda cluster: (cluster ^ place) <= 1,
        )
        for leaf in range(leaves)
    ]
    near_ref[...] = jnp.zeros(near_ref.shape, near_ref.dtype)
    for copy in pairs:
        copy.wait()

    def panel_of(column):
        other = lax.div(column, leaves) ^ place
        return panels[rows_at(other * leaves + (column & (leaves - 1)), rows), :]

    for leaf in range(leaves):
        add_slots(near_ref, blocks_hbm, blocks, block_sems, order, leaf, found[leaf], panel_of)


def down_kernel(
    far_list_ref, coarse_list_ref, near_list_ref,
    transfer_ref, coupling_ref, coarse_coupling_ref, row_ref, near_ref,
    level_ref, layer_ref, share_ref, mine_ref, theirs_ref,
    out_ref,
    coefs, sems,
):
    leaves, slots, rank, _ = coupling_ref.shape
    rows = row_ref.shape[1]
    size = leaves * rank
    place = lax.div(near_list_ref[0, 0], leaves)
    copies = [
        pltpu.make_async_copy(
            ref.at[pl.ds(ref.shape[0] - size, size)], coefs.at[pl.ds(n * size, size)], sems.at[n]
        )
        for n, ref in enumerate((level_ref, layer_ref, share_ref, theirs_ref))
    ]
    for copy in copies:
        copy.start()

    local = place & (GROUP - 1)
    total = None
    for slot in range(coarse_list_ref.shape[1]):
        flip = (coarse_list_ref[0, slot] & (GROUP - 1)) ^ local
        where = rows_at(flip >> 1, rank)
        panel = jnp.where((flip & 1) == 0, mine_ref[where, :], theirs_ref[where, :])
        term = dot(coarse_coupling_ref[0, slot], panel)
        total = term if total is None else total + term
    high = total.astype(jnp.bfloat16)
    low = (total - high.astype(jnp.float32)).astype(jnp.bfloat16)
    coarse = jnp.concatenate([high, low], axis=0)

    beyond = jnp.where((place & 2) == 0, place - 2, place + 2)
    for copy in copies:
        copy.wait()

    def panel_of(leaf, slot):
        column = far_list_ref[leaf, slot]
        cluster = lax.div(column, leaves)
        which = jnp.where(
            cluster == (place ^ 2), 0,
            jnp.where(cluster == beyond, 1, jnp.where(cluster == (place ^ 1), 2, 3)),
        )
        return coefs[rows_at(which * leaves + column - cluster * leaves, rank), :]

    for leaf in range(leaves):
        matrix = transfer_ref[leaf]
        total = dot(jnp.concatenate([matrix, matrix], axis=1), coarse)
        for slot in range(0, slots, 2):
            both = jnp.concatenate([coupling_ref[leaf, slot], coupling_ref[leaf, slot + 1]], axis=1)
            panels = jnp.concatenate([panel_of(leaf, slot), panel_of(leaf, slot + 1)], axis=0)
            total = total + dot(both, panels)
        result = near_ref[leaf] + dot(row_ref[leaf], total.astype(jnp.bfloat16))
        out_ref[pl.ds(leaf * rows, rows), :] = result.astype(jnp.bfloat16)


def across_kernel(
    list_ref, count_ref, blocks_hbm, near_ref, across_ref,
    total_ref,
    blocks, order, sems,
):
    leaves, _, rows, _ = blocks.shape
    place = lax.div(list_ref[0, 0], leaves)
    found = [
        pick_slots(
            list_ref, count_ref, blocks_hbm, blocks, sems, order, leaf,
            lambda cluster: (cluster ^ place) > 1,
        )
        for leaf in range(leaves)
    ]
    total_ref[...] = near_ref[...]

    def panel_of(column):
        return across_ref[rows_at(column & (leaves - 1), rows), :]

    for leaf in range(leaves):
        add_slots(total_ref, blocks_hbm, blocks, sems, order, leaf, found[leaf], panel_of)


def call(kernel, name, outs, specs, args, scratch=(), flops=0, moved=0, limit=4):
    many = isinstance(outs, tuple)
    return pl.pallas_call(
        kernel,
        out_shape=outs,
        in_specs=specs,
        out_specs=(VMEM,) * len(outs) if many else VMEM,
        scratch_shapes=list(scratch),
        cost_estimate=pl.CostEstimate(flops=flops, bytes_accessed=moved, transcendentals=0),
        compiler_params=pltpu.CompilerParams(vmem_limit_bytes=limit * MIB),
        name=name,
    )(*args)


def body(
    source,
    near_blocks,
    near_list,
    near_count,
    col_basis,
    row_basis,
    transfer,
    far_list,
    far_coupling,
    coarse_list,
    coarse_coupling,
):
    leaves, slots, rows, _ = near_blocks.shape
    rank = col_basis.shape[2]
    width = source.shape[1]
    count = lax.axis_size("row")
    far_slots = far_coupling.shape[1]

    def send(value, target):
        pairs = [(d, target(d)) for d in range(count) if 0 <= target(d) < count]
        return lax.ppermute(value, "row", pairs)

    def panel(blocks, dtype=jnp.bfloat16):
        return jax.ShapeDtypeStruct((blocks * rank, width), dtype)

    share, lift = call(
        up_kernel, "up",
        (jax.ShapeDtypeStruct((leaves * (rows + rank), width), jnp.bfloat16), panel(leaves + 1)),
        [VMEM] * 3, (source, col_basis, transfer),
        flops=2 * leaves * rank * width * (rows + rank),
        moved=2 * leaves * rows * (width + rank), limit=8,
    )
    lift_level = send(lift, lambda d: d ^ 2)
    across = send(source, lambda d: d + 1 if d & 1 else d - 1)
    share_other = send(share, lambda d: d ^ 1)

    level, pair = call(
        pair_kernel, "pair", (panel(leaves), panel(2)),
        [VMEM] * 2 + [ANY], (lift, lift_level, share_other),
    )
    layers = [send(pair, lambda d, bit=bit: d ^ bit) for bit in (4, 8, 12)]
    layer = send(level, lambda d: d - 4 if d & 2 else d + 4)
    mine = call(
        pass_kernel, "pass", panel(GROUP // 2 + leaves), [SMEM] + [VMEM] * 6,
        (near_list, pair, *layers, level, layer),
    )
    theirs = send(mine, lambda d: d ^ 1)

    picked = [
        pltpu.VMEM(near_blocks.shape, jnp.bfloat16),
        pltpu.SMEM((leaves, slots), jnp.int32),
        pltpu.SemaphoreType.DMA((leaves, slots)),
    ]
    near = call(
        near_kernel, "near", jax.ShapeDtypeStruct((leaves, rows, width), jnp.float32),
        [SMEM, SMEM] + [ANY] * 3, (near_list, near_count, near_blocks, share, share_other),
        scratch=[
            picked[0],
            pltpu.VMEM((2 * leaves * rows, width), jnp.bfloat16),
            *picked[1:],
            pltpu.SemaphoreType.DMA((2,)),
        ],
        limit=48,
    )
    near = call(
        across_kernel, "across", jax.ShapeDtypeStruct((leaves, rows, width), jnp.float32),
        [SMEM] * 2 + [ANY] + [VMEM] * 2, (near_list, near_count, near_blocks, near, across),
        scratch=picked,
        flops=16 * leaves * slots * rows * rows * width,
        moved=2 * leaves * slots * rows * rows, limit=48,
    )
    return call(
        down_kernel, "down", jax.ShapeDtypeStruct(source.shape, jnp.bfloat16),
        [SMEM] * 3 + [VMEM] * 5 + [ANY] * 3 + [VMEM] * 2,
        (
            far_list, coarse_list, near_list, transfer, far_coupling, coarse_coupling, row_basis,
            near, level, layer, share_other, mine, theirs,
        ),
        scratch=[
            pltpu.VMEM((4 * leaves * rank, width), jnp.bfloat16),
            pltpu.SemaphoreType.DMA((4,)),
        ],
        flops=2 * leaves * (far_slots + 4) * rank * rank * width,
        moved=2 * leaves * far_slots * rank * rank, limit=12,
    )


def solution(mesh):
    placed = (
        P(("clip", "row"), None),
        P(("clip", "row"), None, None, None),
        P(("clip", "row"), None),
        P(("clip", "row")),
        P(("clip", "row"), None, None),
        P(("clip", "row"), None, None),
        P(("clip", "row"), None, None),
        P(("clip", "row"), None),
        P(("clip", "row"), None, None, None),
        P(("clip", "row"), None),
        P(("clip", "row"), None, None, None),
    )
    return jax.shard_map(
        body, mesh=mesh, in_specs=placed, out_specs=P(("clip", "row"), None), check_vma=False
    )
```

```python
import jax
import jax.numpy as jnp
from jax import lax
from jax.experimental import pallas as pl
from jax.experimental.pallas import tpu as pltpu
from jax.sharding import PartitionSpec as P

GROUP = 16
CHUNK = 4
MIB = 2**20

VMEM = pl.BlockSpec(memory_space=pltpu.VMEM)
SMEM = pl.BlockSpec(memory_space=pltpu.SMEM)
ANY = pl.BlockSpec(memory_space=pl.ANY)


def dot(a, b):
    return jnp.dot(a, b, preferred_element_type=jnp.float32)


def dot_t(a, b):
    return lax.dot_general(
        a, b, (((0,), (0,)), ((), ())), preferred_element_type=jnp.float32
    )


def rows_at(index, rows):
    return pl.ds(pl.multiple_of(index * rows, rows), rows)


def up_kernel(source_ref, col_ref, transfer_ref, share_ref, lift_ref):
    leaves, rows, rank = col_ref.shape
    total = None
    for leaf in range(leaves):
        panel = source_ref[pl.ds(leaf * rows, rows), :]
        share_ref[pl.ds(leaf * rows, rows), :] = panel
        coef = dot_t(col_ref[leaf], panel).astype(jnp.bfloat16)
        lift_ref[pl.ds(leaf * rank, rank), :] = coef
        share_ref[pl.ds(leaves * rows + leaf * rank, rank), :] = coef
        term = dot_t(transfer_ref[leaf], coef)
        total = term if total is None else total + term
    lift_ref[pl.ds(leaves * rank, rank), :] = total.astype(jnp.bfloat16)


def pair_kernel(own_ref, lift_ref, share_ref, _, level_ref, pair_ref, source_ref):
    size = level_ref.shape[0]
    rank = own_ref.shape[0] - size
    level_ref[...] = lift_ref[pl.ds(0, size), :]
    pair_ref[pl.ds(0, rank), :] = own_ref[pl.ds(size, rank), :]
    pair_ref[pl.ds(rank, rank), :] = lift_ref[pl.ds(size, rank), :]
    source_ref[...] = share_ref[pl.ds(0, source_ref.shape[0]), :]


def pass_kernel(list_ref, *refs):
    *layers, level_ref, layer_ref, out_ref = refs
    at = 0
    for ref in layers:
        out_ref[pl.ds(at, ref.shape[0]), :] = ref[...]
        at += ref.shape[0]
    place = lax.div(list_ref[0, 0], list_ref.shape[0])
    corner = place & 3
    level = (corner == 0) | (corner == 3)
    out_ref[pl.ds(at, level_ref.shape[0]), :] = jnp.where(level, level_ref[...], layer_ref[...])


def pick_slots(list_ref, count_ref, blocks_hbm, blocks, sems, order_ref, leaf, keep):
    leaves, _ = list_ref.shape

    def step(slot, found):
        column = list_ref[leaf, slot]
        kept = keep(lax.div(column, leaves))

        @pl.when(kept)
        def _():
            order_ref[leaf, found] = column
            pltpu.make_async_copy(
                blocks_hbm.at[leaf, slot], blocks.at[leaf, found], sems.at[leaf, found]
            ).start()

        return found + kept.astype(jnp.int32)

    found = lax.fori_loop(0, count_ref[leaf], step, 0)
    for pad in range(CHUNK):
        order_ref[leaf, found + pad] = -1
    return found


def add_slots(total_ref, blocks_hbm, blocks, sems, order_ref, leaf, found, panel_of):
    for first in range(0, blocks.shape[1], CHUNK):
        @pl.when(first < found)
        def _():
            for n in range(first, first + CHUNK):
                @pl.when(n < found)
                def _():
                    pltpu.make_async_copy(
                        blocks_hbm.at[leaf, 0], blocks.at[leaf, n], sems.at[leaf, n]
                    ).wait()
            total = total_ref[leaf]
            for n in range(first, first + CHUNK):
                block = blocks[leaf, jnp.where(n < found, n, 0)]
                total = total + dot(block, panel_of(order_ref[leaf, n]))
            total_ref[leaf] = total


def near_kernel(
    list_ref, count_ref, blocks_hbm, own_ref, share_ref,
    near_ref,
    blocks, panels, order, block_sems, panel_sems,
):
    leaves, _, rows, _ = blocks.shape
    size = leaves * rows
    place = lax.div(list_ref[0, 0], leaves)
    pairs = [
        pltpu.make_async_copy(
            ref.at[pl.ds(0, size)], panels.at[pl.ds(which * size, size)], panel_sems.at[which]
        )
        for which, ref in enumerate((own_ref, share_ref))
    ]
    for copy in pairs:
        copy.start()
    found = [
        pick_slots(
            list_ref, count_ref, blocks_hbm, blocks, block_sems, order, leaf,
            lambda cluster: (cluster ^ place) <= 1,
        )
        for leaf in range(leaves)
    ]
    near_ref[...] = jnp.zeros(near_ref.shape, near_ref.dtype)
    panels[pl.ds(2 * size, rows), :] = jnp.zeros((rows, panels.shape[1]), panels.dtype)
    for copy in pairs:
        copy.wait()

    def panel_of(column):
        index = (lax.div(column, leaves) ^ place) * leaves + (column & (leaves - 1))
        return panels[rows_at(jnp.where(column < 0, 2 * leaves, index), rows), :]

    for leaf in range(leaves):
        add_slots(near_ref, blocks_hbm, blocks, block_sems, order, leaf, found[leaf], panel_of)


def down_kernel(
    far_list_ref, coarse_list_ref, near_list_ref,
    transfer_ref, coupling_ref, coarse_coupling_ref, row_ref, near_ref,
    level_ref, layer_ref, share_ref, mine_ref, theirs_ref,
    out_ref,
    coefs, sems,
):
    leaves, slots, rank, _ = coupling_ref.shape
    rows = row_ref.shape[1]
    size = leaves * rank
    place = lax.div(near_list_ref[0, 0], leaves)
    copies = [
        pltpu.make_async_copy(
            ref.at[pl.ds(ref.shape[0] - size, size)], coefs.at[pl.ds(n * size, size)], sems.at[n]
        )
        for n, ref in enumerate((level_ref, layer_ref, share_ref, theirs_ref))
    ]
    for copy in copies:
        copy.start()

    local = place & (GROUP - 1)
    total = None
    for slot in range(coarse_list_ref.shape[1]):
        flip = (coarse_list_ref[0, slot] & (GROUP - 1)) ^ local
        where = rows_at(flip >> 1, rank)
        panel = jnp.where((flip & 1) == 0, mine_ref[where, :], theirs_ref[where, :])
        term = dot(coarse_coupling_ref[0, slot], panel)
        total = term if total is None else total + term
    high = total.astype(jnp.bfloat16)
    low = (total - high.astype(jnp.float32)).astype(jnp.bfloat16)
    coarse = jnp.concatenate([high, low], axis=0)

    beyond = jnp.where((place & 2) == 0, place - 2, place + 2)
    for copy in copies:
        copy.wait()

    def panel_of(leaf, slot):
        column = far_list_ref[leaf, slot]
        cluster = lax.div(column, leaves)
        which = jnp.where(
            cluster == (place ^ 2), 0,
            jnp.where(cluster == beyond, 1, jnp.where(cluster == (place ^ 1), 2, 3)),
        )
        return coefs[rows_at(which * leaves + column - cluster * leaves, rank), :]

    for leaf in range(leaves):
        matrix = transfer_ref[leaf]
        total = dot(jnp.concatenate([matrix, matrix], axis=1), coarse)
        for slot in range(0, slots, 2):
            both = jnp.concatenate([coupling_ref[leaf, slot], coupling_ref[leaf, slot + 1]], axis=1)
            panels = jnp.concatenate([panel_of(leaf, slot), panel_of(leaf, slot + 1)], axis=0)
            total = total + dot(both, panels)
        result = near_ref[leaf] + dot(row_ref[leaf], total.astype(jnp.bfloat16))
        out_ref[pl.ds(leaf * rows, rows), :] = result.astype(jnp.bfloat16)


def across_kernel(
    list_ref, count_ref, blocks_hbm, near_ref, across_ref,
    total_ref,
    blocks, order, sems,
):
    leaves, _, rows, _ = blocks.shape
    place = lax.div(list_ref[0, 0], leaves)
    found = [
        pick_slots(
            list_ref, count_ref, blocks_hbm, blocks, sems, order, leaf,
            lambda cluster: (cluster ^ place) > 1,
        )
        for leaf in range(leaves)
    ]
    total_ref[...] = near_ref[...]

    def panel_of(column):
        panel = across_ref[rows_at(column & (leaves - 1), rows), :]
        return jnp.where(column < 0, jnp.zeros_like(panel), panel)

    for leaf in range(leaves):
        add_slots(total_ref, blocks_hbm, blocks, sems, order, leaf, found[leaf], panel_of)


def call(kernel, name, outs, specs, args, scratch=(), flops=0, moved=0, limit=4):
    many = isinstance(outs, tuple)
    return pl.pallas_call(
        kernel,
        out_shape=outs,
        in_specs=specs,
        out_specs=(VMEM,) * len(outs) if many else VMEM,
        scratch_shapes=list(scratch),
        cost_estimate=pl.CostEstimate(flops=flops, bytes_accessed=moved, transcendentals=0),
        compiler_params=pltpu.CompilerParams(vmem_limit_bytes=limit * MIB),
        name=name,
    )(*args)


def body(
    source,
    near_blocks,
    near_list,
    near_count,
    col_basis,
    row_basis,
    transfer,
    far_list,
    far_coupling,
    coarse_list,
    coarse_coupling,
):
    leaves, slots, rows, _ = near_blocks.shape
    rank = col_basis.shape[2]
    width = source.shape[1]
    count = lax.axis_size("row")
    far_slots = far_coupling.shape[1]

    def send(value, target):
        pairs = [(d, target(d)) for d in range(count) if 0 <= target(d) < count]
        return lax.ppermute(value, "row", pairs)

    def panel(blocks, dtype=jnp.bfloat16):
        return jax.ShapeDtypeStruct((blocks * rank, width), dtype)

    share, lift = call(
        up_kernel, "up",
        (jax.ShapeDtypeStruct((leaves * (rows + rank), width), jnp.bfloat16), panel(leaves + 1)),
        [VMEM] * 3, (source, col_basis, transfer),
        flops=2 * leaves * rank * width * (rows + rank),
        moved=2 * leaves * rows * (width + rank), limit=8,
    )
    lift_level = send(lift, lambda d: d ^ 2)
    share_other = send(share, lambda d: d ^ 1)

    picked = [
        pltpu.VMEM(near_blocks.shape, jnp.bfloat16),
        pltpu.SMEM((leaves, slots + CHUNK), jnp.int32),
        pltpu.SemaphoreType.DMA((leaves, slots)),
    ]
    near = call(
        near_kernel, "near", jax.ShapeDtypeStruct((leaves, rows, width), jnp.float32),
        [SMEM, SMEM] + [ANY] * 3, (near_list, near_count, near_blocks, share, share_other),
        scratch=[
            picked[0],
            pltpu.VMEM(((2 * leaves + 1) * rows, width), jnp.bfloat16),
            *picked[1:],
            pltpu.SemaphoreType.DMA((2,)),
        ],
        limit=48,
    )
    level, pair, source_own = call(
        pair_kernel, "pair", (panel(leaves), panel(2), jax.ShapeDtypeStruct(source.shape, jnp.bfloat16)),
        [VMEM] * 3 + [ANY], (lift, lift_level, share, near),
    )
    across = send(source_own, lambda d: d + 1 if d & 1 else d - 1)
    layers = [send(pair, lambda d, bit=bit: d ^ bit) for bit in (4, 8, 12)]
    layer = send(level, lambda d: d - 4 if d & 2 else d + 4)
    mine = call(
        pass_kernel, "pass", panel(GROUP // 2 + leaves), [SMEM] + [VMEM] * 6,
        (near_list, pair, *layers, level, layer),
    )
    theirs = send(mine, lambda d: d ^ 1)

    near = call(
        across_kernel, "across", jax.ShapeDtypeStruct((leaves, rows, width), jnp.float32),
        [SMEM] * 2 + [ANY] + [VMEM] * 2, (near_list, near_count, near_blocks, near, across),
        scratch=picked,
        flops=16 * leaves * slots * rows * rows * width,
        moved=2 * leaves * slots * rows * rows, limit=48,
    )
    return call(
        down_kernel, "down", jax.ShapeDtypeStruct(source.shape, jnp.bfloat16),
        [SMEM] * 3 + [VMEM] * 5 + [ANY] * 3 + [VMEM] * 2,
        (
            far_list, coarse_list, near_list, transfer, far_coupling, coarse_coupling, row_basis,
            near, level, layer, share_other, mine, theirs,
        ),
        scratch=[
            pltpu.VMEM((4 * leaves * rank, width), jnp.bfloat16),
            pltpu.SemaphoreType.DMA((4,)),
        ],
        flops=2 * leaves * (far_slots + 4) * rank * rank * width,
        moved=2 * leaves * far_slots * rank * rank, limit=12,
    )


def solution(mesh):
    placed = (
        P(("clip", "row"), None),
        P(("clip", "row"), None, None, None),
        P(("clip", "row"), None),
        P(("clip", "row")),
        P(("clip", "row"), None, None),
        P(("clip", "row"), None, None),
        P(("clip", "row"), None, None),
        P(("clip", "row"), None),
        P(("clip", "row"), None, None, None),
        P(("clip", "row"), None),
        P(("clip", "row"), None, None, None),
    )
    return jax.shard_map(
        body, mesh=mesh, in_specs=placed, out_specs=P(("clip", "row"), None), check_vma=False
    )
```

```python
import jax
import jax.numpy as jnp
from jax import lax
from jax.experimental import pallas as pl
from jax.experimental.pallas import tpu as pltpu
from jax.sharding import PartitionSpec as P

GROUP = 16
CHUNK = 4
AHEAD = 4
MIB = 2**20

VMEM = pl.BlockSpec(memory_space=pltpu.VMEM)
SMEM = pl.BlockSpec(memory_space=pltpu.SMEM)
ANY = pl.BlockSpec(memory_space=pl.ANY)


def dot(a, b):
    return jnp.dot(a, b, preferred_element_type=jnp.float32)


def dot_t(a, b):
    return lax.dot_general(
        a, b, (((0,), (0,)), ((), ())), preferred_element_type=jnp.float32
    )


def rows_at(index, rows):
    return pl.ds(pl.multiple_of(index * rows, rows), rows)


def up_kernel(
    source_hbm, col_hbm, transfer_hbm,
    share_ref, parent_ref,
    col, transfer, sems,
):
    leaves, rows, rank = col.shape
    copies = []
    for leaf in range(leaves):
        panel = pl.ds(leaf * rows, rows)
        for n, (source, target) in enumerate((
            (source_hbm.at[panel], share_ref.at[panel]),
            (col_hbm.at[leaf], col.at[leaf]),
            (transfer_hbm.at[leaf], transfer.at[leaf]),
        )):
            copies.append(pltpu.make_async_copy(source, target, sems.at[leaf, n]))
            copies[-1].start()
    total = None
    for leaf in range(leaves):
        for copy in copies[3 * leaf:3 * leaf + 3]:
            copy.wait()
        coef = dot_t(col[leaf], share_ref[pl.ds(leaf * rows, rows), :]).astype(jnp.bfloat16)
        share_ref[pl.ds(leaves * rows + leaf * rank, rank), :] = coef
        term = dot_t(transfer[leaf], coef)
        total = term if total is None else total + term
    parent_ref[...] = total.astype(jnp.bfloat16)


def pair_kernel(own_ref, other_ref, share_ref, _, pair_ref, coef_ref, source_ref):
    rank = own_ref.shape[0]
    rows = source_ref.shape[0]
    coef_ref[...] = share_ref[pl.ds(rows, coef_ref.shape[0]), :]
    source_ref[...] = share_ref[pl.ds(0, rows), :]
    pair_ref[pl.ds(0, rank), :] = own_ref[...]
    pair_ref[pl.ds(rank, rank), :] = other_ref[...]


def join_kernel(*refs):
    *pieces, _, out_ref = refs
    at = 0
    for ref in pieces:
        out_ref[pl.ds(at, ref.shape[0]), :] = ref[...]
        at += ref.shape[0]


def pick_kernel(list_ref, level_ref, layer_ref, out_ref):
    place = lax.div(list_ref[0, 0], list_ref.shape[0])
    corner = place & 3
    level = (corner == 0) | (corner == 3)
    out_ref[...] = jnp.where(level, level_ref[...], layer_ref[...])


def near_kernel(
    list_ref, count_ref, blocks_hbm, own_ref, share_ref, across_ref,
    near_ref,
    blocks, panels, block_sems, panel_sems,
):
    leaves, slots, rows, _ = blocks.shape
    chunks = slots // CHUNK
    size = leaves * rows
    place = lax.div(list_ref[0, 0], leaves)

    def live(step):
        return step % chunks * CHUNK < count_ref[step // chunks]

    def block_copy(step):
        leaf, chunk = step // chunks, step % chunks
        where = pl.ds(chunk * CHUNK, CHUNK)
        return pltpu.make_async_copy(
            blocks_hbm.at[leaf, where], blocks.at[leaf, where], block_sems.at[leaf, chunk]
        )

    def start(step):
        if step < leaves * chunks:
            @pl.when(live(step))
            def _():
                block_copy(step).start()

    pairs = [
        pltpu.make_async_copy(
            ref.at[pl.ds(0, size)], panels.at[pl.ds(which * size, size)], panel_sems.at[which]
        )
        for which, ref in enumerate((own_ref, share_ref, across_ref))
    ]
    for copy in pairs:
        copy.start()
    for step in range(AHEAD):
        start(step)
    panels[pl.ds(3 * size, rows), :] = jnp.zeros((rows, panels.shape[1]), panels.dtype)
    for copy in pairs:
        copy.wait()

    def panel_of(leaf, slot):
        column = list_ref[leaf, slot]
        which = jnp.minimum(lax.div(column, leaves) ^ place, 2)
        index = which * leaves + (column & (leaves - 1))
        index = jnp.where(slot < count_ref[leaf], index, 3 * leaves)
        return panels[rows_at(index, rows), :]

    for step in range(leaves * chunks):
        leaf, chunk = step // chunks, step % chunks
        start(step + AHEAD)

        @pl.when(live(step))
        def _():
            block_copy(step).wait()
            total = None if chunk == 0 else near_ref[leaf]
            for slot in range(chunk * CHUNK, (chunk + 1) * CHUNK):
                term = dot(blocks[leaf, slot], panel_of(leaf, slot))
                total = term if total is None else total + term
            near_ref[leaf] = total


def down_kernel(
    far_list_ref, coarse_list_ref, near_list_ref,
    transfer_ref, coupling_ref, coarse_coupling_ref, row_ref, near_ref,
    level_ref, layer_ref, share_ref, passed_ref, mine_ref, theirs_ref,
    out_ref,
    coefs, sems,
):
    leaves, slots, rank, _ = coupling_ref.shape
    rows = row_ref.shape[1]
    size = leaves * rank
    place = lax.div(near_list_ref[0, 0], leaves)
    copies = [
        pltpu.make_async_copy(
            ref.at[pl.ds(ref.shape[0] - size, size)], coefs.at[pl.ds(n * size, size)], sems.at[n]
        )
        for n, ref in enumerate((level_ref, layer_ref, share_ref, passed_ref))
    ]
    for copy in copies:
        copy.start()

    local = place & (GROUP - 1)
    total = None
    for slot in range(coarse_list_ref.shape[1]):
        flip = (coarse_list_ref[0, slot] & (GROUP - 1)) ^ local
        where = rows_at(flip >> 1, rank)
        panel = jnp.where((flip & 1) == 0, mine_ref[where, :], theirs_ref[where, :])
        term = dot(coarse_coupling_ref[0, slot], panel)
        total = term if total is None else total + term
    high = total.astype(jnp.bfloat16)
    low = (total - high.astype(jnp.float32)).astype(jnp.bfloat16)
    coarse = jnp.concatenate([high, low], axis=0)

    beyond = jnp.where((place & 2) == 0, place - 2, place + 2)
    for copy in copies:
        copy.wait()

    def panel_of(leaf, slot):
        column = far_list_ref[leaf, slot]
        cluster = lax.div(column, leaves)
        which = jnp.where(
            cluster == (place ^ 2), 0,
            jnp.where(cluster == beyond, 1, jnp.where(cluster == (place ^ 1), 2, 3)),
        )
        return coefs[rows_at(which * leaves + column - cluster * leaves, rank), :]

    for leaf in range(leaves):
        matrix = transfer_ref[leaf]
        total = dot(jnp.concatenate([matrix, matrix], axis=1), coarse)
        for slot in range(0, slots, 2):
            both = jnp.concatenate([coupling_ref[leaf, slot], coupling_ref[leaf, slot + 1]], axis=1)
            panels = jnp.concatenate([panel_of(leaf, slot), panel_of(leaf, slot + 1)], axis=0)
            total = total + dot(both, panels)
        result = near_ref[leaf] + dot(row_ref[leaf], total.astype(jnp.bfloat16))
        out_ref[pl.ds(leaf * rows, rows), :] = result.astype(jnp.bfloat16)


def call(kernel, name, outs, specs, args, scratch=(), flops=0, moved=0, limit=4):
    many = isinstance(outs, tuple)
    return pl.pallas_call(
        kernel,
        out_shape=outs,
        in_specs=specs,
        out_specs=(VMEM,) * len(outs) if many else VMEM,
        scratch_shapes=list(scratch),
        cost_estimate=pl.CostEstimate(flops=flops, bytes_accessed=moved, transcendentals=0),
        compiler_params=pltpu.CompilerParams(vmem_limit_bytes=limit * MIB),
        name=name,
    )(*args)


def body(
    source,
    near_blocks,
    near_list,
    near_count,
    col_basis,
    row_basis,
    transfer,
    far_list,
    far_coupling,
    coarse_list,
    coarse_coupling,
):
    leaves, slots, rows, _ = near_blocks.shape
    rank = col_basis.shape[2]
    width = source.shape[1]
    count = lax.axis_size("row")
    far_slots = far_coupling.shape[1]

    def send(value, target):
        pairs = [(d, target(d)) for d in range(count) if 0 <= target(d) < count]
        return lax.ppermute(value, "row", pairs)

    def panel(blocks, dtype=jnp.bfloat16):
        return jax.ShapeDtypeStruct((blocks * rank, width), dtype)

    share, parent = call(
        up_kernel, "up",
        (jax.ShapeDtypeStruct((leaves * (rows + rank), width), jnp.bfloat16), panel(1)),
        [ANY] * 3, (source, col_basis, transfer),
        scratch=[
            pltpu.VMEM(col_basis.shape, jnp.bfloat16),
            pltpu.VMEM(transfer.shape, jnp.bfloat16),
            pltpu.SemaphoreType.DMA((leaves, 3)),
        ],
        flops=2 * leaves * rank * width * (rows + rank),
        moved=2 * leaves * rows * (width + rank), limit=16,
    )
    parent_level = send(parent, lambda d: d ^ 2)
    share_other = send(share, lambda d: d ^ 1)

    pair, coef, panels = call(
        pair_kernel, "pair",
        (panel(2), panel(leaves), jax.ShapeDtypeStruct(source.shape, jnp.bfloat16)),
        [VMEM] * 3 + [ANY], (parent, parent_level, share, share_other),
    )
    level = send(coef, lambda d: d ^ 2)
    across = send(panels, lambda d: d + 1 if d & 1 else d - 1)
    layers = [send(pair, lambda d, bit=bit: d ^ bit) for bit in (4, 8, 12)]

    layer = send(level, lambda d: d - 4 if d & 2 else d + 4)
    near = call(
        near_kernel, "near", jax.ShapeDtypeStruct((leaves, rows, width), jnp.float32),
        [SMEM, SMEM] + [ANY] * 4,
        (near_list, near_count, near_blocks, share, share_other, across),
        scratch=[
            pltpu.VMEM(near_blocks.shape, jnp.bfloat16),
            pltpu.VMEM(((3 * leaves + 1) * rows, width), jnp.bfloat16),
            pltpu.SemaphoreType.DMA((leaves, slots // CHUNK)),
            pltpu.SemaphoreType.DMA((3,)),
        ],
        flops=0,
        limit=48,
    )
    mine = call(join_kernel, "mine", panel(GROUP // 2), [VMEM] * 4 + [ANY], (pair, *layers, near))
    theirs = send(mine, lambda d: d ^ 1)
    picked = call(
        pick_kernel, "pick", panel(leaves), [SMEM] + [VMEM] * 2, (near_list, level, layer)
    )
    passed = send(picked, lambda d: d ^ 1)
    return call(
        down_kernel, "down", jax.ShapeDtypeStruct(source.shape, jnp.bfloat16),
        [SMEM] * 3 + [VMEM] * 5 + [ANY] * 4 + [VMEM] * 2,
        (
            far_list, coarse_list, near_list, transfer, far_coupling, coarse_coupling, row_basis,
            near, level, layer, share_other, passed, mine, theirs,
        ),
        scratch=[
            pltpu.VMEM((4 * leaves * rank, width), jnp.bfloat16),
            pltpu.SemaphoreType.DMA((4,)),
        ],
        flops=2 * leaves * (far_slots + 4) * rank * rank * width,
        moved=2 * leaves * far_slots * rank * rank, limit=12,
    )


def solution(mesh):
    placed = (
        P(("clip", "row"), None),
        P(("clip", "row"), None, None, None),
        P(("clip", "row"), None),
        P(("clip", "row")),
        P(("clip", "row"), None, None),
        P(("clip", "row"), None, None),
        P(("clip", "row"), None, None),
        P(("clip", "row"), None),
        P(("clip", "row"), None, None, None),
        P(("clip", "row"), None),
        P(("clip", "row"), None, None, None),
    )
    return jax.shard_map(
        body, mesh=mesh, in_specs=placed, out_specs=P(("clip", "row"), None), check_vma=False
    )
```

```python
import jax
import jax.numpy as jnp
from jax import lax
from jax.experimental import pallas as pl
from jax.experimental.pallas import tpu as pltpu
from jax.sharding import PartitionSpec as P

GROUP = 16
CHUNK = 4
MIB = 2**20

VMEM = pl.BlockSpec(memory_space=pltpu.VMEM)
SMEM = pl.BlockSpec(memory_space=pltpu.SMEM)
ANY = pl.BlockSpec(memory_space=pl.ANY)


def dot(a, b):
    return jnp.dot(a, b, preferred_element_type=jnp.float32)


def dot_t(a, b):
    return lax.dot_general(
        a, b, (((0,), (0,)), ((), ())), preferred_element_type=jnp.float32
    )


def rows_at(index, rows):
    return pl.ds(pl.multiple_of(index * rows, rows), rows)


def up_kernel(source_ref, col_ref, transfer_ref, share_ref, coef_ref, parent_ref):
    leaves, rows, rank = col_ref.shape
    total = None
    for leaf in range(leaves):
        panel = source_ref[pl.ds(leaf * rows, rows), :]
        share_ref[pl.ds(leaf * rows, rows), :] = panel
        coef = dot_t(col_ref[leaf], panel).astype(jnp.bfloat16)
        coef_ref[pl.ds(leaf * rank, rank), :] = coef
        share_ref[pl.ds(leaves * rows + leaf * rank, rank), :] = coef
        term = dot_t(transfer_ref[leaf], coef)
        total = term if total is None else total + term
    parent_ref[...] = total.astype(jnp.bfloat16)


def join_kernel(*refs):
    *pieces, level_ref, _, out_ref, relay_ref = refs
    relay_ref[...] = level_ref[...]
    at = 0
    for ref in pieces:
        out_ref[pl.ds(at, ref.shape[0]), :] = ref[...]
        at += ref.shape[0]


def pass_kernel(list_ref, *refs):
    *layers, level_ref, layer_ref, out_ref = refs
    at = 0
    for ref in layers:
        out_ref[pl.ds(at, ref.shape[0]), :] = ref[...]
        at += ref.shape[0]
    place = lax.div(list_ref[0, 0], list_ref.shape[0])
    corner = place & 3
    level = (corner == 0) | (corner == 3)
    out_ref[pl.ds(at, level_ref.shape[0]), :] = jnp.where(level, level_ref[...], layer_ref[...])


def pick_slots(list_ref, count_ref, blocks_hbm, blocks, sems, order_ref, leaf, keep):
    leaves, _ = list_ref.shape

    def step(slot, found):
        column = list_ref[leaf, slot]
        kept = keep(lax.div(column, leaves))

        @pl.when(kept)
        def _():
            order_ref[leaf, found] = column
            pltpu.make_async_copy(
                blocks_hbm.at[leaf, slot], blocks.at[leaf, found], sems.at[leaf, found]
            ).start()

        return found + kept.astype(jnp.int32)

    found = lax.fori_loop(0, count_ref[leaf], step, 0)
    for pad in range(CHUNK):
        order_ref[leaf, found + pad] = -1
    return found


def add_slots(total_ref, blocks_hbm, blocks, sems, order_ref, leaf, found, panel_of):
    for first in range(0, blocks.shape[1], CHUNK):
        @pl.when(first < found)
        def _():
            for n in range(first, first + CHUNK):
                @pl.when(n < found)
                def _():
                    pltpu.make_async_copy(
                        blocks_hbm.at[leaf, 0], blocks.at[leaf, n], sems.at[leaf, n]
                    ).wait()
            total = total_ref[leaf]
            for n in range(first, first + CHUNK):
                block = blocks[leaf, jnp.where(n < found, n, 0)]
                total = total + dot(block, panel_of(order_ref[leaf, n]))
            total_ref[leaf] = total


def near_kernel(
    list_ref, count_ref, blocks_hbm, own_ref, share_ref,
    near_ref,
    blocks, panels, order, block_sems, panel_sems,
):
    leaves, _, rows, _ = blocks.shape
    size = leaves * rows
    place = lax.div(list_ref[0, 0], leaves)
    pairs = [
        pltpu.make_async_copy(
            ref.at[pl.ds(0, size)], panels.at[pl.ds(which * size, size)], panel_sems.at[which]
        )
        for which, ref in enumerate((own_ref, share_ref))
    ]
    for copy in pairs:
        copy.start()
    found = [
        pick_slots(
            list_ref, count_ref, blocks_hbm, blocks, block_sems, order, leaf,
            lambda cluster: (cluster ^ place) <= 1,
        )
        for leaf in range(leaves)
    ]
    near_ref[...] = jnp.zeros(near_ref.shape, near_ref.dtype)
    panels[pl.ds(2 * size, rows), :] = jnp.zeros((rows, panels.shape[1]), panels.dtype)
    for copy in pairs:
        copy.wait()

    def panel_of(column):
        index = (lax.div(column, leaves) ^ place) * leaves + (column & (leaves - 1))
        return panels[rows_at(jnp.where(column < 0, 2 * leaves, index), rows), :]

    for leaf in range(leaves):
        add_slots(near_ref, blocks_hbm, blocks, block_sems, order, leaf, found[leaf], panel_of)


def down_kernel(
    far_list_ref, coarse_list_ref, near_list_ref,
    transfer_ref, coupling_ref, coarse_coupling_ref, row_ref, near_ref,
    level_ref, layer_ref, share_ref, mine_ref, theirs_ref,
    out_ref,
    coefs, sems,
):
    leaves, slots, rank, _ = coupling_ref.shape
    rows = row_ref.shape[1]
    size = leaves * rank
    place = lax.div(near_list_ref[0, 0], leaves)
    copies = [
        pltpu.make_async_copy(
            ref.at[pl.ds(ref.shape[0] - size, size)], coefs.at[pl.ds(n * size, size)], sems.at[n]
        )
        for n, ref in enumerate((level_ref, layer_ref, share_ref, theirs_ref))
    ]
    for copy in copies:
        copy.start()

    local = place & (GROUP - 1)
    total = None
    for slot in range(coarse_list_ref.shape[1]):
        flip = (coarse_list_ref[0, slot] & (GROUP - 1)) ^ local
        where = rows_at((flip & 2) * 2 + (flip >> 2), rank)
        panel = jnp.where((flip & 1) == 0, mine_ref[where, :], theirs_ref[where, :])
        term = dot(coarse_coupling_ref[0, slot], panel)
        total = term if total is None else total + term
    high = total.astype(jnp.bfloat16)
    low = (total - high.astype(jnp.float32)).astype(jnp.bfloat16)
    coarse = jnp.concatenate([high, low], axis=0)

    beyond = jnp.where((place & 2) == 0, place - 2, place + 2)
    for copy in copies:
        copy.wait()

    def panel_of(leaf, slot):
        column = far_list_ref[leaf, slot]
        cluster = lax.div(column, leaves)
        which = jnp.where(
            cluster == (place ^ 2), 0,
            jnp.where(cluster == beyond, 1, jnp.where(cluster == (place ^ 1), 2, 3)),
        )
        return coefs[rows_at(which * leaves + column - cluster * leaves, rank), :]

    for leaf in range(leaves):
        matrix = transfer_ref[leaf]
        total = dot(jnp.concatenate([matrix, matrix], axis=1), coarse)
        for slot in range(0, slots, 2):
            both = jnp.concatenate([coupling_ref[leaf, slot], coupling_ref[leaf, slot + 1]], axis=1)
            panels = jnp.concatenate([panel_of(leaf, slot), panel_of(leaf, slot + 1)], axis=0)
            total = total + dot(both, panels)
        result = near_ref[leaf] + dot(row_ref[leaf], total.astype(jnp.bfloat16))
        out_ref[pl.ds(leaf * rows, rows), :] = result.astype(jnp.bfloat16)


def across_kernel(
    list_ref, count_ref, blocks_hbm, near_ref, across_ref,
    total_ref,
    blocks, order, sems,
):
    leaves, _, rows, _ = blocks.shape
    place = lax.div(list_ref[0, 0], leaves)
    found = [
        pick_slots(
            list_ref, count_ref, blocks_hbm, blocks, sems, order, leaf,
            lambda cluster: (cluster ^ place) > 1,
        )
        for leaf in range(leaves)
    ]
    total_ref[...] = near_ref[...]

    def panel_of(column):
        panel = across_ref[rows_at(column & (leaves - 1), rows), :]
        return jnp.where(column < 0, jnp.zeros_like(panel), panel)

    for leaf in range(leaves):
        add_slots(total_ref, blocks_hbm, blocks, sems, order, leaf, found[leaf], panel_of)


def call(kernel, name, outs, specs, args, scratch=(), flops=0, moved=0, limit=4):
    many = isinstance(outs, tuple)
    return pl.pallas_call(
        kernel,
        out_shape=outs,
        in_specs=specs,
        out_specs=(VMEM,) * len(outs) if many else VMEM,
        scratch_shapes=list(scratch),
        cost_estimate=pl.CostEstimate(flops=flops, bytes_accessed=moved, transcendentals=0),
        compiler_params=pltpu.CompilerParams(vmem_limit_bytes=limit * MIB),
        name=name,
    )(*args)


def body(
    source,
    near_blocks,
    near_list,
    near_count,
    col_basis,
    row_basis,
    transfer,
    far_list,
    far_coupling,
    coarse_list,
    coarse_coupling,
):
    leaves, slots, rows, _ = near_blocks.shape
    rank = col_basis.shape[2]
    width = source.shape[1]
    count = lax.axis_size("row")
    far_slots = far_coupling.shape[1]

    def send(value, target):
        pairs = [(d, target(d)) for d in range(count) if 0 <= target(d) < count]
        return lax.ppermute(value, "row", pairs)

    def panel(blocks, dtype=jnp.bfloat16):
        return jax.ShapeDtypeStruct((blocks * rank, width), dtype)

    share, coef, parent = call(
        up_kernel, "up",
        (jax.ShapeDtypeStruct((leaves * (rows + rank), width), jnp.bfloat16), panel(leaves), panel(1)),
        [VMEM] * 3, (source, col_basis, transfer),
        flops=2 * leaves * rank * width * (rows + rank),
        moved=2 * leaves * rows * (width + rank), limit=8,
    )
    layers = [send(parent, lambda d, bit=bit: d ^ bit) for bit in (4, 8, 12)]
    share_other = send(share, lambda d: d ^ 1)
    level = send(coef, lambda d: d ^ 2)
    across = send(source, lambda d: d + 1 if d & 1 else d - 1)

    picked = [
        pltpu.VMEM(near_blocks.shape, jnp.bfloat16),
        pltpu.SMEM((leaves, slots + CHUNK), jnp.int32),
        pltpu.SemaphoreType.DMA((leaves, slots)),
    ]
    near = call(
        near_kernel, "near", jax.ShapeDtypeStruct((leaves, rows, width), jnp.float32),
        [SMEM, SMEM] + [ANY] * 3, (near_list, near_count, near_blocks, share, share_other),
        scratch=[
            picked[0],
            pltpu.VMEM(((2 * leaves + 1) * rows, width), jnp.bfloat16),
            *picked[1:],
            pltpu.SemaphoreType.DMA((2,)),
        ],
        limit=48,
    )
    column, relay = call(
        join_kernel, "column", (panel(GROUP // 4), panel(leaves)), [VMEM] * 5 + [ANY],
        (parent, *layers, level, near),
    )
    beside = send(column, lambda d: d ^ 2)
    layer = send(relay, lambda d: d - 4 if d & 2 else d + 4)
    mine = call(
        pass_kernel, "pass", panel(GROUP // 2 + leaves), [SMEM] + [VMEM] * 4,
        (near_list, column, beside, level, layer),
    )
    theirs = send(mine, lambda d: d ^ 1)
    near = call(
        across_kernel, "across", jax.ShapeDtypeStruct((leaves, rows, width), jnp.float32),
        [SMEM] * 2 + [ANY] + [VMEM] * 2, (near_list, near_count, near_blocks, near, across),
        scratch=picked,
        flops=16 * leaves * slots * rows * rows * width,
        moved=2 * leaves * slots * rows * rows, limit=48,
    )
    return call(
        down_kernel, "down", jax.ShapeDtypeStruct(source.shape, jnp.bfloat16),
        [SMEM] * 3 + [VMEM] * 5 + [ANY] * 3 + [VMEM] * 2,
        (
            far_list, coarse_list, near_list, transfer, far_coupling, coarse_coupling, row_basis,
            near, level, layer, share_other, mine, theirs,
        ),
        scratch=[
            pltpu.VMEM((4 * leaves * rank, width), jnp.bfloat16),
            pltpu.SemaphoreType.DMA((4,)),
        ],
        flops=2 * leaves * (far_slots + 4) * rank * rank * width,
        moved=2 * leaves * far_slots * rank * rank, limit=12,
    )


def solution(mesh):
    placed = (
        P(("clip", "row"), None),
        P(("clip", "row"), None, None, None),
        P(("clip", "row"), None),
        P(("clip", "row")),
        P(("clip", "row"), None, None),
        P(("clip", "row"), None, None),
        P(("clip", "row"), None, None),
        P(("clip", "row"), None),
        P(("clip", "row"), None, None, None),
        P(("clip", "row"), None),
        P(("clip", "row"), None, None, None),
    )
    return jax.shard_map(
        body, mesh=mesh, in_specs=placed, out_specs=P(("clip", "row"), None), check_vma=False
    )
```

```python
import jax
import jax.numpy as jnp
from jax import lax
from jax.experimental import pallas as pl
from jax.experimental.pallas import tpu as pltpu
from jax.sharding import PartitionSpec as P

GROUP = 16
CHUNK = 4
MIB = 2**20

VMEM = pl.BlockSpec(memory_space=pltpu.VMEM)
SMEM = pl.BlockSpec(memory_space=pltpu.SMEM)
ANY = pl.BlockSpec(memory_space=pl.ANY)


def dot(a, b):
    return jnp.dot(a, b, preferred_element_type=jnp.float32)


def dot_t(a, b):
    return lax.dot_general(
        a, b, (((0,), (0,)), ((), ())), preferred_element_type=jnp.float32
    )


def rows_at(index, rows):
    return pl.ds(pl.multiple_of(index * rows, rows), rows)


def up_kernel(source_ref, col_ref, transfer_ref, share_ref, coef_ref, parent_ref):
    leaves, rows, rank = col_ref.shape
    total = None
    for leaf in range(leaves):
        panel = source_ref[pl.ds(leaf * rows, rows), :]
        share_ref[pl.ds(leaf * rows, rows), :] = panel
        coef = dot_t(col_ref[leaf], panel).astype(jnp.bfloat16)
        coef_ref[pl.ds(leaf * rank, rank), :] = coef
        share_ref[pl.ds(leaves * rows + leaf * rank, rank), :] = coef
        term = dot_t(transfer_ref[leaf], coef)
        total = term if total is None else total + term
    parent_ref[...] = total.astype(jnp.bfloat16)


def join_kernel(*refs):
    *pieces, level_ref, _, out_ref, relay_ref = refs
    relay_ref[...] = level_ref[...]
    at = 0
    for ref in pieces:
        out_ref[pl.ds(at, ref.shape[0]), :] = ref[...]
        at += ref.shape[0]


def pick_kernel(list_ref, level_ref, layer_ref, out_ref):
    corner = lax.div(list_ref[0, 0], list_ref.shape[0]) & 3
    level = (corner == 0) | (corner == 3)
    out_ref[...] = jnp.where(level, level_ref[...], layer_ref[...])


def hand_kernel(in_ref, _, __, out_ref):
    out_ref[...] = in_ref[...]


def pick_slots(list_ref, count_ref, blocks_hbm, blocks, sems, order_ref, leaf, keep):
    leaves, _ = list_ref.shape

    def step(slot, found):
        column = list_ref[leaf, slot]
        kept = keep(lax.div(column, leaves))

        @pl.when(kept)
        def _():
            order_ref[leaf, found] = column
            pltpu.make_async_copy(
                blocks_hbm.at[leaf, slot], blocks.at[leaf, found], sems.at[leaf, found]
            ).start()

        return found + kept.astype(jnp.int32)

    found = lax.fori_loop(0, count_ref[leaf], step, 0)
    for pad in range(CHUNK):
        order_ref[leaf, found + pad] = -1
    return found


def add_slots(total_ref, blocks_hbm, blocks, sems, order_ref, leaf, found, panel_of):
    for first in range(0, blocks.shape[1], CHUNK):
        @pl.when(first < found)
        def _():
            for n in range(first, first + CHUNK):
                @pl.when(n < found)
                def _():
                    pltpu.make_async_copy(
                        blocks_hbm.at[leaf, 0], blocks.at[leaf, n], sems.at[leaf, n]
                    ).wait()
            total = total_ref[leaf]
            for n in range(first, first + CHUNK):
                block = blocks[leaf, jnp.where(n < found, n, 0)]
                total = total + dot(block, panel_of(order_ref[leaf, n]))
            total_ref[leaf] = total


def near_kernel(
    list_ref, count_ref, blocks_hbm, own_ref, share_ref,
    near_ref,
    blocks, panels, order, block_sems, panel_sems,
):
    leaves, _, rows, _ = blocks.shape
    size = leaves * rows
    place = lax.div(list_ref[0, 0], leaves)
    pairs = [
        pltpu.make_async_copy(
            ref.at[pl.ds(0, size)], panels.at[pl.ds(which * size, size)], panel_sems.at[which]
        )
        for which, ref in enumerate((own_ref, share_ref))
    ]
    for copy in pairs:
        copy.start()
    found = [
        pick_slots(
            list_ref, count_ref, blocks_hbm, blocks, block_sems, order, leaf,
            lambda cluster: (cluster ^ place) <= 1,
        )
        for leaf in range(leaves)
    ]
    near_ref[...] = jnp.zeros(near_ref.shape, near_ref.dtype)
    panels[pl.ds(2 * size, rows), :] = jnp.zeros((rows, panels.shape[1]), panels.dtype)
    for copy in pairs:
        copy.wait()

    def panel_of(column):
        index = (lax.div(column, leaves) ^ place) * leaves + (column & (leaves - 1))
        return panels[rows_at(jnp.where(column < 0, 2 * leaves, index), rows), :]

    for leaf in range(leaves):
        add_slots(near_ref, blocks_hbm, blocks, block_sems, order, leaf, found[leaf], panel_of)


def far_kernel(
    list_ref, near_list_ref, coupling_ref, level_ref, layer_ref, share_ref, passed_ref,
    far_ref,
    coefs, sems,
):
    leaves, slots, rank, _ = coupling_ref.shape
    size = leaves * rank
    place = lax.div(near_list_ref[0, 0], leaves)
    beyond = jnp.where((place & 2) == 0, place - 2, place + 2)
    copies = [
        pltpu.make_async_copy(
            ref.at[pl.ds(ref.shape[0] - size, size)], coefs.at[pl.ds(n * size, size)], sems.at[n]
        )
        for n, ref in enumerate((level_ref, layer_ref, share_ref, passed_ref))
    ]
    for copy in copies:
        copy.start()
    for copy in copies:
        copy.wait()

    def panel_of(leaf, slot):
        column = list_ref[leaf, slot]
        cluster = lax.div(column, leaves)
        which = jnp.where(
            cluster == (place ^ 2), 0,
            jnp.where(cluster == beyond, 1, jnp.where(cluster == (place ^ 1), 2, 3)),
        )
        return coefs[rows_at(which * leaves + column - cluster * leaves, rank), :]

    for leaf in range(leaves):
        total = None
        for slot in range(0, slots, 2):
            both = jnp.concatenate([coupling_ref[leaf, slot], coupling_ref[leaf, slot + 1]], axis=1)
            panels = jnp.concatenate([panel_of(leaf, slot), panel_of(leaf, slot + 1)], axis=0)
            term = dot(both, panels)
            total = term if total is None else total + term
        far_ref[pl.ds(leaf * rank, rank), :] = total


def down_kernel(
    list_ref, near_list_ref, transfer_ref, coupling_ref, row_ref, near_ref, far_ref,
    column_ref, beside_ref, their_column_ref, their_beside_ref,
    out_ref,
):
    leaves, rows, rank = row_ref.shape
    local = lax.div(near_list_ref[0, 0], leaves) & (GROUP - 1)
    total = None
    for slot in range(list_ref.shape[1]):
        flip = (list_ref[0, slot] & (GROUP - 1)) ^ local
        where = rows_at(flip >> 2, rank)
        mine = jnp.where((flip & 2) == 0, column_ref[where, :], beside_ref[where, :])
        theirs = jnp.where((flip & 2) == 0, their_column_ref[where, :], their_beside_ref[where, :])
        term = dot(coupling_ref[0, slot], jnp.where((flip & 1) == 0, mine, theirs))
        total = term if total is None else total + term
    high = total.astype(jnp.bfloat16)
    low = (total - high.astype(jnp.float32)).astype(jnp.bfloat16)
    coarse = jnp.concatenate([high, low], axis=0)
    for leaf in range(leaves):
        matrix = transfer_ref[leaf]
        spread = dot(jnp.concatenate([matrix, matrix], axis=1), coarse)
        down = (far_ref[pl.ds(leaf * rank, rank), :] + spread).astype(jnp.bfloat16)
        result = near_ref[leaf] + dot(row_ref[leaf], down)
        out_ref[pl.ds(leaf * rows, rows), :] = result.astype(jnp.bfloat16)


def across_kernel(
    list_ref, count_ref, blocks_hbm, near_ref, across_ref,
    total_ref,
    blocks, order, sems,
):
    leaves, _, rows, _ = blocks.shape
    place = lax.div(list_ref[0, 0], leaves)
    found = [
        pick_slots(
            list_ref, count_ref, blocks_hbm, blocks, sems, order, leaf,
            lambda cluster: (cluster ^ place) > 1,
        )
        for leaf in range(leaves)
    ]
    total_ref[...] = near_ref[...]

    def panel_of(column):
        panel = across_ref[rows_at(column & (leaves - 1), rows), :]
        return jnp.where(column < 0, jnp.zeros_like(panel), panel)

    for leaf in range(leaves):
        add_slots(total_ref, blocks_hbm, blocks, sems, order, leaf, found[leaf], panel_of)


def call(kernel, name, outs, specs, args, scratch=(), flops=0, moved=0, limit=4):
    many = isinstance(outs, tuple)
    return pl.pallas_call(
        kernel,
        out_shape=outs,
        in_specs=specs,
        out_specs=(VMEM,) * len(outs) if many else VMEM,
        scratch_shapes=list(scratch),
        cost_estimate=pl.CostEstimate(flops=flops, bytes_accessed=moved, transcendentals=0),
        compiler_params=pltpu.CompilerParams(vmem_limit_bytes=limit * MIB),
        name=name,
    )(*args)


def body(
    source,
    near_blocks,
    near_list,
    near_count,
    col_basis,
    row_basis,
    transfer,
    far_list,
    far_coupling,
    coarse_list,
    coarse_coupling,
):
    leaves, slots, rows, _ = near_blocks.shape
    rank = col_basis.shape[2]
    width = source.shape[1]
    count = lax.axis_size("row")
    far_slots = far_coupling.shape[1]

    def send(value, target):
        pairs = [(d, target(d)) for d in range(count) if 0 <= target(d) < count]
        return lax.ppermute(value, "row", pairs)

    def panel(blocks, dtype=jnp.bfloat16):
        return jax.ShapeDtypeStruct((blocks * rank, width), dtype)

    share, coef, parent = call(
        up_kernel, "up",
        (jax.ShapeDtypeStruct((leaves * (rows + rank), width), jnp.bfloat16), panel(leaves), panel(1)),
        [VMEM] * 3, (source, col_basis, transfer),
        flops=2 * leaves * rank * width * (rows + rank),
        moved=2 * leaves * rows * (width + rank), limit=8,
    )
    layers = [send(parent, lambda d, bit=bit: d ^ bit) for bit in (4, 8, 12)]
    share_other = send(share, lambda d: d ^ 1)
    level = send(coef, lambda d: d ^ 2)
    across = send(source, lambda d: d + 1 if d & 1 else d - 1)

    picked = [
        pltpu.VMEM(near_blocks.shape, jnp.bfloat16),
        pltpu.SMEM((leaves, slots + CHUNK), jnp.int32),
        pltpu.SemaphoreType.DMA((leaves, slots)),
    ]
    near = call(
        near_kernel, "near", jax.ShapeDtypeStruct((leaves, rows, width), jnp.float32),
        [SMEM, SMEM] + [ANY] * 3, (near_list, near_count, near_blocks, share, share_other),
        scratch=[
            picked[0],
            pltpu.VMEM(((2 * leaves + 1) * rows, width), jnp.bfloat16),
            *picked[1:],
            pltpu.SemaphoreType.DMA((2,)),
        ],
        limit=48,
    )
    column, relay = call(
        join_kernel, "column", (panel(GROUP // 4), panel(leaves)), [VMEM] * 5 + [ANY],
        (parent, *layers, level, near),
    )
    beside = send(column, lambda d: d ^ 2)
    layer = send(relay, lambda d: d - 4 if d & 2 else d + 4)
    their_column = send(column, lambda d: d ^ 1)
    picked_coef = call(
        pick_kernel, "pick", panel(leaves), [SMEM] + [VMEM] * 2, (near_list, level, layer)
    )
    passed = send(picked_coef, lambda d: d ^ 1)
    near = call(
        across_kernel, "across", jax.ShapeDtypeStruct((leaves, rows, width), jnp.float32),
        [SMEM] * 2 + [ANY] + [VMEM] * 2, (near_list, near_count, near_blocks, near, across),
        scratch=picked,
        flops=16 * leaves * slots * rows * rows * width,
        moved=2 * leaves * slots * rows * rows, limit=48,
    )
    far = call(
        far_kernel, "far", panel(leaves, jnp.float32), [SMEM] * 2 + [VMEM] + [ANY] * 4,
        (far_list, near_list, far_coupling, level, layer, share_other, passed),
        scratch=[
            pltpu.VMEM((4 * leaves * rank, width), jnp.bfloat16),
            pltpu.SemaphoreType.DMA((4,)),
        ],
        flops=2 * leaves * far_slots * rank * rank * width,
        moved=2 * leaves * far_slots * rank * rank, limit=10,
    )
    handed = call(
        hand_kernel, "hand", panel(GROUP // 4), [VMEM] + [ANY] * 2, (beside, far, near)
    )
    their_beside = send(handed, lambda d: d ^ 1)
    return call(
        down_kernel, "down", jax.ShapeDtypeStruct(source.shape, jnp.bfloat16),
        [SMEM] * 2 + [VMEM] * 9,
        (
            coarse_list, near_list, transfer, coarse_coupling, row_basis, near, far,
            column, handed, their_column, their_beside,
        ),
        flops=8 * leaves * rank * rank * width,
        moved=4 * leaves * rows * width, limit=8,
    )


def solution(mesh):
    placed = (
        P(("clip", "row"), None),
        P(("clip", "row"), None, None, None),
        P(("clip", "row"), None),
        P(("clip", "row")),
        P(("clip", "row"), None, None),
        P(("clip", "row"), None, None),
        P(("clip", "row"), None, None),
        P(("clip", "row"), None),
        P(("clip", "row"), None, None, None),
        P(("clip", "row"), None),
        P(("clip", "row"), None, None, None),
    )
    return jax.shard_map(
        body, mesh=mesh, in_specs=placed, out_specs=P(("clip", "row"), None), check_vma=False
    )
```

```python
import jax
import jax.numpy as jnp
from jax import lax
from jax.experimental import pallas as pl
from jax.experimental.pallas import tpu as pltpu
from jax.sharding import PartitionSpec as P

GROUP = 16
CHUNK = 4
MIB = 2**20

VMEM = pl.BlockSpec(memory_space=pltpu.VMEM)
SMEM = pl.BlockSpec(memory_space=pltpu.SMEM)
ANY = pl.BlockSpec(memory_space=pl.ANY)


def dot(a, b):
    return jnp.dot(a, b, preferred_element_type=jnp.float32)


def dot_t(a, b):
    return lax.dot_general(
        a, b, (((0,), (0,)), ((), ())), preferred_element_type=jnp.float32
    )


def rows_at(index, rows):
    return pl.ds(pl.multiple_of(index * rows, rows), rows)


def up_kernel(source_ref, col_ref, transfer_ref, share_ref, coef_ref, parent_ref):
    leaves, rows, rank = col_ref.shape
    total = None
    for leaf in range(leaves):
        panel = source_ref[pl.ds(leaf * rows, rows), :]
        share_ref[pl.ds(leaf * rows, rows), :] = panel
        coef = dot_t(col_ref[leaf], panel).astype(jnp.bfloat16)
        coef_ref[pl.ds(leaf * rank, rank), :] = coef
        share_ref[pl.ds(leaves * rows + leaf * rank, rank), :] = coef
        term = dot_t(transfer_ref[leaf], coef)
        total = term if total is None else total + term
    parent_ref[...] = total.astype(jnp.bfloat16)


def join_kernel(*refs):
    *pieces, out_ref = refs
    at = 0
    for ref in pieces:
        out_ref[pl.ds(at, ref.shape[0]), :] = ref[...]
        at += ref.shape[0]


def pick_kernel(list_ref, level_ref, layer_ref, _, out_ref):
    corner = lax.div(list_ref[0, 0], list_ref.shape[0]) & 3
    level = (corner == 0) | (corner == 3)
    out_ref[...] = jnp.where(level, level_ref[...], layer_ref[...])


def hand_kernel(in_ref, _, out_ref):
    out_ref[...] = in_ref[pl.ds(0, out_ref.shape[0]), :]


def pick_slots(list_ref, count_ref, blocks_hbm, blocks, sems, order_ref, leaf, keep):
    leaves, _ = list_ref.shape

    def step(slot, found):
        column = list_ref[leaf, slot]
        kept = keep(lax.div(column, leaves))

        @pl.when(kept)
        def _():
            order_ref[leaf, found] = column
            pltpu.make_async_copy(
                blocks_hbm.at[leaf, slot], blocks.at[leaf, found], sems.at[leaf, found]
            ).start()

        return found + kept.astype(jnp.int32)

    found = lax.fori_loop(0, count_ref[leaf], step, 0)
    for pad in range(CHUNK):
        order_ref[leaf, found + pad] = -1
    return found


def add_slots(total_ref, blocks_hbm, blocks, sems, order_ref, leaf, found, panel_of):
    for first in range(0, blocks.shape[1], CHUNK):
        @pl.when(first < found)
        def _():
            for n in range(first, first + CHUNK):
                @pl.when(n < found)
                def _():
                    pltpu.make_async_copy(
                        blocks_hbm.at[leaf, 0], blocks.at[leaf, n], sems.at[leaf, n]
                    ).wait()
            total = total_ref[leaf]
            for n in range(first, first + CHUNK):
                block = blocks[leaf, jnp.where(n < found, n, 0)]
                total = total + dot(block, panel_of(order_ref[leaf, n]))
            total_ref[leaf] = total


def near_kernel(
    list_ref, count_ref, blocks_hbm, own_ref, share_ref,
    near_ref,
    blocks, panels, order, block_sems, panel_sems,
):
    leaves, _, rows, _ = blocks.shape
    size = leaves * rows
    place = lax.div(list_ref[0, 0], leaves)
    pairs = [
        pltpu.make_async_copy(
            ref.at[pl.ds(0, size)], panels.at[pl.ds(which * size, size)], panel_sems.at[which]
        )
        for which, ref in enumerate((own_ref, share_ref))
    ]
    for copy in pairs:
        copy.start()
    found = [
        pick_slots(
            list_ref, count_ref, blocks_hbm, blocks, block_sems, order, leaf,
            lambda cluster: (cluster ^ place) <= 1,
        )
        for leaf in range(leaves)
    ]
    near_ref[...] = jnp.zeros(near_ref.shape, near_ref.dtype)
    panels[pl.ds(2 * size, rows), :] = jnp.zeros((rows, panels.shape[1]), panels.dtype)
    for copy in pairs:
        copy.wait()

    def panel_of(column):
        index = (lax.div(column, leaves) ^ place) * leaves + (column & (leaves - 1))
        return panels[rows_at(jnp.where(column < 0, 2 * leaves, index), rows), :]

    for leaf in range(leaves):
        add_slots(near_ref, blocks_hbm, blocks, block_sems, order, leaf, found[leaf], panel_of)


def far_kernel(
    list_ref, near_list_ref, coupling_ref, level_ref, layer_ref, share_ref, passed_ref,
    far_ref,
    coefs, sems,
):
    leaves, slots, rank, _ = coupling_ref.shape
    size = leaves * rank
    place = lax.div(near_list_ref[0, 0], leaves)
    beyond = jnp.where((place & 2) == 0, place - 2, place + 2)
    copies = [
        pltpu.make_async_copy(
            ref.at[pl.ds(ref.shape[0] - size, size)], coefs.at[pl.ds(n * size, size)], sems.at[n]
        )
        for n, ref in enumerate((level_ref, layer_ref, share_ref, passed_ref))
    ]
    for copy in copies:
        copy.start()
    for copy in copies:
        copy.wait()

    def panel_of(leaf, slot):
        column = list_ref[leaf, slot]
        cluster = lax.div(column, leaves)
        which = jnp.where(
            cluster == (place ^ 2), 0,
            jnp.where(cluster == beyond, 1, jnp.where(cluster == (place ^ 1), 2, 3)),
        )
        return coefs[rows_at(which * leaves + column - cluster * leaves, rank), :]

    for leaf in range(leaves):
        total = None
        for slot in range(0, slots, 2):
            both = jnp.concatenate([coupling_ref[leaf, slot], coupling_ref[leaf, slot + 1]], axis=1)
            panels = jnp.concatenate([panel_of(leaf, slot), panel_of(leaf, slot + 1)], axis=0)
            term = dot(both, panels)
            total = term if total is None else total + term
        far_ref[pl.ds(leaf * rank, rank), :] = total


def down_kernel(
    list_ref, near_list_ref, transfer_ref, coupling_ref, row_ref, near_ref, far_ref,
    column_ref, beside_ref, their_column_ref, their_beside_ref,
    out_ref,
):
    leaves, rows, rank = row_ref.shape
    local = lax.div(near_list_ref[0, 0], leaves) & (GROUP - 1)
    total = None
    for slot in range(list_ref.shape[1]):
        flip = (list_ref[0, slot] & (GROUP - 1)) ^ local
        where = rows_at(flip >> 2, rank)
        mine = jnp.where((flip & 2) == 0, column_ref[where, :], beside_ref[where, :])
        theirs = jnp.where((flip & 2) == 0, their_column_ref[where, :], their_beside_ref[where, :])
        term = dot(coupling_ref[0, slot], jnp.where((flip & 1) == 0, mine, theirs))
        total = term if total is None else total + term
    high = total.astype(jnp.bfloat16)
    low = (total - high.astype(jnp.float32)).astype(jnp.bfloat16)
    coarse = jnp.concatenate([high, low], axis=0)
    for leaf in range(leaves):
        matrix = transfer_ref[leaf]
        spread = dot(jnp.concatenate([matrix, matrix], axis=1), coarse)
        down = (far_ref[pl.ds(leaf * rank, rank), :] + spread).astype(jnp.bfloat16)
        result = near_ref[leaf] + dot(row_ref[leaf], down)
        out_ref[pl.ds(leaf * rows, rows), :] = result.astype(jnp.bfloat16)


def across_kernel(
    list_ref, count_ref, blocks_hbm, near_ref, across_ref, _,
    total_ref,
    blocks, order, sems,
):
    leaves, _, rows, _ = blocks.shape
    place = lax.div(list_ref[0, 0], leaves)
    found = [
        pick_slots(
            list_ref, count_ref, blocks_hbm, blocks, sems, order, leaf,
            lambda cluster: (cluster ^ place) > 1,
        )
        for leaf in range(leaves)
    ]
    total_ref[...] = near_ref[...]

    def panel_of(column):
        panel = across_ref[rows_at(column & (leaves - 1), rows), :]
        return jnp.where(column < 0, jnp.zeros_like(panel), panel)

    for leaf in range(leaves):
        add_slots(total_ref, blocks_hbm, blocks, sems, order, leaf, found[leaf], panel_of)


def call(kernel, name, outs, specs, args, scratch=(), flops=0, moved=0, limit=4):
    many = isinstance(outs, tuple)
    return pl.pallas_call(
        kernel,
        out_shape=outs,
        in_specs=specs,
        out_specs=(VMEM,) * len(outs) if many else VMEM,
        scratch_shapes=list(scratch),
        cost_estimate=pl.CostEstimate(flops=flops, bytes_accessed=moved, transcendentals=0),
        compiler_params=pltpu.CompilerParams(vmem_limit_bytes=limit * MIB),
        name=name,
    )(*args)


def body(
    source,
    near_blocks,
    near_list,
    near_count,
    col_basis,
    row_basis,
    transfer,
    far_list,
    far_coupling,
    coarse_list,
    coarse_coupling,
):
    leaves, slots, rows, _ = near_blocks.shape
    rank = col_basis.shape[2]
    width = source.shape[1]
    count = lax.axis_size("row")
    far_slots = far_coupling.shape[1]

    def send(value, target):
        pairs = [(d, target(d)) for d in range(count) if 0 <= target(d) < count]
        return lax.ppermute(value, "row", pairs)

    def panel(blocks, dtype=jnp.bfloat16):
        return jax.ShapeDtypeStruct((blocks * rank, width), dtype)

    share, coef, parent = call(
        up_kernel, "up",
        (jax.ShapeDtypeStruct((leaves * (rows + rank), width), jnp.bfloat16), panel(leaves), panel(1)),
        [VMEM] * 3, (source, col_basis, transfer),
        flops=2 * leaves * rank * width * (rows + rank),
        moved=2 * leaves * rows * (width + rank), limit=8,
    )
    layers = [send(parent, lambda d, bit=bit: d ^ bit) for bit in (4, 8, 12)]
    share_other = send(share, lambda d: d ^ 1)
    level = send(coef, lambda d: d ^ 2)
    panels = call(
        hand_kernel, "panels", jax.ShapeDtypeStruct(source.shape, jnp.bfloat16), [VMEM, ANY],
        (share, share_other),
    )
    across = send(panels, lambda d: d + 1 if d & 1 else d - 1)

    picked = [
        pltpu.VMEM(near_blocks.shape, jnp.bfloat16),
        pltpu.SMEM((leaves, slots + CHUNK), jnp.int32),
        pltpu.SemaphoreType.DMA((leaves, slots)),
    ]
    near = call(
        near_kernel, "near", jax.ShapeDtypeStruct((leaves, rows, width), jnp.float32),
        [SMEM, SMEM] + [ANY] * 3, (near_list, near_count, near_blocks, share, share_other),
        scratch=[
            picked[0],
            pltpu.VMEM(((2 * leaves + 1) * rows, width), jnp.bfloat16),
            *picked[1:],
            pltpu.SemaphoreType.DMA((2,)),
        ],
        limit=48,
    )
    relay = call(hand_kernel, "relay", panel(leaves), [VMEM, ANY], (level, near))
    layer = send(relay, lambda d: d - 4 if d & 2 else d + 4)
    column = call(join_kernel, "column", panel(GROUP // 4), [VMEM] * 4, (parent, *layers))
    beside = send(column, lambda d: d ^ 2)
    their_column = send(column, lambda d: d ^ 1)
    near = call(
        across_kernel, "across", jax.ShapeDtypeStruct((leaves, rows, width), jnp.float32),
        [SMEM] * 2 + [ANY] + [VMEM] * 2 + [ANY],
        (near_list, near_count, near_blocks, near, across, column),
        scratch=picked,
        flops=leaves * slots * rows * rows * width, moved=0, limit=48,
    )
    picked_coef = call(
        pick_kernel, "pick", panel(leaves), [SMEM] + [VMEM] * 2 + [ANY], (near_list, level, layer, near)
    )
    passed = send(picked_coef, lambda d: d ^ 1)
    far = call(
        far_kernel, "far", panel(leaves, jnp.float32), [SMEM] * 2 + [VMEM] + [ANY] * 4,
        (far_list, near_list, far_coupling, level, layer, share_other, passed),
        scratch=[
            pltpu.VMEM((4 * leaves * rank, width), jnp.bfloat16),
            pltpu.SemaphoreType.DMA((4,)),
        ],
        flops=2 * leaves * far_slots * rank * rank * width,
        moved=2 * leaves * far_slots * rank * rank, limit=10,
    )
    their_beside = send(beside, lambda d: d ^ 1)
    return call(
        down_kernel, "down", jax.ShapeDtypeStruct(source.shape, jnp.bfloat16),
        [SMEM] * 2 + [VMEM] * 9,
        (
            coarse_list, near_list, transfer, coarse_coupling, row_basis, near, far,
            column, beside, their_column, their_beside,
        ),
        flops=8 * leaves * rank * rank * width,
        moved=4 * leaves * rows * width, limit=8,
    )


def solution(mesh):
    placed = (
        P(("clip", "row"), None),
        P(("clip", "row"), None, None, None),
        P(("clip", "row"), None),
        P(("clip", "row")),
        P(("clip", "row"), None, None),
        P(("clip", "row"), None, None),
        P(("clip", "row"), None, None),
        P(("clip", "row"), None),
        P(("clip", "row"), None, None, None),
        P(("clip", "row"), None),
        P(("clip", "row"), None, None, None),
    )
    return jax.shard_map(
        body, mesh=mesh, in_specs=placed, out_specs=P(("clip", "row"), None), check_vma=False
    )
```

```python
import jax
import jax.numpy as jnp
from jax import lax
from jax.experimental import pallas as pl
from jax.experimental.pallas import tpu as pltpu
from jax.sharding import PartitionSpec as P

GROUP = 16
CHUNK = 4
AHEAD = 4
MIB = 2**20

VMEM = pl.BlockSpec(memory_space=pltpu.VMEM)
SMEM = pl.BlockSpec(memory_space=pltpu.SMEM)
ANY = pl.BlockSpec(memory_space=pl.ANY)


def dot(a, b):
    return jnp.dot(a, b, preferred_element_type=jnp.float32)


def dot_t(a, b):
    return lax.dot_general(
        a, b, (((0,), (0,)), ((), ())), preferred_element_type=jnp.float32
    )


def rows_at(index, rows):
    return pl.ds(pl.multiple_of(index * rows, rows), rows)


def up_kernel(source_ref, col_ref, transfer_ref, share_ref, coef_ref, parent_ref):
    leaves, rows, rank = col_ref.shape
    total = None
    for leaf in range(leaves):
        panel = source_ref[pl.ds(leaf * rows, rows), :]
        share_ref[pl.ds(leaf * rows, rows), :] = panel
        coef = dot_t(col_ref[leaf], panel).astype(jnp.bfloat16)
        coef_ref[pl.ds(leaf * rank, rank), :] = coef
        share_ref[pl.ds(leaves * rows + leaf * rank, rank), :] = coef
        term = dot_t(transfer_ref[leaf], coef)
        total = term if total is None else total + term
    parent_ref[...] = total.astype(jnp.bfloat16)


def join_kernel(*refs):
    *pieces, out_ref = refs
    at = 0
    for ref in pieces:
        out_ref[pl.ds(at, ref.shape[0]), :] = ref[...]
        at += ref.shape[0]


def pick_kernel(list_ref, level_ref, layer_ref, out_ref):
    corner = lax.div(list_ref[0, 0], list_ref.shape[0]) & 3
    level = (corner == 0) | (corner == 3)
    out_ref[...] = jnp.where(level, level_ref[...], layer_ref[...])


def hand_kernel(in_ref, *refs):
    out_ref = refs[-1]
    out_ref[...] = in_ref[pl.ds(0, out_ref.shape[0]), :]


def near_kernel(
    list_ref, count_ref, blocks_hbm, own_ref, share_ref, across_ref,
    near_ref,
    blocks, panels, block_sems, panel_sems,
):
    leaves, slots, rows, _ = blocks.shape
    chunks = slots // CHUNK
    size = leaves * rows
    place = lax.div(list_ref[0, 0], leaves)

    def live(step):
        return step % chunks * CHUNK < count_ref[step // chunks]

    def block_copy(step):
        leaf, chunk = step // chunks, step % chunks
        where = pl.ds(chunk * CHUNK, CHUNK)
        return pltpu.make_async_copy(
            blocks_hbm.at[leaf, where], blocks.at[leaf, where], block_sems.at[leaf, chunk]
        )

    def start(step):
        if step < leaves * chunks:
            @pl.when(live(step))
            def _():
                block_copy(step).start()

    pairs = [
        pltpu.make_async_copy(
            ref.at[pl.ds(0, size)], panels.at[pl.ds(which * size, size)], panel_sems.at[which]
        )
        for which, ref in enumerate((own_ref, share_ref, across_ref))
    ]
    for copy in pairs:
        copy.start()
    for step in range(AHEAD):
        start(step)
    panels[pl.ds(3 * size, rows), :] = jnp.zeros((rows, panels.shape[1]), panels.dtype)
    for copy in pairs:
        copy.wait()

    def panel_of(leaf, slot):
        column = list_ref[leaf, slot]
        which = jnp.minimum(lax.div(column, leaves) ^ place, 2)
        index = which * leaves + (column & (leaves - 1))
        index = jnp.where(slot < count_ref[leaf], index, 3 * leaves)
        return panels[rows_at(index, rows), :]

    for step in range(leaves * chunks):
        leaf, chunk = step // chunks, step % chunks
        start(step + AHEAD)

        @pl.when(live(step))
        def _():
            block_copy(step).wait()
            total = None if chunk == 0 else near_ref[leaf]
            for slot in range(chunk * CHUNK, (chunk + 1) * CHUNK):
                term = dot(blocks[leaf, slot], panel_of(leaf, slot))
                total = term if total is None else total + term
            near_ref[leaf] = total


def far_kernel(
    list_ref, near_list_ref, coupling_ref, level_ref, layer_ref, share_ref, passed_ref,
    far_ref,
    coefs, sems,
):
    leaves, slots, rank, _ = coupling_ref.shape
    size = leaves * rank
    place = lax.div(near_list_ref[0, 0], leaves)
    beyond = jnp.where((place & 2) == 0, place - 2, place + 2)
    copies = [
        pltpu.make_async_copy(
            ref.at[pl.ds(ref.shape[0] - size, size)], coefs.at[pl.ds(n * size, size)], sems.at[n]
        )
        for n, ref in enumerate((level_ref, layer_ref, share_ref, passed_ref))
    ]
    for copy in copies:
        copy.start()
    for copy in copies:
        copy.wait()

    def panel_of(leaf, slot):
        column = list_ref[leaf, slot]
        cluster = lax.div(column, leaves)
        which = jnp.where(
            cluster == (place ^ 2), 0,
            jnp.where(cluster == beyond, 1, jnp.where(cluster == (place ^ 1), 2, 3)),
        )
        return coefs[rows_at(which * leaves + column - cluster * leaves, rank), :]

    for leaf in range(leaves):
        total = None
        for slot in range(0, slots, 2):
            both = jnp.concatenate([coupling_ref[leaf, slot], coupling_ref[leaf, slot + 1]], axis=1)
            panels = jnp.concatenate([panel_of(leaf, slot), panel_of(leaf, slot + 1)], axis=0)
            term = dot(both, panels)
            total = term if total is None else total + term
        far_ref[pl.ds(leaf * rank, rank), :] = total


def down_kernel(
    list_ref, near_list_ref, transfer_ref, coupling_ref, row_ref, near_ref, far_ref,
    column_ref, beside_ref, their_column_ref, their_beside_ref,
    out_ref,
):
    leaves, rows, rank = row_ref.shape
    local = lax.div(near_list_ref[0, 0], leaves) & (GROUP - 1)
    total = None
    for slot in range(list_ref.shape[1]):
        flip = (list_ref[0, slot] & (GROUP - 1)) ^ local
        where = rows_at(flip >> 2, rank)
        mine = jnp.where((flip & 2) == 0, column_ref[where, :], beside_ref[where, :])
        theirs = jnp.where((flip & 2) == 0, their_column_ref[where, :], their_beside_ref[where, :])
        term = dot(coupling_ref[0, slot], jnp.where((flip & 1) == 0, mine, theirs))
        total = term if total is None else total + term
    high = total.astype(jnp.bfloat16)
    low = (total - high.astype(jnp.float32)).astype(jnp.bfloat16)
    coarse = jnp.concatenate([high, low], axis=0)
    for leaf in range(leaves):
        matrix = transfer_ref[leaf]
        spread = dot(jnp.concatenate([matrix, matrix], axis=1), coarse)
        down = (far_ref[pl.ds(leaf * rank, rank), :] + spread).astype(jnp.bfloat16)
        result = near_ref[leaf] + dot(row_ref[leaf], down)
        out_ref[pl.ds(leaf * rows, rows), :] = result.astype(jnp.bfloat16)


def call(kernel, name, outs, specs, args, scratch=(), flops=0, moved=0, limit=4):
    many = isinstance(outs, tuple)
    return pl.pallas_call(
        kernel,
        out_shape=outs,
        in_specs=specs,
        out_specs=(VMEM,) * len(outs) if many else VMEM,
        scratch_shapes=list(scratch),
        cost_estimate=pl.CostEstimate(flops=flops, bytes_accessed=moved, transcendentals=0),
        compiler_params=pltpu.CompilerParams(vmem_limit_bytes=limit * MIB),
        name=name,
    )(*args)


def body(
    source,
    near_blocks,
    near_list,
    near_count,
    col_basis,
    row_basis,
    transfer,
    far_list,
    far_coupling,
    coarse_list,
    coarse_coupling,
):
    leaves, slots, rows, _ = near_blocks.shape
    rank = col_basis.shape[2]
    width = source.shape[1]
    count = lax.axis_size("row")
    far_slots = far_coupling.shape[1]

    def send(value, target):
        pairs = [(d, target(d)) for d in range(count) if 0 <= target(d) < count]
        return lax.ppermute(value, "row", pairs)

    def panel(blocks, dtype=jnp.bfloat16):
        return jax.ShapeDtypeStruct((blocks * rank, width), dtype)

    share, coef, parent = call(
        up_kernel, "up",
        (jax.ShapeDtypeStruct((leaves * (rows + rank), width), jnp.bfloat16), panel(leaves), panel(1)),
        [VMEM] * 3, (source, col_basis, transfer),
        flops=2 * leaves * rank * width * (rows + rank),
        moved=2 * leaves * rows * (width + rank), limit=8,
    )
    layers = [send(parent, lambda d, bit=bit: d ^ bit) for bit in (4, 8, 12)]
    share_other = send(share, lambda d: d ^ 1)
    level = send(coef, lambda d: d ^ 2)
    panels = call(
        hand_kernel, "panels", jax.ShapeDtypeStruct(source.shape, jnp.bfloat16), [VMEM] + [ANY] * 1,
        (share, share_other),
    )
    across = send(panels, lambda d: d + 1 if d & 1 else d - 1)

    layer = send(level, lambda d: d - 4 if d & 2 else d + 4)
    column = call(join_kernel, "column", panel(GROUP // 4), [VMEM] * 4, (parent, *layers))
    beside = send(column, lambda d: d ^ 2)
    their_column = send(column, lambda d: d ^ 1)
    near = call(
        near_kernel, "near", jax.ShapeDtypeStruct((leaves, rows, width), jnp.float32),
        [SMEM, SMEM] + [ANY] * 4,
        (near_list, near_count, near_blocks, share, share_other, across),
        scratch=[
            pltpu.VMEM(near_blocks.shape, jnp.bfloat16),
            pltpu.VMEM(((3 * leaves + 1) * rows, width), jnp.bfloat16),
            pltpu.SemaphoreType.DMA((leaves, slots // CHUNK)),
            pltpu.SemaphoreType.DMA((3,)),
        ],
        limit=48,
    )
    picked_coef = call(
        pick_kernel, "pick", panel(leaves), [SMEM] + [VMEM] * 2, (near_list, level, layer)
    )
    passed = send(picked_coef, lambda d: d ^ 1)
    far = call(
        far_kernel, "far", panel(leaves, jnp.float32), [SMEM] * 2 + [VMEM] + [ANY] * 4,
        (far_list, near_list, far_coupling, level, layer, share_other, passed),
        scratch=[
            pltpu.VMEM((4 * leaves * rank, width), jnp.bfloat16),
            pltpu.SemaphoreType.DMA((4,)),
        ],
        flops=2 * leaves * far_slots * rank * rank * width,
        moved=2 * leaves * far_slots * rank * rank, limit=10,
    )
    handed = call(hand_kernel, "hand", panel(GROUP // 4), [VMEM, ANY], (beside, near))
    their_beside = send(handed, lambda d: d ^ 1)
    return call(
        down_kernel, "down", jax.ShapeDtypeStruct(source.shape, jnp.bfloat16),
        [SMEM] * 2 + [VMEM] * 9,
        (
            coarse_list, near_list, transfer, coarse_coupling, row_basis, near, far,
            column, handed, their_column, their_beside,
        ),
        flops=8 * leaves * rank * rank * width,
        moved=4 * leaves * rows * width, limit=8,
    )


def solution(mesh):
    placed = (
        P(("clip", "row"), None),
        P(("clip", "row"), None, None, None),
        P(("clip", "row"), None),
        P(("clip", "row")),
        P(("clip", "row"), None, None),
        P(("clip", "row"), None, None),
        P(("clip", "row"), None, None),
        P(("clip", "row"), None),
        P(("clip", "row"), None, None, None),
        P(("clip", "row"), None),
        P(("clip", "row"), None, None, None),
    )
    return jax.shard_map(
        body, mesh=mesh, in_specs=placed, out_specs=P(("clip", "row"), None), check_vma=False
    )
```

```python
import jax
import jax.numpy as jnp
from jax import lax
from jax.experimental import pallas as pl
from jax.experimental.pallas import tpu as pltpu
from jax.sharding import PartitionSpec as P

GROUP = 16
CHUNK = 4
AHEAD = 8
MIB = 2**20

VMEM = pl.BlockSpec(memory_space=pltpu.VMEM)
SMEM = pl.BlockSpec(memory_space=pltpu.SMEM)
ANY = pl.BlockSpec(memory_space=pl.ANY)


def dot(a, b):
    return jnp.dot(a, b, preferred_element_type=jnp.float32)


def dot_t(a, b):
    return lax.dot_general(
        a, b, (((0,), (0,)), ((), ())), preferred_element_type=jnp.float32
    )


def rows_at(index, rows):
    return pl.ds(pl.multiple_of(index * rows, rows), rows)


def up_kernel(source_ref, col_ref, transfer_ref, share_ref, coef_ref, parent_ref):
    leaves, rows, rank = col_ref.shape
    total = None
    for leaf in range(leaves):
        panel = source_ref[pl.ds(leaf * rows, rows), :]
        share_ref[pl.ds(leaf * rows, rows), :] = panel
        coef = dot_t(col_ref[leaf], panel).astype(jnp.bfloat16)
        coef_ref[pl.ds(leaf * rank, rank), :] = coef
        share_ref[pl.ds(leaves * rows + leaf * rank, rank), :] = coef
        term = dot_t(transfer_ref[leaf], coef)
        total = term if total is None else total + term
    parent_ref[...] = total.astype(jnp.bfloat16)


def join_kernel(*refs):
    *pieces, out_ref = refs
    at = 0
    for ref in pieces:
        out_ref[pl.ds(at, ref.shape[0]), :] = ref[...]
        at += ref.shape[0]


def pick_kernel(level_ref, layer_ref, out_ref):
    corner = lax.axis_index("row") & 3
    level = (corner == 0) | (corner == 3)
    out_ref[...] = jnp.where(level, level_ref[...], layer_ref[...])


def hand_kernel(in_ref, *refs):
    out_ref = refs[-1]
    out_ref[...] = in_ref[pl.ds(0, out_ref.shape[0]), :]


def near_kernel(
    list_ref, count_ref, blocks_hbm, own_ref, share_ref, across_ref,
    near_ref,
    blocks, panels, block_sems, panel_sems,
):
    leaves, slots, rows, _ = blocks.shape
    chunks = slots // CHUNK
    size = leaves * rows
    place = lax.axis_index("row")

    copies = []
    for step in range(leaves * chunks):
        leaf, chunk = step // chunks, step % chunks
        where = pl.ds(chunk * CHUNK, CHUNK)
        copies.append(pltpu.make_async_copy(
            blocks_hbm.at[leaf, where], blocks.at[leaf, where], block_sems.at[leaf, chunk]
        ))
    pairs = [
        pltpu.make_async_copy(
            ref.at[pl.ds(0, size)], panels.at[pl.ds(which * size, size)], panel_sems.at[which]
        )
        for which, ref in enumerate((own_ref, share_ref, across_ref))
    ]
    for copy in pairs:
        copy.start()
    for copy in copies[:AHEAD]:
        copy.start()
    panels[pl.ds(3 * size, rows), :] = jnp.zeros((rows, panels.shape[1]), panels.dtype)
    for copy in pairs:
        copy.wait()

    def panel_of(leaf, slot):
        column = list_ref[leaf, slot]
        which = jnp.minimum(lax.div(column, leaves) ^ place, 2)
        index = which * leaves + (column & (leaves - 1))
        index = jnp.where(slot < count_ref[leaf], index, 3 * leaves)
        return panels[rows_at(index, rows), :]

    for leaf in range(leaves):
        total = None
        for slot in range(slots):
            if slot % CHUNK == 0:
                step = leaf * chunks + slot // CHUNK
                if step + AHEAD < len(copies):
                    copies[step + AHEAD].start()
                copies[step].wait()
            term = dot(blocks[leaf, slot], panel_of(leaf, slot))
            total = term if total is None else total + term
        near_ref[leaf] = total


def far_kernel(
    list_ref, coupling_ref, level_ref, layer_ref, share_ref, passed_ref,
    far_ref,
    coefs, sems,
):
    leaves, slots, rank, _ = coupling_ref.shape
    size = leaves * rank
    place = lax.axis_index("row")
    beyond = jnp.where((place & 2) == 0, place - 2, place + 2)
    copies = [
        pltpu.make_async_copy(
            ref.at[pl.ds(ref.shape[0] - size, size)], coefs.at[pl.ds(n * size, size)], sems.at[n]
        )
        for n, ref in enumerate((level_ref, layer_ref, share_ref, passed_ref))
    ]
    for copy in copies:
        copy.start()
    for copy in copies:
        copy.wait()

    def panel_of(leaf, slot):
        column = list_ref[leaf, slot]
        cluster = lax.div(column, leaves)
        which = jnp.where(
            cluster == (place ^ 2), 0,
            jnp.where(cluster == beyond, 1, jnp.where(cluster == (place ^ 1), 2, 3)),
        )
        return coefs[rows_at(which * leaves + column - cluster * leaves, rank), :]

    for leaf in range(leaves):
        total = None
        for slot in range(0, slots, 2):
            both = jnp.concatenate([coupling_ref[leaf, slot], coupling_ref[leaf, slot + 1]], axis=1)
            panels = jnp.concatenate([panel_of(leaf, slot), panel_of(leaf, slot + 1)], axis=0)
            term = dot(both, panels)
            total = term if total is None else total + term
        far_ref[pl.ds(leaf * rank, rank), :] = total


def down_kernel(
    list_ref, transfer_ref, coupling_ref, row_ref, near_ref, far_ref,
    column_ref, beside_ref, their_column_ref, their_beside_ref,
    out_ref,
):
    leaves, rows, rank = row_ref.shape
    local = lax.axis_index("row") & (GROUP - 1)
    total = None
    for slot in range(list_ref.shape[1]):
        flip = (list_ref[0, slot] & (GROUP - 1)) ^ local
        where = rows_at(flip >> 2, rank)
        mine = jnp.where((flip & 2) == 0, column_ref[where, :], beside_ref[where, :])
        theirs = jnp.where((flip & 2) == 0, their_column_ref[where, :], their_beside_ref[where, :])
        term = dot(coupling_ref[0, slot], jnp.where((flip & 1) == 0, mine, theirs))
        total = term if total is None else total + term
    high = total.astype(jnp.bfloat16)
    low = (total - high.astype(jnp.float32)).astype(jnp.bfloat16)
    coarse = jnp.concatenate([high, low], axis=0)
    for leaf in range(leaves):
        matrix = transfer_ref[leaf]
        spread = dot(jnp.concatenate([matrix, matrix], axis=1), coarse)
        down = (far_ref[pl.ds(leaf * rank, rank), :] + spread).astype(jnp.bfloat16)
        result = near_ref[leaf] + dot(row_ref[leaf], down)
        out_ref[pl.ds(leaf * rows, rows), :] = result.astype(jnp.bfloat16)


def call(kernel, name, outs, specs, args, scratch=(), flops=0, moved=0, limit=4):
    many = isinstance(outs, tuple)
    return pl.pallas_call(
        kernel,
        out_shape=outs,
        in_specs=specs,
        out_specs=(VMEM,) * len(outs) if many else VMEM,
        scratch_shapes=list(scratch),
        cost_estimate=pl.CostEstimate(flops=flops, bytes_accessed=moved, transcendentals=0),
        compiler_params=pltpu.CompilerParams(vmem_limit_bytes=limit * MIB),
        name=name,
    )(*args)


def body(
    source,
    near_blocks,
    near_list,
    near_count,
    col_basis,
    row_basis,
    transfer,
    far_list,
    far_coupling,
    coarse_list,
    coarse_coupling,
):
    leaves, slots, rows, _ = near_blocks.shape
    rank = col_basis.shape[2]
    width = source.shape[1]
    count = lax.axis_size("row")
    far_slots = far_coupling.shape[1]

    def send(value, target):
        pairs = [(d, target(d)) for d in range(count) if 0 <= target(d) < count]
        return lax.ppermute(value, "row", pairs)

    def panel(blocks, dtype=jnp.bfloat16):
        return jax.ShapeDtypeStruct((blocks * rank, width), dtype)

    share, coef, parent = call(
        up_kernel, "up",
        (jax.ShapeDtypeStruct((leaves * (rows + rank), width), jnp.bfloat16), panel(leaves), panel(1)),
        [VMEM] * 3, (source, col_basis, transfer),
        flops=2 * leaves * rank * width * (rows + rank),
        moved=2 * leaves * rows * (width + rank), limit=8,
    )
    layers = [send(parent, lambda d, bit=bit: d ^ bit) for bit in (4, 8, 12)]
    share_other = send(share, lambda d: d ^ 1)
    level = send(coef, lambda d: d ^ 2)
    panels = call(
        hand_kernel, "panels", jax.ShapeDtypeStruct(source.shape, jnp.bfloat16), [VMEM] + [ANY] * 1,
        (share, share_other),
    )
    across = send(panels, lambda d: d + 1 if d & 1 else d - 1)

    layer = send(level, lambda d: d - 4 if d & 2 else d + 4)
    column = call(join_kernel, "column", panel(GROUP // 4), [VMEM] * 4, (parent, *layers))
    beside = send(column, lambda d: d ^ 2)
    their_column = send(column, lambda d: d ^ 1)
    near = call(
        near_kernel, "near", jax.ShapeDtypeStruct((leaves, rows, width), jnp.float32),
        [SMEM, SMEM] + [ANY] * 4,
        (near_list, near_count, near_blocks, share, share_other, across),
        scratch=[
            pltpu.VMEM(near_blocks.shape, jnp.bfloat16),
            pltpu.VMEM(((3 * leaves + 1) * rows, width), jnp.bfloat16),
            pltpu.SemaphoreType.DMA((leaves, slots // CHUNK)),
            pltpu.SemaphoreType.DMA((3,)),
        ],
        limit=48,
    )
    picked_coef = call(
        pick_kernel, "pick", panel(leaves), [VMEM] * 2, (level, layer)
    )
    passed = send(picked_coef, lambda d: d ^ 1)
    far = call(
        far_kernel, "far", panel(leaves, jnp.float32), [SMEM, VMEM] + [ANY] * 4,
        (far_list, far_coupling, level, layer, share_other, passed),
        scratch=[
            pltpu.VMEM((4 * leaves * rank, width), jnp.bfloat16),
            pltpu.SemaphoreType.DMA((4,)),
        ],
        flops=2 * leaves * far_slots * rank * rank * width,
        moved=2 * leaves * far_slots * rank * rank, limit=10,
    )
    handed = call(hand_kernel, "hand", panel(GROUP // 4), [VMEM, ANY], (beside, near))
    their_beside = send(handed, lambda d: d ^ 1)
    return call(
        down_kernel, "down", jax.ShapeDtypeStruct(source.shape, jnp.bfloat16),
        [SMEM] + [VMEM] * 9,
        (
            coarse_list, transfer, coarse_coupling, row_basis, near, far,
            column, handed, their_column, their_beside,
        ),
        flops=8 * leaves * rank * rank * width,
        moved=4 * leaves * rows * width, limit=8,
    )


def solution(mesh):
    placed = (
        P(("clip", "row"), None),
        P(("clip", "row"), None, None, None),
        P(("clip", "row"), None),
        P(("clip", "row")),
        P(("clip", "row"), None, None),
        P(("clip", "row"), None, None),
        P(("clip", "row"), None, None),
        P(("clip", "row"), None),
        P(("clip", "row"), None, None, None),
        P(("clip", "row"), None),
        P(("clip", "row"), None, None, None),
    )
    return jax.shard_map(
        body, mesh=mesh, in_specs=placed, out_specs=P(("clip", "row"), None), check_vma=False
    )
```

```python
import jax
import jax.numpy as jnp
from jax import lax
from jax.experimental import pallas as pl
from jax.experimental.pallas import tpu as pltpu
from jax.sharding import PartitionSpec as P

GROUP = 16
CHUNK = 4
AHEAD = 4
MIB = 2**20

VMEM = pl.BlockSpec(memory_space=pltpu.VMEM)
SMEM = pl.BlockSpec(memory_space=pltpu.SMEM)
ANY = pl.BlockSpec(memory_space=pl.ANY)


def dot(a, b):
    return jnp.dot(a, b, preferred_element_type=jnp.float32)


def dot_t(a, b):
    return lax.dot_general(
        a, b, (((0,), (0,)), ((), ())), preferred_element_type=jnp.float32
    )


def rows_at(index, rows):
    return pl.ds(pl.multiple_of(index * rows, rows), rows)


def up_kernel(source_ref, col_ref, transfer_ref, share_ref, coef_ref, parent_ref):
    leaves, rows, rank = col_ref.shape
    total = None
    for leaf in range(leaves):
        panel = source_ref[pl.ds(leaf * rows, rows), :]
        share_ref[pl.ds(leaf * rows, rows), :] = panel
        coef = dot_t(col_ref[leaf], panel).astype(jnp.bfloat16)
        coef_ref[pl.ds(leaf * rank, rank), :] = coef
        share_ref[pl.ds(leaves * rows + leaf * rank, rank), :] = coef
        term = dot_t(transfer_ref[leaf], coef)
        total = term if total is None else total + term
    parent_ref[...] = total.astype(jnp.bfloat16)


def join_kernel(*refs):
    *pieces, out_ref = refs
    at = 0
    for ref in pieces:
        out_ref[pl.ds(at, ref.shape[0]), :] = ref[...]
        at += ref.shape[0]


def pick_kernel(level_ref, layer_ref, out_ref):
    corner = lax.axis_index("row") & 3
    level = (corner == 0) | (corner == 3)
    out_ref[...] = jnp.where(level, level_ref[...], layer_ref[...])


def hand_kernel(in_ref, *refs):
    out_ref = refs[-1]
    out_ref[...] = in_ref[pl.ds(0, out_ref.shape[0]), :]


def near_kernel(
    index_ref, blocks_hbm, own_ref, share_ref, across_ref,
    near_ref,
    blocks, panels, block_sems, panel_sems,
):
    leaves, slots, rows, _ = blocks.shape
    chunks = slots // CHUNK
    size = leaves * rows

    def live(step):
        return index_ref[step // chunks, step % chunks * CHUNK] < 3 * leaves

    def block_copy(step):
        leaf, chunk = step // chunks, step % chunks
        where = pl.ds(chunk * CHUNK, CHUNK)
        return pltpu.make_async_copy(
            blocks_hbm.at[leaf, where], blocks.at[leaf, where], block_sems.at[leaf, chunk]
        )

    def start(step):
        if step < leaves * chunks:
            @pl.when(live(step))
            def _():
                block_copy(step).start()

    pairs = [
        pltpu.make_async_copy(
            ref.at[pl.ds(0, size)], panels.at[pl.ds(which * size, size)], panel_sems.at[which]
        )
        for which, ref in enumerate((own_ref, share_ref, across_ref))
    ]
    for copy in pairs:
        copy.start()
    for step in range(AHEAD):
        start(step)
    panels[pl.ds(3 * size, rows), :] = jnp.zeros((rows, panels.shape[1]), panels.dtype)
    for copy in pairs:
        copy.wait()

    def term(leaf, slot):
        return dot(blocks[leaf, slot], panels[rows_at(index_ref[leaf, slot], rows), :])

    for step in range(leaves * chunks):
        leaf, first = step // chunks, step % chunks * CHUNK
        start(step + AHEAD)

        @pl.when(live(step))
        def _():
            block_copy(step).wait()
            even = term(leaf, first) + term(leaf, first + 2)
            odd = term(leaf, first + 1) + term(leaf, first + 3)
            total = even + odd
            near_ref[leaf] = total if first == 0 else near_ref[leaf] + total


def far_kernel(
    list_ref, coupling_ref, level_ref, layer_ref, share_ref, passed_ref,
    far_ref,
    coefs, sems,
):
    leaves, slots, rank, _ = coupling_ref.shape
    size = leaves * rank
    place = lax.axis_index("row")
    beyond = jnp.where((place & 2) == 0, place - 2, place + 2)
    copies = [
        pltpu.make_async_copy(
            ref.at[pl.ds(ref.shape[0] - size, size)], coefs.at[pl.ds(n * size, size)], sems.at[n]
        )
        for n, ref in enumerate((level_ref, layer_ref, share_ref, passed_ref))
    ]
    for copy in copies:
        copy.start()
    for copy in copies:
        copy.wait()

    def panel_of(leaf, slot):
        column = list_ref[leaf, slot]
        cluster = lax.div(column, leaves)
        which = jnp.where(
            cluster == (place ^ 2), 0,
            jnp.where(cluster == beyond, 1, jnp.where(cluster == (place ^ 1), 2, 3)),
        )
        return coefs[rows_at(which * leaves + column - cluster * leaves, rank), :]

    for leaf in range(leaves):
        total = None
        for slot in range(0, slots, 2):
            both = jnp.concatenate([coupling_ref[leaf, slot], coupling_ref[leaf, slot + 1]], axis=1)
            panels = jnp.concatenate([panel_of(leaf, slot), panel_of(leaf, slot + 1)], axis=0)
            term = dot(both, panels)
            total = term if total is None else total + term
        far_ref[pl.ds(leaf * rank, rank), :] = total


def down_kernel(
    list_ref, transfer_ref, coupling_ref, row_ref, near_ref, far_ref,
    column_ref, beside_ref, their_column_ref, their_beside_ref,
    out_ref,
):
    leaves, rows, rank = row_ref.shape
    local = lax.axis_index("row") & (GROUP - 1)
    total = None
    for slot in range(list_ref.shape[1]):
        flip = (list_ref[0, slot] & (GROUP - 1)) ^ local
        where = rows_at(flip >> 2, rank)
        mine = jnp.where((flip & 2) == 0, column_ref[where, :], beside_ref[where, :])
        theirs = jnp.where((flip & 2) == 0, their_column_ref[where, :], their_beside_ref[where, :])
        term = dot(coupling_ref[0, slot], jnp.where((flip & 1) == 0, mine, theirs))
        total = term if total is None else total + term
    high = total.astype(jnp.bfloat16)
    low = (total - high.astype(jnp.float32)).astype(jnp.bfloat16)
    coarse = jnp.concatenate([high, low], axis=0)
    for leaf in range(leaves):
        matrix = transfer_ref[leaf]
        spread = dot(jnp.concatenate([matrix, matrix], axis=1), coarse)
        down = (far_ref[pl.ds(leaf * rank, rank), :] + spread).astype(jnp.bfloat16)
        result = near_ref[leaf] + dot(row_ref[leaf], down)
        out_ref[pl.ds(leaf * rows, rows), :] = result.astype(jnp.bfloat16)


def call(kernel, name, outs, specs, args, scratch=(), flops=0, moved=0, limit=4):
    many = isinstance(outs, tuple)
    return pl.pallas_call(
        kernel,
        out_shape=outs,
        in_specs=specs,
        out_specs=(VMEM,) * len(outs) if many else VMEM,
        scratch_shapes=list(scratch),
        cost_estimate=pl.CostEstimate(flops=flops, bytes_accessed=moved, transcendentals=0),
        compiler_params=pltpu.CompilerParams(vmem_limit_bytes=limit * MIB),
        name=name,
    )(*args)


def body(
    source,
    near_blocks,
    near_list,
    near_count,
    col_basis,
    row_basis,
    transfer,
    far_list,
    far_coupling,
    coarse_list,
    coarse_coupling,
):
    leaves, slots, rows, _ = near_blocks.shape
    rank = col_basis.shape[2]
    width = source.shape[1]
    count = lax.axis_size("row")
    far_slots = far_coupling.shape[1]

    def send(value, target):
        pairs = [(d, target(d)) for d in range(count) if 0 <= target(d) < count]
        return lax.ppermute(value, "row", pairs)

    def panel(blocks, dtype=jnp.bfloat16):
        return jax.ShapeDtypeStruct((blocks * rank, width), dtype)

    share, coef, parent = call(
        up_kernel, "up",
        (jax.ShapeDtypeStruct((leaves * (rows + rank), width), jnp.bfloat16), panel(leaves), panel(1)),
        [VMEM] * 3, (source, col_basis, transfer),
        flops=2 * leaves * rank * width * (rows + rank),
        moved=2 * leaves * rows * (width + rank), limit=8,
    )
    layers = [send(parent, lambda d, bit=bit: d ^ bit) for bit in (4, 8, 12)]
    share_other = send(share, lambda d: d ^ 1)
    level = send(coef, lambda d: d ^ 2)
    panels = call(
        hand_kernel, "panels", jax.ShapeDtypeStruct(source.shape, jnp.bfloat16), [VMEM] + [ANY] * 1,
        (share, share_other),
    )
    across = send(panels, lambda d: d + 1 if d & 1 else d - 1)

    layer = send(level, lambda d: d - 4 if d & 2 else d + 4)
    column = call(join_kernel, "column", panel(GROUP // 4), [VMEM] * 4, (parent, *layers))
    beside = send(column, lambda d: d ^ 2)
    their_column = send(column, lambda d: d ^ 1)
    place = lax.axis_index("row")
    live = lax.broadcasted_iota(jnp.int32, (leaves, slots), 1) < near_count[:, None]
    which = jnp.minimum((near_list // leaves) ^ place, 2)
    index = jnp.where(live, which * leaves + near_list % leaves, 3 * leaves)
    near = call(
        near_kernel, "near", jax.ShapeDtypeStruct((leaves, rows, width), jnp.float32),
        [SMEM] + [ANY] * 4, (index, near_blocks, share, share_other, across),
        scratch=[
            pltpu.VMEM(near_blocks.shape, jnp.bfloat16),
            pltpu.VMEM(((3 * leaves + 1) * rows, width), jnp.bfloat16),
            pltpu.SemaphoreType.DMA((leaves, slots // CHUNK)),
            pltpu.SemaphoreType.DMA((3,)),
        ],
        flops=10**9, limit=48,
    )
    picked_coef = call(
        pick_kernel, "pick", panel(leaves), [VMEM] * 2, (level, layer)
    )
    passed = send(picked_coef, lambda d: d ^ 1)
    far = call(
        far_kernel, "far", panel(leaves, jnp.float32), [SMEM, VMEM] + [ANY] * 4,
        (far_list, far_coupling, level, layer, share_other, passed),
        scratch=[
            pltpu.VMEM((4 * leaves * rank, width), jnp.bfloat16),
            pltpu.SemaphoreType.DMA((4,)),
        ],
        flops=2 * leaves * far_slots * rank * rank * width,
        moved=2 * leaves * far_slots * rank * rank, limit=10,
    )
    handed = call(hand_kernel, "hand", panel(GROUP // 4), [VMEM, ANY], (beside, near))
    their_beside = send(handed, lambda d: d ^ 1)
    return call(
        down_kernel, "down", jax.ShapeDtypeStruct(source.shape, jnp.bfloat16),
        [SMEM] + [VMEM] * 9,
        (
            coarse_list, transfer, coarse_coupling, row_basis, near, far,
            column, handed, their_column, their_beside,
        ),
        flops=8 * leaves * rank * rank * width,
        moved=4 * leaves * rows * width, limit=8,
    )


def solution(mesh):
    placed = (
        P(("clip", "row"), None),
        P(("clip", "row"), None, None, None),
        P(("clip", "row"), None),
        P(("clip", "row")),
        P(("clip", "row"), None, None),
        P(("clip", "row"), None, None),
        P(("clip", "row"), None, None),
        P(("clip", "row"), None),
        P(("clip", "row"), None, None, None),
        P(("clip", "row"), None),
        P(("clip", "row"), None, None, None),
    )
    return jax.shard_map(
        body, mesh=mesh, in_specs=placed, out_specs=P(("clip", "row"), None), check_vma=False
    )
```

```python
import jax
import jax.numpy as jnp
from jax import lax
from jax.experimental import pallas as pl
from jax.experimental.pallas import tpu as pltpu
from jax.sharding import PartitionSpec as P

GROUP = 16
CHUNK = 4
MIB = 2**20

VMEM = pl.BlockSpec(memory_space=pltpu.VMEM)
SMEM = pl.BlockSpec(memory_space=pltpu.SMEM)
ANY = pl.BlockSpec(memory_space=pl.ANY)


def dot(a, b):
    return jnp.dot(a, b, preferred_element_type=jnp.float32)


def dot_t(a, b):
    return lax.dot_general(
        a, b, (((0,), (0,)), ((), ())), preferred_element_type=jnp.float32
    )


def rows_at(index, rows):
    return pl.ds(pl.multiple_of(index * rows, rows), rows)


def up_kernel(source_ref, col_ref, transfer_ref, share_ref, coef_ref, parent_ref):
    leaves, rows, rank = col_ref.shape
    total = None
    for leaf in range(leaves):
        panel = source_ref[pl.ds(leaf * rows, rows), :]
        share_ref[pl.ds(leaf * rows, rows), :] = panel
        coef = dot_t(col_ref[leaf], panel).astype(jnp.bfloat16)
        coef_ref[pl.ds(leaf * rank, rank), :] = coef
        share_ref[pl.ds(leaves * rows + leaf * rank, rank), :] = coef
        term = dot_t(transfer_ref[leaf], coef)
        total = term if total is None else total + term
    parent_ref[...] = total.astype(jnp.bfloat16)


def join_kernel(*refs):
    *pieces, _, out_ref = refs
    at = 0
    for ref in pieces:
        out_ref[pl.ds(at, ref.shape[0]), :] = ref[...]
        at += ref.shape[0]


def pick_kernel(level_ref, layer_ref, out_ref):
    corner = lax.axis_index("row") & 3
    level = (corner == 0) | (corner == 3)
    out_ref[...] = jnp.where(level, level_ref[...], layer_ref[...])


def hand_kernel(in_ref, *refs):
    out_ref = refs[-1]
    out_ref[...] = in_ref[pl.ds(0, out_ref.shape[0]), :]


def pick_slots(index_ref, blocks_hbm, blocks, sems, order_ref, low, high):
    leaves, slots, rows, _ = blocks.shape

    def picker(leaf):
        def step(slot, found):
            panel = index_ref[leaf, slot]
            kept = (panel >= low) & (panel < high)

            @pl.when(kept)
            def _():
                order_ref[leaf, found] = panel - low
                pltpu.make_async_copy(
                    blocks_hbm.at[leaf, slot], blocks.at[leaf, found], sems.at[leaf, found]
                ).start()

            return found + kept.astype(jnp.int32)

        return step

    found = [lax.fori_loop(0, slots, picker(leaf), 0) for leaf in range(leaves)]
    for leaf in range(leaves):
        for pad in range(CHUNK):
            order_ref[leaf, found[leaf] + pad] = high - low
    return found


def add_slots(total_ref, blocks_hbm, blocks, sems, order_ref, found, panels):
    leaves, slots, rows, _ = blocks.shape
    for leaf in range(leaves):
        count = found[leaf]

        def term(n):
            block = blocks[leaf, jnp.where(n < count, n, 0)]
            return dot(block, panels[rows_at(order_ref[leaf, n], rows), :])

        for first in range(0, slots, CHUNK):
            @pl.when(first < count)
            def _():
                for n in range(first, first + CHUNK):
                    @pl.when(n < count)
                    def _():
                        pltpu.make_async_copy(
                            blocks_hbm.at[leaf, 0], blocks.at[leaf, n], sems.at[leaf, n]
                        ).wait()
                even = term(first) + term(first + 2)
                odd = term(first + 1) + term(first + 3)
                total_ref[leaf] = total_ref[leaf] + (even + odd)


def near_kernel(
    index_ref, blocks_hbm, own_ref, share_ref,
    near_ref,
    blocks, panels, order, block_sems, panel_sems,
):
    leaves, _, rows, _ = blocks.shape
    size = leaves * rows
    pairs = [
        pltpu.make_async_copy(
            ref.at[pl.ds(0, size)], panels.at[pl.ds(which * size, size)], panel_sems.at[which]
        )
        for which, ref in enumerate((own_ref, share_ref))
    ]
    for copy in pairs:
        copy.start()
    found = pick_slots(index_ref, blocks_hbm, blocks, block_sems, order, 0, 2 * leaves)
    near_ref[...] = jnp.zeros(near_ref.shape, near_ref.dtype)
    panels[pl.ds(2 * size, rows), :] = jnp.zeros((rows, panels.shape[1]), panels.dtype)
    for copy in pairs:
        copy.wait()
    add_slots(near_ref, blocks_hbm, blocks, block_sems, order, found, panels)


def across_kernel(
    index_ref, blocks_hbm, near_ref, across_ref,
    total_ref,
    blocks, panels, order, block_sems, panel_sems,
):
    leaves, _, rows, _ = blocks.shape
    size = leaves * rows
    copy = pltpu.make_async_copy(across_ref, panels.at[pl.ds(0, size)], panel_sems.at[0])
    copy.start()
    found = pick_slots(
        index_ref, blocks_hbm, blocks, block_sems, order, 2 * leaves, 3 * leaves
    )
    total_ref[...] = near_ref[...]
    panels[pl.ds(size, rows), :] = jnp.zeros((rows, panels.shape[1]), panels.dtype)
    copy.wait()
    add_slots(total_ref, blocks_hbm, blocks, block_sems, order, found, panels)


def far_kernel(
    list_ref, coupling_ref, level_ref, layer_ref, share_ref, passed_ref,
    far_ref,
    coefs, sems,
):
    leaves, slots, rank, _ = coupling_ref.shape
    size = leaves * rank
    place = lax.axis_index("row")
    beyond = jnp.where((place & 2) == 0, place - 2, place + 2)
    copies = [
        pltpu.make_async_copy(
            ref.at[pl.ds(ref.shape[0] - size, size)], coefs.at[pl.ds(n * size, size)], sems.at[n]
        )
        for n, ref in enumerate((level_ref, layer_ref, share_ref, passed_ref))
    ]
    for copy in copies:
        copy.start()
    for copy in copies:
        copy.wait()

    def panel_of(leaf, slot):
        column = list_ref[leaf, slot]
        cluster = lax.div(column, leaves)
        which = jnp.where(
            cluster == (place ^ 2), 0,
            jnp.where(cluster == beyond, 1, jnp.where(cluster == (place ^ 1), 2, 3)),
        )
        return coefs[rows_at(which * leaves + column - cluster * leaves, rank), :]

    for leaf in range(leaves):
        total = None
        for slot in range(0, slots, 2):
            both = jnp.concatenate([coupling_ref[leaf, slot], coupling_ref[leaf, slot + 1]], axis=1)
            panels = jnp.concatenate([panel_of(leaf, slot), panel_of(leaf, slot + 1)], axis=0)
            term = dot(both, panels)
            total = term if total is None else total + term
        far_ref[pl.ds(leaf * rank, rank), :] = total


def down_kernel(
    list_ref, transfer_ref, coupling_ref, row_ref, near_ref, far_ref,
    column_ref, beside_ref, their_column_ref, their_beside_ref,
    out_ref,
):
    leaves, rows, rank = row_ref.shape
    local = lax.axis_index("row") & (GROUP - 1)
    total = None
    for slot in range(list_ref.shape[1]):
        flip = (list_ref[0, slot] & (GROUP - 1)) ^ local
        where = rows_at(flip >> 2, rank)
        mine = jnp.where((flip & 2) == 0, column_ref[where, :], beside_ref[where, :])
        theirs = jnp.where((flip & 2) == 0, their_column_ref[where, :], their_beside_ref[where, :])
        term = dot(coupling_ref[0, slot], jnp.where((flip & 1) == 0, mine, theirs))
        total = term if total is None else total + term
    high = total.astype(jnp.bfloat16)
    low = (total - high.astype(jnp.float32)).astype(jnp.bfloat16)
    coarse = jnp.concatenate([high, low], axis=0)
    for leaf in range(leaves):
        matrix = transfer_ref[leaf]
        spread = dot(jnp.concatenate([matrix, matrix], axis=1), coarse)
        down = (far_ref[pl.ds(leaf * rank, rank), :] + spread).astype(jnp.bfloat16)
        result = near_ref[leaf] + dot(row_ref[leaf], down)
        out_ref[pl.ds(leaf * rows, rows), :] = result.astype(jnp.bfloat16)


def call(kernel, name, outs, specs, args, scratch=(), flops=0, moved=0, limit=4):
    many = isinstance(outs, tuple)
    return pl.pallas_call(
        kernel,
        out_shape=outs,
        in_specs=specs,
        out_specs=(VMEM,) * len(outs) if many else VMEM,
        scratch_shapes=list(scratch),
        cost_estimate=pl.CostEstimate(flops=flops, bytes_accessed=moved, transcendentals=0),
        compiler_params=pltpu.CompilerParams(vmem_limit_bytes=limit * MIB),
        name=name,
    )(*args)


def body(
    source,
    near_blocks,
    near_list,
    near_count,
    col_basis,
    row_basis,
    transfer,
    far_list,
    far_coupling,
    coarse_list,
    coarse_coupling,
):
    leaves, slots, rows, _ = near_blocks.shape
    rank = col_basis.shape[2]
    width = source.shape[1]
    count = lax.axis_size("row")
    far_slots = far_coupling.shape[1]

    def send(value, target):
        pairs = [(d, target(d)) for d in range(count) if 0 <= target(d) < count]
        return lax.ppermute(value, "row", pairs)

    def panel(blocks, dtype=jnp.bfloat16):
        return jax.ShapeDtypeStruct((blocks * rank, width), dtype)

    share, coef, parent = call(
        up_kernel, "up",
        (jax.ShapeDtypeStruct((leaves * (rows + rank), width), jnp.bfloat16), panel(leaves), panel(1)),
        [VMEM] * 3, (source, col_basis, transfer),
        flops=2 * leaves * rank * width * (rows + rank),
        moved=2 * leaves * rows * (width + rank), limit=8,
    )
    layers = [send(parent, lambda d, bit=bit: d ^ bit) for bit in (4, 8, 12)]
    share_other = send(share, lambda d: d ^ 1)
    level = send(coef, lambda d: d ^ 2)
    panels = call(
        hand_kernel, "panels", jax.ShapeDtypeStruct(source.shape, jnp.bfloat16), [VMEM] + [ANY] * 1,
        (share, share_other),
    )
    across = send(panels, lambda d: d + 1 if d & 1 else d - 1)

    place = lax.axis_index("row")
    live = lax.broadcasted_iota(jnp.int32, (leaves, slots), 1) < near_count[:, None]
    which = jnp.minimum((near_list // leaves) ^ place, 2)
    index = jnp.where(live, which * leaves + near_list % leaves, 3 * leaves)
    def slots_scratch(panels):
        return [
            pltpu.VMEM(near_blocks.shape, jnp.bfloat16),
            pltpu.VMEM((panels * rows, width), jnp.bfloat16),
            pltpu.SMEM((leaves, slots + CHUNK), jnp.int32),
            pltpu.SemaphoreType.DMA((leaves, slots)),
            pltpu.SemaphoreType.DMA((2,)),
        ]

    shape = jax.ShapeDtypeStruct((leaves, rows, width), jnp.float32)
    near = call(
        near_kernel, "near", shape, [SMEM] + [ANY] * 3,
        (index, near_blocks, share, share_other),
        scratch=slots_scratch(2 * leaves + 1), flops=10**9, limit=48,
    )
    layer = send(level, lambda d: d - 4 if d & 2 else d + 4)
    column = call(join_kernel, "column", panel(GROUP // 4), [VMEM] * 4 + [ANY],
        (parent, *layers, near))
    beside = send(column, lambda d: d ^ 2)
    their_column = send(column, lambda d: d ^ 1)
    near = call(
        across_kernel, "across", shape, [SMEM, ANY, VMEM, ANY],
        (index, near_blocks, near, across),
        scratch=slots_scratch(leaves + 1), flops=10**9, limit=48,
    )
    picked_coef = call(
        pick_kernel, "pick", panel(leaves), [VMEM] * 2, (level, layer)
    )
    passed = send(picked_coef, lambda d: d ^ 1)
    far = call(
        far_kernel, "far", panel(leaves, jnp.float32), [SMEM, VMEM] + [ANY] * 4,
        (far_list, far_coupling, level, layer, share_other, passed),
        scratch=[
            pltpu.VMEM((4 * leaves * rank, width), jnp.bfloat16),
            pltpu.SemaphoreType.DMA((4,)),
        ],
        flops=2 * leaves * far_slots * rank * rank * width,
        moved=2 * leaves * far_slots * rank * rank, limit=10,
    )
    handed = call(hand_kernel, "hand", panel(GROUP // 4), [VMEM, ANY], (beside, near))
    their_beside = send(handed, lambda d: d ^ 1)
    return call(
        down_kernel, "down", jax.ShapeDtypeStruct(source.shape, jnp.bfloat16),
        [SMEM] + [VMEM] * 9,
        (
            coarse_list, transfer, coarse_coupling, row_basis, near, far,
            column, handed, their_column, their_beside,
        ),
        flops=8 * leaves * rank * rank * width,
        moved=4 * leaves * rows * width, limit=8,
    )


def solution(mesh):
    placed = (
        P(("clip", "row"), None),
        P(("clip", "row"), None, None, None),
        P(("clip", "row"), None),
        P(("clip", "row")),
        P(("clip", "row"), None, None),
        P(("clip", "row"), None, None),
        P(("clip", "row"), None, None),
        P(("clip", "row"), None),
        P(("clip", "row"), None, None, None),
        P(("clip", "row"), None),
        P(("clip", "row"), None, None, None),
    )
    return jax.shard_map(
        body, mesh=mesh, in_specs=placed, out_specs=P(("clip", "row"), None), check_vma=False
    )
```

```python
import jax
import jax.numpy as jnp
from jax import lax
from jax.experimental import pallas as pl
from jax.experimental.pallas import tpu as pltpu
from jax.sharding import PartitionSpec as P

GROUP = 16
CHUNK = 4
MIB = 2**20

VMEM = pl.BlockSpec(memory_space=pltpu.VMEM)
SMEM = pl.BlockSpec(memory_space=pltpu.SMEM)
ANY = pl.BlockSpec(memory_space=pl.ANY)


def dot(a, b):
    return jnp.dot(a, b, preferred_element_type=jnp.float32)


def dot_t(a, b):
    return lax.dot_general(
        a, b, (((0,), (0,)), ((), ())), preferred_element_type=jnp.float32
    )


def rows_at(index, rows):
    return pl.ds(pl.multiple_of(index * rows, rows), rows)


def coef_kernel(source_ref, col_ref, share_ref, coef_ref):
    leaves, rows, rank = col_ref.shape
    for leaf in range(leaves):
        panel = source_ref[pl.ds(leaf * rows, rows), :]
        share_ref[pl.ds(leaf * rows, rows), :] = panel
        coef = dot_t(col_ref[leaf], panel).astype(jnp.bfloat16)
        coef_ref[pl.ds(leaf * rank, rank), :] = coef
        share_ref[pl.ds(leaves * rows + leaf * rank, rank), :] = coef


def parent_kernel(coef_ref, transfer_ref, parent_ref):
    leaves, rank, _ = transfer_ref.shape
    total = None
    for leaf in range(leaves):
        term = dot_t(transfer_ref[leaf], coef_ref[pl.ds(leaf * rank, rank), :])
        total = term if total is None else total + term
    parent_ref[...] = total.astype(jnp.bfloat16)


def join_kernel(*refs):
    *pieces, _, out_ref = refs
    at = 0
    for ref in pieces:
        out_ref[pl.ds(at, ref.shape[0]), :] = ref[...]
        at += ref.shape[0]


def pick_kernel(level_ref, layer_ref, out_ref):
    corner = lax.axis_index("row") & 3
    level = (corner == 0) | (corner == 3)
    out_ref[...] = jnp.where(level, level_ref[...], layer_ref[...])


def hand_kernel(in_ref, *refs):
    out_ref = refs[-1]
    out_ref[...] = in_ref[pl.ds(0, out_ref.shape[0]), :]


def pick_slots(index_ref, blocks_hbm, blocks, sems, order_ref, low, high):
    leaves, slots, rows, _ = blocks.shape

    def picker(leaf):
        def step(slot, found):
            panel = index_ref[leaf, slot]
            kept = (panel >= low) & (panel < high)

            @pl.when(kept)
            def _():
                order_ref[leaf, found] = panel - low
                pltpu.make_async_copy(
                    blocks_hbm.at[leaf, slot], blocks.at[leaf, found], sems.at[leaf, found]
                ).start()

            return found + kept.astype(jnp.int32)

        return step

    found = [lax.fori_loop(0, slots, picker(leaf), 0) for leaf in range(leaves)]
    for leaf in range(leaves):
        for pad in range(CHUNK):
            order_ref[leaf, found[leaf] + pad] = high - low
    return found


def add_slots(total_ref, blocks_hbm, blocks, sems, order_ref, found, panels):
    leaves, slots, rows, _ = blocks.shape
    for leaf in range(leaves):
        count = found[leaf]

        def term(n):
            block = blocks[leaf, jnp.where(n < count, n, 0)]
            return dot(block, panels[rows_at(order_ref[leaf, n], rows), :])

        for first in range(0, slots, CHUNK):
            @pl.when(first < count)
            def _():
                for n in range(first, first + CHUNK):
                    @pl.when(n < count)
                    def _():
                        pltpu.make_async_copy(
                            blocks_hbm.at[leaf, 0], blocks.at[leaf, n], sems.at[leaf, n]
                        ).wait()
                even = term(first) + term(first + 2)
                odd = term(first + 1) + term(first + 3)
                total_ref[leaf] = total_ref[leaf] + (even + odd)


def near_kernel(
    index_ref, blocks_hbm, own_ref, share_ref,
    near_ref,
    blocks, panels, order, block_sems, panel_sems,
):
    leaves, _, rows, _ = blocks.shape
    size = leaves * rows
    pairs = [
        pltpu.make_async_copy(
            ref.at[pl.ds(0, size)], panels.at[pl.ds(which * size, size)], panel_sems.at[which]
        )
        for which, ref in enumerate((own_ref, share_ref))
    ]
    for copy in pairs:
        copy.start()
    found = pick_slots(index_ref, blocks_hbm, blocks, block_sems, order, 0, 2 * leaves)
    near_ref[...] = jnp.zeros(near_ref.shape, near_ref.dtype)
    panels[pl.ds(2 * size, rows), :] = jnp.zeros((rows, panels.shape[1]), panels.dtype)
    for copy in pairs:
        copy.wait()
    add_slots(near_ref, blocks_hbm, blocks, block_sems, order, found, panels)


def across_kernel(
    index_ref, blocks_hbm, near_ref, across_ref,
    total_ref,
    blocks, panels, order, block_sems, panel_sems,
):
    leaves, _, rows, _ = blocks.shape
    size = leaves * rows
    copy = pltpu.make_async_copy(across_ref, panels.at[pl.ds(0, size)], panel_sems.at[0])
    copy.start()
    found = pick_slots(
        index_ref, blocks_hbm, blocks, block_sems, order, 2 * leaves, 3 * leaves
    )
    total_ref[...] = near_ref[...]
    panels[pl.ds(size, rows), :] = jnp.zeros((rows, panels.shape[1]), panels.dtype)
    copy.wait()
    add_slots(total_ref, blocks_hbm, blocks, block_sems, order, found, panels)


def far_kernel(
    list_ref, coupling_ref, level_ref, layer_ref, share_ref, passed_ref,
    far_ref,
    coefs, sems,
):
    leaves, slots, rank, _ = coupling_ref.shape
    size = leaves * rank
    place = lax.axis_index("row")
    beyond = jnp.where((place & 2) == 0, place - 2, place + 2)
    copies = [
        pltpu.make_async_copy(
            ref.at[pl.ds(ref.shape[0] - size, size)], coefs.at[pl.ds(n * size, size)], sems.at[n]
        )
        for n, ref in enumerate((level_ref, layer_ref, share_ref, passed_ref))
    ]
    for copy in copies:
        copy.start()
    for copy in copies:
        copy.wait()

    def panel_of(leaf, slot):
        column = list_ref[leaf, slot]
        cluster = lax.div(column, leaves)
        which = jnp.where(
            cluster == (place ^ 2), 0,
            jnp.where(cluster == beyond, 1, jnp.where(cluster == (place ^ 1), 2, 3)),
        )
        return coefs[rows_at(which * leaves + column - cluster * leaves, rank), :]

    for leaf in range(leaves):
        total = None
        for slot in range(0, slots, 2):
            both = jnp.concatenate([coupling_ref[leaf, slot], coupling_ref[leaf, slot + 1]], axis=1)
            panels = jnp.concatenate([panel_of(leaf, slot), panel_of(leaf, slot + 1)], axis=0)
            term = dot(both, panels)
            total = term if total is None else total + term
        far_ref[pl.ds(leaf * rank, rank), :] = total


def down_kernel(
    list_ref, transfer_ref, coupling_ref, row_ref, near_ref, far_ref,
    column_ref, beside_ref, their_column_ref, their_beside_ref,
    out_ref,
):
    leaves, rows, rank = row_ref.shape
    local = lax.axis_index("row") & (GROUP - 1)

    def panel_of(slot):
        flip = (list_ref[0, slot] & (GROUP - 1)) ^ local
        where = rows_at(flip >> 2, rank)
        mine = jnp.where((flip & 2) == 0, column_ref[where, :], beside_ref[where, :])
        theirs = jnp.where((flip & 2) == 0, their_column_ref[where, :], their_beside_ref[where, :])
        return jnp.where((flip & 1) == 0, mine, theirs)

    terms = []
    for slot in range(0, list_ref.shape[1], 2):
        both = jnp.concatenate([coupling_ref[0, slot], coupling_ref[0, slot + 1]], axis=1)
        terms.append(dot(both, jnp.concatenate([panel_of(slot), panel_of(slot + 1)], axis=0)))
    while len(terms) > 1:
        terms = [first + second for first, second in zip(terms[::2], terms[1::2])]
    high = terms[0].astype(jnp.bfloat16)
    low = (terms[0] - high.astype(jnp.float32)).astype(jnp.bfloat16)
    matrix = transfer_ref[...].reshape(leaves * rank, rank)
    spread = dot(
        jnp.concatenate([matrix, matrix], axis=1), jnp.concatenate([high, low], axis=0)
    )
    down = (far_ref[...] + spread).astype(jnp.bfloat16)
    for leaf in range(leaves):
        result = near_ref[leaf] + dot(row_ref[leaf], down[leaf * rank:(leaf + 1) * rank])
        out_ref[pl.ds(leaf * rows, rows), :] = result.astype(jnp.bfloat16)


def call(kernel, name, outs, specs, args, scratch=(), flops=0, moved=0, limit=4):
    many = isinstance(outs, tuple)
    return pl.pallas_call(
        kernel,
        out_shape=outs,
        in_specs=specs,
        out_specs=(VMEM,) * len(outs) if many else VMEM,
        scratch_shapes=list(scratch),
        cost_estimate=pl.CostEstimate(flops=flops, bytes_accessed=moved, transcendentals=0),
        compiler_params=pltpu.CompilerParams(vmem_limit_bytes=limit * MIB),
        name=name,
    )(*args)


def body(
    source,
    near_blocks,
    near_list,
    near_count,
    col_basis,
    row_basis,
    transfer,
    far_list,
    far_coupling,
    coarse_list,
    coarse_coupling,
):
    leaves, slots, rows, _ = near_blocks.shape
    rank = col_basis.shape[2]
    width = source.shape[1]
    count = lax.axis_size("row")
    far_slots = far_coupling.shape[1]

    def send(value, target):
        pairs = [(d, target(d)) for d in range(count) if 0 <= target(d) < count]
        return lax.ppermute(value, "row", pairs)

    def panel(blocks, dtype=jnp.bfloat16):
        return jax.ShapeDtypeStruct((blocks * rank, width), dtype)

    share, coef = call(
        coef_kernel, "coef",
        (jax.ShapeDtypeStruct((leaves * (rows + rank), width), jnp.bfloat16), panel(leaves)),
        [VMEM] * 2, (source, col_basis), flops=2 * leaves * rank * width * rows,
        moved=2 * leaves * rows * (width + rank), limit=8,
    )
    parent = call(parent_kernel, "parent", panel(1), [VMEM] * 2, (coef, transfer))
    layers = [send(parent, lambda d, bit=bit: d ^ bit) for bit in (4, 8, 12)]
    share_other = send(share, lambda d: d ^ 1)
    level = send(coef, lambda d: d ^ 2)
    panels = call(
        hand_kernel, "panels", jax.ShapeDtypeStruct(source.shape, jnp.bfloat16), [VMEM] + [ANY] * 1,
        (share, share_other),
    )
    across = send(panels, lambda d: d + 1 if d & 1 else d - 1)

    place = lax.axis_index("row")
    live = lax.broadcasted_iota(jnp.int32, (leaves, slots), 1) < near_count[:, None]
    which = jnp.minimum((near_list // leaves) ^ place, 2)
    index = jnp.where(live, which * leaves + near_list % leaves, 3 * leaves)
    def slots_scratch(panels):
        return [
            pltpu.VMEM(near_blocks.shape, jnp.bfloat16),
            pltpu.VMEM((panels * rows, width), jnp.bfloat16),
            pltpu.SMEM((leaves, slots + CHUNK), jnp.int32),
            pltpu.SemaphoreType.DMA((leaves, slots)),
            pltpu.SemaphoreType.DMA((2,)),
        ]

    shape = jax.ShapeDtypeStruct((leaves, rows, width), jnp.float32)
    near = call(
        near_kernel, "near", shape, [SMEM] + [ANY] * 3,
        (index, near_blocks, share, share_other),
        scratch=slots_scratch(2 * leaves + 1), flops=10**9, limit=48,
    )
    layer = send(level, lambda d: d - 4 if d & 2 else d + 4)
    column = call(join_kernel, "column", panel(GROUP // 4), [VMEM] * 4 + [ANY],
        (parent, *layers, near))
    beside = send(column, lambda d: d ^ 2)
    their_column = send(column, lambda d: d ^ 1)
    near = call(
        across_kernel, "across", shape, [SMEM, ANY, VMEM, ANY],
        (index, near_blocks, near, across),
        scratch=slots_scratch(leaves + 1), flops=10**9, limit=48,
    )
    picked_coef = call(
        pick_kernel, "pick", panel(leaves), [VMEM] * 2, (level, layer)
    )
    passed = send(picked_coef, lambda d: d ^ 1)
    far = call(
        far_kernel, "far", panel(leaves, jnp.float32), [SMEM, VMEM] + [ANY] * 4,
        (far_list, far_coupling, level, layer, share_other, passed),
        scratch=[
            pltpu.VMEM((4 * leaves * rank, width), jnp.bfloat16),
            pltpu.SemaphoreType.DMA((4,)),
        ],
        flops=2 * leaves * far_slots * rank * rank * width,
        moved=2 * leaves * far_slots * rank * rank, limit=10,
    )
    handed = call(hand_kernel, "hand", panel(GROUP // 4), [VMEM, ANY], (beside, near))
    their_beside = send(handed, lambda d: d ^ 1)
    return call(
        down_kernel, "down", jax.ShapeDtypeStruct(source.shape, jnp.bfloat16),
        [SMEM] + [VMEM] * 9,
        (
            coarse_list, transfer, coarse_coupling, row_basis, near, far,
            column, handed, their_column, their_beside,
        ),
        flops=8 * leaves * rank * rank * width,
        moved=4 * leaves * rows * width, limit=8,
    )


def solution(mesh):
    placed = (
        P(("clip", "row"), None),
        P(("clip", "row"), None, None, None),
        P(("clip", "row"), None),
        P(("clip", "row")),
        P(("clip", "row"), None, None),
        P(("clip", "row"), None, None),
        P(("clip", "row"), None, None),
        P(("clip", "row"), None),
        P(("clip", "row"), None, None, None),
        P(("clip", "row"), None),
        P(("clip", "row"), None, None, None),
    )
    return jax.shard_map(
        body, mesh=mesh, in_specs=placed, out_specs=P(("clip", "row"), None), check_vma=False
    )
```

```python
import jax
import jax.numpy as jnp
from jax import lax
from jax.experimental import pallas as pl
from jax.experimental.pallas import tpu as pltpu
from jax.sharding import PartitionSpec as P

GROUP = 16
CHUNK = 4
MIB = 2**20

VMEM = pl.BlockSpec(memory_space=pltpu.VMEM)
SMEM = pl.BlockSpec(memory_space=pltpu.SMEM)
ANY = pl.BlockSpec(memory_space=pl.ANY)


def dot(a, b):
    return jnp.dot(a, b, preferred_element_type=jnp.float32)


def dot_t(a, b):
    return lax.dot_general(
        a, b, (((0,), (0,)), ((), ())), preferred_element_type=jnp.float32
    )


def rows_at(index, rows):
    return pl.ds(pl.multiple_of(index * rows, rows), rows)


def coef_kernel(source_ref, col_ref, share_ref, coef_ref):
    leaves, rows, rank = col_ref.shape
    for leaf in range(leaves):
        panel = source_ref[pl.ds(leaf * rows, rows), :]
        share_ref[pl.ds(leaf * rows, rows), :] = panel
        coef = dot_t(col_ref[leaf], panel).astype(jnp.bfloat16)
        coef_ref[pl.ds(leaf * rank, rank), :] = coef
        share_ref[pl.ds(leaves * rows + leaf * rank, rank), :] = coef


def parent_kernel(coef_ref, transfer_ref, parent_ref):
    leaves, rank, _ = transfer_ref.shape
    total = None
    for leaf in range(leaves):
        term = dot_t(transfer_ref[leaf], coef_ref[pl.ds(leaf * rank, rank), :])
        total = term if total is None else total + term
    parent_ref[...] = total.astype(jnp.bfloat16)


def join_kernel(*refs):
    *pieces, out_ref = refs
    at = 0
    for ref in pieces:
        out_ref[pl.ds(at, ref.shape[0]), :] = ref[...]
        at += ref.shape[0]


def pick_kernel(level_ref, layer_ref, _, out_ref):
    corner = lax.axis_index("row") & 3
    level = (corner == 0) | (corner == 3)
    out_ref[...] = jnp.where(level, level_ref[...], layer_ref[...])


def hand_kernel(in_ref, *refs):
    out_ref = refs[-1]
    out_ref[...] = in_ref[pl.ds(0, out_ref.shape[0]), :]


def pick_slots(index_ref, blocks_hbm, blocks, sems, order_ref, low, high):
    leaves, slots, rows, _ = blocks.shape

    def picker(leaf):
        def step(slot, found):
            panel = index_ref[leaf, slot]
            kept = (panel >= low) & (panel < high)

            @pl.when(kept)
            def _():
                order_ref[leaf, found] = panel - low
                pltpu.make_async_copy(
                    blocks_hbm.at[leaf, slot], blocks.at[leaf, found], sems.at[leaf, found]
                ).start()

            return found + kept.astype(jnp.int32)

        return step

    found = [lax.fori_loop(0, slots, picker(leaf), 0) for leaf in range(leaves)]
    for leaf in range(leaves):
        for pad in range(CHUNK):
            order_ref[leaf, found[leaf] + pad] = high - low
    return found


def add_slots(total_ref, blocks_hbm, blocks, sems, order_ref, found, panels):
    leaves, slots, rows, _ = blocks.shape
    for leaf in range(leaves):
        count = found[leaf]

        def term(n):
            block = blocks[leaf, jnp.where(n < count, n, 0)]
            return dot(block, panels[rows_at(order_ref[leaf, n], rows), :])

        for first in range(0, slots, CHUNK):
            @pl.when(first < count)
            def _():
                for n in range(first, first + CHUNK):
                    @pl.when(n < count)
                    def _():
                        pltpu.make_async_copy(
                            blocks_hbm.at[leaf, 0], blocks.at[leaf, n], sems.at[leaf, n]
                        ).wait()
                even = term(first) + term(first + 2)
                odd = term(first + 1) + term(first + 3)
                total_ref[leaf] = total_ref[leaf] + (even + odd)


def near_kernel(
    index_ref, blocks_hbm, own_ref, share_ref, _,
    near_ref,
    blocks, panels, order, block_sems, panel_sems,
):
    leaves, _, rows, _ = blocks.shape
    size = leaves * rows
    pairs = [
        pltpu.make_async_copy(
            ref.at[pl.ds(0, size)], panels.at[pl.ds(which * size, size)], panel_sems.at[which]
        )
        for which, ref in enumerate((own_ref, share_ref))
    ]
    for copy in pairs:
        copy.start()
    found = pick_slots(index_ref, blocks_hbm, blocks, block_sems, order, 0, 2 * leaves)
    near_ref[...] = jnp.zeros(near_ref.shape, near_ref.dtype)
    panels[pl.ds(2 * size, rows), :] = jnp.zeros((rows, panels.shape[1]), panels.dtype)
    for copy in pairs:
        copy.wait()
    add_slots(near_ref, blocks_hbm, blocks, block_sems, order, found, panels)


def across_kernel(
    index_ref, blocks_hbm, near_ref, across_ref,
    total_ref,
    blocks, panels, order, block_sems, panel_sems,
):
    leaves, _, rows, _ = blocks.shape
    size = leaves * rows
    copy = pltpu.make_async_copy(across_ref, panels.at[pl.ds(0, size)], panel_sems.at[0])
    copy.start()
    found = pick_slots(
        index_ref, blocks_hbm, blocks, block_sems, order, 2 * leaves, 3 * leaves
    )
    total_ref[...] = near_ref[...]
    panels[pl.ds(size, rows), :] = jnp.zeros((rows, panels.shape[1]), panels.dtype)
    copy.wait()
    add_slots(total_ref, blocks_hbm, blocks, block_sems, order, found, panels)


def far_kernel(
    list_ref, coupling_ref, level_ref, layer_ref, share_ref, passed_ref,
    far_ref,
    coefs, sems,
):
    leaves, slots, rank, _ = coupling_ref.shape
    size = leaves * rank
    place = lax.axis_index("row")
    beyond = jnp.where((place & 2) == 0, place - 2, place + 2)
    copies = [
        pltpu.make_async_copy(
            ref.at[pl.ds(ref.shape[0] - size, size)], coefs.at[pl.ds(n * size, size)], sems.at[n]
        )
        for n, ref in enumerate((level_ref, layer_ref, share_ref, passed_ref))
    ]
    for copy in copies:
        copy.start()
    for copy in copies:
        copy.wait()

    def panel_of(leaf, slot):
        column = list_ref[leaf, slot]
        cluster = lax.div(column, leaves)
        which = jnp.where(
            cluster == (place ^ 2), 0,
            jnp.where(cluster == beyond, 1, jnp.where(cluster == (place ^ 1), 2, 3)),
        )
        return coefs[rows_at(which * leaves + column - cluster * leaves, rank), :]

    for leaf in range(leaves):
        total = None
        for slot in range(0, slots, 2):
            both = jnp.concatenate([coupling_ref[leaf, slot], coupling_ref[leaf, slot + 1]], axis=1)
            panels = jnp.concatenate([panel_of(leaf, slot), panel_of(leaf, slot + 1)], axis=0)
            term = dot(both, panels)
            total = term if total is None else total + term
        far_ref[pl.ds(leaf * rank, rank), :] = total


def down_kernel(
    list_ref, transfer_ref, coupling_ref, row_ref, near_ref, far_ref,
    column_ref, beside_ref, their_column_ref, their_beside_ref,
    out_ref,
):
    leaves, rows, rank = row_ref.shape
    local = lax.axis_index("row") & (GROUP - 1)

    def panel_of(slot):
        flip = (list_ref[0, slot] & (GROUP - 1)) ^ local
        where = rows_at(flip >> 2, rank)
        mine = jnp.where((flip & 2) == 0, column_ref[where, :], beside_ref[where, :])
        theirs = jnp.where((flip & 2) == 0, their_column_ref[where, :], their_beside_ref[where, :])
        return jnp.where((flip & 1) == 0, mine, theirs)

    terms = []
    for slot in range(0, list_ref.shape[1], 2):
        both = jnp.concatenate([coupling_ref[0, slot], coupling_ref[0, slot + 1]], axis=1)
        terms.append(dot(both, jnp.concatenate([panel_of(slot), panel_of(slot + 1)], axis=0)))
    while len(terms) > 1:
        terms = [first + second for first, second in zip(terms[::2], terms[1::2])]
    high = terms[0].astype(jnp.bfloat16)
    low = (terms[0] - high.astype(jnp.float32)).astype(jnp.bfloat16)
    matrix = transfer_ref[...].reshape(leaves * rank, rank)
    spread = dot(
        jnp.concatenate([matrix, matrix], axis=1), jnp.concatenate([high, low], axis=0)
    )
    down = (far_ref[...] + spread).astype(jnp.bfloat16)
    for leaf in range(leaves):
        result = near_ref[leaf] + dot(row_ref[leaf], down[leaf * rank:(leaf + 1) * rank])
        out_ref[pl.ds(leaf * rows, rows), :] = result.astype(jnp.bfloat16)


def call(kernel, name, outs, specs, args, scratch=(), flops=0, moved=0, limit=4):
    many = isinstance(outs, tuple)
    return pl.pallas_call(
        kernel,
        out_shape=outs,
        in_specs=specs,
        out_specs=(VMEM,) * len(outs) if many else VMEM,
        scratch_shapes=list(scratch),
        cost_estimate=pl.CostEstimate(flops=flops, bytes_accessed=moved, transcendentals=0),
        compiler_params=pltpu.CompilerParams(vmem_limit_bytes=limit * MIB),
        name=name,
    )(*args)


def body(
    source,
    near_blocks,
    near_list,
    near_count,
    col_basis,
    row_basis,
    transfer,
    far_list,
    far_coupling,
    coarse_list,
    coarse_coupling,
):
    leaves, slots, rows, _ = near_blocks.shape
    rank = col_basis.shape[2]
    width = source.shape[1]
    count = lax.axis_size("row")
    far_slots = far_coupling.shape[1]

    def send(value, target):
        pairs = [(d, target(d)) for d in range(count) if 0 <= target(d) < count]
        return lax.ppermute(value, "row", pairs)

    def panel(blocks, dtype=jnp.bfloat16):
        return jax.ShapeDtypeStruct((blocks * rank, width), dtype)

    share, coef = call(
        coef_kernel, "coef",
        (jax.ShapeDtypeStruct((leaves * (rows + rank), width), jnp.bfloat16), panel(leaves)),
        [VMEM] * 2, (source, col_basis), flops=2 * leaves * rank * width * rows,
        moved=2 * leaves * rows * (width + rank), limit=8,
    )
    parent = call(parent_kernel, "parent", panel(1), [VMEM] * 2, (coef, transfer))
    layers = [send(parent, lambda d, bit=bit: d ^ bit) for bit in (4, 8, 12)]
    share_other = send(share, lambda d: d ^ 1)
    level = send(coef, lambda d: d ^ 2)
    panels = call(
        hand_kernel, "panels", jax.ShapeDtypeStruct(source.shape, jnp.bfloat16), [VMEM] + [ANY] * 3,
        (share, layers[0], layers[1], share_other),
    )
    across = send(panels, lambda d: d + 1 if d & 1 else d - 1)

    column = call(join_kernel, "column", panel(GROUP // 4), [VMEM] * 4, (parent, *layers))
    place = lax.axis_index("row")
    live = lax.broadcasted_iota(jnp.int32, (leaves, slots), 1) < near_count[:, None]
    which = jnp.minimum((near_list // leaves) ^ place, 2)
    index = jnp.where(live, which * leaves + near_list % leaves, 3 * leaves)
    def slots_scratch(panels):
        return [
            pltpu.VMEM(near_blocks.shape, jnp.bfloat16),
            pltpu.VMEM((panels * rows, width), jnp.bfloat16),
            pltpu.SMEM((leaves, slots + CHUNK), jnp.int32),
            pltpu.SemaphoreType.DMA((leaves, slots)),
            pltpu.SemaphoreType.DMA((2,)),
        ]

    shape = jax.ShapeDtypeStruct((leaves, rows, width), jnp.float32)
    early = call(
        near_kernel, "near", shape, [SMEM] + [ANY] * 4,
        (index, near_blocks, share, share_other, column),
        scratch=slots_scratch(2 * leaves + 1), flops=10**9, limit=48,
    )
    layer = send(level, lambda d: d - 4 if d & 2 else d + 4)
    beside = send(column, lambda d: d ^ 2)
    their_column = send(column, lambda d: d ^ 1)
    near = call(
        across_kernel, "across", shape, [SMEM, ANY, VMEM, ANY],
        (index, near_blocks, early, across),
        scratch=slots_scratch(leaves + 1), flops=0, limit=48,
    )
    picked_coef = call(
        pick_kernel, "pick", panel(leaves), [VMEM] * 2 + [ANY], (level, layer, early)
    )
    passed = send(picked_coef, lambda d: d ^ 1)
    far = call(
        far_kernel, "far", panel(leaves, jnp.float32), [SMEM, VMEM] + [ANY] * 4,
        (far_list, far_coupling, level, layer, share_other, passed),
        scratch=[
            pltpu.VMEM((4 * leaves * rank, width), jnp.bfloat16),
            pltpu.SemaphoreType.DMA((4,)),
        ],
        flops=2 * leaves * far_slots * rank * rank * width,
        moved=2 * leaves * far_slots * rank * rank, limit=10,
    )
    handed = call(hand_kernel, "hand", panel(GROUP // 4), [VMEM, ANY], (beside, near))
    their_beside = send(handed, lambda d: d ^ 1)
    return call(
        down_kernel, "down", jax.ShapeDtypeStruct(source.shape, jnp.bfloat16),
        [SMEM] + [VMEM] * 9,
        (
            coarse_list, transfer, coarse_coupling, row_basis, near, far,
            column, handed, their_column, their_beside,
        ),
        flops=8 * leaves * rank * rank * width,
        moved=4 * leaves * rows * width, limit=8,
    )


def solution(mesh):
    placed = (
        P(("clip", "row"), None),
        P(("clip", "row"), None, None, None),
        P(("clip", "row"), None),
        P(("clip", "row")),
        P(("clip", "row"), None, None),
        P(("clip", "row"), None, None),
        P(("clip", "row"), None, None),
        P(("clip", "row"), None),
        P(("clip", "row"), None, None, None),
        P(("clip", "row"), None),
        P(("clip", "row"), None, None, None),
    )
    return jax.shard_map(
        body, mesh=mesh, in_specs=placed, out_specs=P(("clip", "row"), None), check_vma=False
    )
```

```python
import jax
import jax.numpy as jnp
from jax import lax
from jax.experimental import pallas as pl
from jax.experimental.pallas import tpu as pltpu
from jax.sharding import PartitionSpec as P

GROUP = 16
CHUNK = 4
MIB = 2**20

VMEM = pl.BlockSpec(memory_space=pltpu.VMEM)
SMEM = pl.BlockSpec(memory_space=pltpu.SMEM)
ANY = pl.BlockSpec(memory_space=pl.ANY)


def dot(a, b):
    return jnp.dot(a, b, preferred_element_type=jnp.float32)


def dot_t(a, b):
    return lax.dot_general(
        a, b, (((0,), (0,)), ((), ())), preferred_element_type=jnp.float32
    )


def rows_at(index, rows):
    return pl.ds(pl.multiple_of(index * rows, rows), rows)


def coef_kernel(source_ref, col_ref, share_ref, coef_ref):
    leaves, rows, rank = col_ref.shape
    for leaf in range(leaves):
        panel = source_ref[pl.ds(leaf * rows, rows), :]
        share_ref[pl.ds(leaf * rows, rows), :] = panel
        coef = dot_t(col_ref[leaf], panel).astype(jnp.bfloat16)
        coef_ref[pl.ds(leaf * rank, rank), :] = coef
        share_ref[pl.ds(leaves * rows + leaf * rank, rank), :] = coef


def parent_kernel(coef_ref, transfer_ref, parent_ref):
    leaves, rank, _ = transfer_ref.shape
    total = None
    for leaf in range(leaves):
        term = dot_t(transfer_ref[leaf], coef_ref[pl.ds(leaf * rank, rank), :])
        total = term if total is None else total + term
    parent_ref[...] = total.astype(jnp.bfloat16)


def join_kernel(*refs):
    *pieces, _, out_ref = refs
    at = 0
    for ref in pieces:
        out_ref[pl.ds(at, ref.shape[0]), :] = ref[...]
        at += ref.shape[0]


def pick_kernel(level_ref, layer_ref, out_ref):
    corner = lax.axis_index("row") & 3
    level = (corner == 0) | (corner == 3)
    out_ref[...] = jnp.where(level, level_ref[...], layer_ref[...])


def hand_kernel(in_ref, *refs):
    out_ref = refs[-1]
    out_ref[...] = in_ref[pl.ds(0, out_ref.shape[0]), :]


def pick_slots(index_ref, blocks_hbm, blocks, sems, order_ref, low, high):
    leaves, slots, rows, _ = blocks.shape

    def picker(leaf):
        def step(slot, found):
            panel = index_ref[leaf, slot]
            kept = (panel >= low) & (panel < high)

            @pl.when(kept)
            def _():
                order_ref[leaf, found] = panel - low
                pltpu.make_async_copy(
                    blocks_hbm.at[leaf, slot], blocks.at[leaf, found], sems.at[leaf, found]
                ).start()

            return found + kept.astype(jnp.int32)

        return step

    found = [lax.fori_loop(0, slots, picker(leaf), 0) for leaf in range(leaves)]
    for leaf in range(leaves):
        for pad in range(CHUNK):
            order_ref[leaf, found[leaf] + pad] = high - low
    return found


def add_slots(total_ref, blocks_hbm, blocks, sems, order_ref, found, panels):
    leaves, slots, rows, _ = blocks.shape
    for leaf in range(leaves):
        count = found[leaf]

        def term(n):
            block = blocks[leaf, jnp.where(n < count, n, 0)]
            return dot(block, panels[rows_at(order_ref[leaf, n], rows), :])

        for first in range(0, slots, CHUNK):
            @pl.when(first < count)
            def _():
                for n in range(first, first + CHUNK):
                    @pl.when(n < count)
                    def _():
                        pltpu.make_async_copy(
                            blocks_hbm.at[leaf, 0], blocks.at[leaf, n], sems.at[leaf, n]
                        ).wait()
                even = term(first) + term(first + 2)
                odd = term(first + 1) + term(first + 3)
                total_ref[leaf] = total_ref[leaf] + (even + odd)


def near_kernel(
    index_ref, blocks_hbm, own_ref, share_ref,
    near_ref,
    blocks, panels, order, block_sems, panel_sems,
):
    leaves, _, rows, _ = blocks.shape
    size = leaves * rows
    pairs = [
        pltpu.make_async_copy(
            ref.at[pl.ds(0, size)], panels.at[pl.ds(which * size, size)], panel_sems.at[which]
        )
        for which, ref in enumerate((own_ref, share_ref))
    ]
    for copy in pairs:
        copy.start()
    found = pick_slots(index_ref, blocks_hbm, blocks, block_sems, order, 0, 2 * leaves)
    near_ref[...] = jnp.zeros(near_ref.shape, near_ref.dtype)
    panels[pl.ds(2 * size, rows), :] = jnp.zeros((rows, panels.shape[1]), panels.dtype)
    for copy in pairs:
        copy.wait()
    add_slots(near_ref, blocks_hbm, blocks, block_sems, order, found, panels)


def across_kernel(
    index_ref, blocks_hbm, near_ref, across_ref,
    total_ref,
    blocks, panels, order, block_sems, panel_sems,
):
    leaves, _, rows, _ = blocks.shape
    size = leaves * rows
    copy = pltpu.make_async_copy(across_ref, panels.at[pl.ds(0, size)], panel_sems.at[0])
    copy.start()
    found = pick_slots(
        index_ref, blocks_hbm, blocks, block_sems, order, 2 * leaves, 3 * leaves
    )
    total_ref[...] = near_ref[...]
    panels[pl.ds(size, rows), :] = jnp.zeros((rows, panels.shape[1]), panels.dtype)
    copy.wait()
    add_slots(total_ref, blocks_hbm, blocks, block_sems, order, found, panels)


def far_kernel(
    list_ref, coupling_ref, level_ref, layer_ref, share_ref, passed_ref,
    far_ref,
    coefs, sems,
):
    leaves, slots, rank, _ = coupling_ref.shape
    size = leaves * rank
    place = lax.axis_index("row")
    beyond = jnp.where((place & 2) == 0, place - 2, place + 2)
    copies = [
        pltpu.make_async_copy(
            ref.at[pl.ds(ref.shape[0] - size, size)], coefs.at[pl.ds(n * size, size)], sems.at[n]
        )
        for n, ref in enumerate((level_ref, layer_ref, share_ref, passed_ref))
    ]
    for copy in copies:
        copy.start()
    for copy in copies:
        copy.wait()

    def panel_of(leaf, slot):
        column = list_ref[leaf, slot]
        cluster = lax.div(column, leaves)
        which = jnp.where(
            cluster == (place ^ 2), 0,
            jnp.where(cluster == beyond, 1, jnp.where(cluster == (place ^ 1), 2, 3)),
        )
        return coefs[rows_at(which * leaves + column - cluster * leaves, rank), :]

    for leaf in range(leaves):
        total = None
        for slot in range(0, slots, 2):
            both = jnp.concatenate([coupling_ref[leaf, slot], coupling_ref[leaf, slot + 1]], axis=1)
            panels = jnp.concatenate([panel_of(leaf, slot), panel_of(leaf, slot + 1)], axis=0)
            term = dot(both, panels)
            total = term if total is None else total + term
        far_ref[pl.ds(leaf * rank, rank), :] = total


def down_kernel(
    list_ref, transfer_ref, coupling_ref, row_ref, near_ref, far_ref,
    column_ref, beside_ref, their_column_ref, their_beside_ref,
    out_ref,
):
    leaves, rows, rank = row_ref.shape
    local = lax.axis_index("row") & (GROUP - 1)

    def panel_of(slot):
        flip = (list_ref[0, slot] & (GROUP - 1)) ^ local
        where = rows_at(flip >> 2, rank)
        mine = jnp.where((flip & 2) == 0, column_ref[where, :], beside_ref[where, :])
        theirs = jnp.where((flip & 2) == 0, their_column_ref[where, :], their_beside_ref[where, :])
        return jnp.where((flip & 1) == 0, mine, theirs)

    terms = []
    for slot in range(0, list_ref.shape[1], 2):
        both = jnp.concatenate([coupling_ref[0, slot], coupling_ref[0, slot + 1]], axis=1)
        terms.append(dot(both, jnp.concatenate([panel_of(slot), panel_of(slot + 1)], axis=0)))
    while len(terms) > 1:
        terms = [first + second for first, second in zip(terms[::2], terms[1::2])]
    high = terms[0].astype(jnp.bfloat16)
    low = (terms[0] - high.astype(jnp.float32)).astype(jnp.bfloat16)
    matrix = transfer_ref[...].reshape(leaves * rank, rank)
    spread = dot(
        jnp.concatenate([matrix, matrix], axis=1), jnp.concatenate([high, low], axis=0)
    )
    down = (far_ref[...] + spread).astype(jnp.bfloat16)
    for leaf in range(leaves):
        result = near_ref[leaf] + dot(row_ref[leaf], down[leaf * rank:(leaf + 1) * rank])
        out_ref[pl.ds(leaf * rows, rows), :] = result.astype(jnp.bfloat16)


def call(kernel, name, outs, specs, args, scratch=(), flops=0, moved=0, limit=4):
    many = isinstance(outs, tuple)
    return pl.pallas_call(
        kernel,
        out_shape=outs,
        in_specs=specs,
        out_specs=(VMEM,) * len(outs) if many else VMEM,
        scratch_shapes=list(scratch),
        cost_estimate=pl.CostEstimate(flops=flops, bytes_accessed=moved, transcendentals=0),
        compiler_params=pltpu.CompilerParams(vmem_limit_bytes=limit * MIB),
        name=name,
    )(*args)


def body(
    source,
    near_blocks,
    near_list,
    near_count,
    col_basis,
    row_basis,
    transfer,
    far_list,
    far_coupling,
    coarse_list,
    coarse_coupling,
):
    leaves, slots, rows, _ = near_blocks.shape
    rank = col_basis.shape[2]
    width = source.shape[1]
    count = lax.axis_size("row")
    far_slots = far_coupling.shape[1]

    def send(value, target):
        pairs = [(d, target(d)) for d in range(count) if 0 <= target(d) < count]
        return lax.ppermute(value, "row", pairs)

    def panel(blocks, dtype=jnp.bfloat16):
        return jax.ShapeDtypeStruct((blocks * rank, width), dtype)

    share, coef = call(
        coef_kernel, "coef",
        (jax.ShapeDtypeStruct((leaves * (rows + rank), width), jnp.bfloat16), panel(leaves)),
        [VMEM] * 2, (source, col_basis), flops=2 * leaves * rank * width * rows,
        moved=2 * leaves * rows * (width + rank), limit=8,
    )
    parent = call(parent_kernel, "parent", panel(1), [VMEM] * 2, (coef, transfer))
    layers = [send(parent, lambda d, bit=bit: d ^ bit) for bit in (4, 8, 12)]
    share_other = send(share, lambda d: d ^ 1)
    level = send(coef, lambda d: d ^ 2)
    panels = call(
        hand_kernel, "panels", jax.ShapeDtypeStruct(source.shape, jnp.bfloat16), [VMEM] + [ANY] * 1,
        (share, share_other),
    )
    across = send(panels, lambda d: d + 1 if d & 1 else d - 1)

    place = lax.axis_index("row")
    live = lax.broadcasted_iota(jnp.int32, (leaves, slots), 1) < near_count[:, None]
    which = jnp.minimum((near_list // leaves) ^ place, 2)
    index = jnp.where(live, which * leaves + near_list % leaves, 3 * leaves)
    def slots_scratch(panels):
        return [
            pltpu.VMEM(near_blocks.shape, jnp.bfloat16),
            pltpu.VMEM((panels * rows, width), jnp.bfloat16),
            pltpu.SMEM((leaves, slots + CHUNK), jnp.int32),
            pltpu.SemaphoreType.DMA((leaves, slots)),
            pltpu.SemaphoreType.DMA((2,)),
        ]

    shape = jax.ShapeDtypeStruct((leaves, rows, width), jnp.float32)
    near = call(
        near_kernel, "near", shape, [SMEM] + [ANY] * 3,
        (index, near_blocks, share, share_other),
        scratch=slots_scratch(2 * leaves + 1), flops=10**9, limit=48,
    )
    layer = send(level, lambda d: d - 4 if d & 2 else d + 4)
    column = call(join_kernel, "column", panel(GROUP // 4), [VMEM] * 4 + [ANY],
        (parent, *layers, near))
    beside = send(column, lambda d: d ^ 2)
    their_column = send(column, lambda d: d ^ 1)
    near = call(
        across_kernel, "across", shape, [SMEM, ANY, VMEM, ANY],
        (index, near_blocks, near, across),
        scratch=slots_scratch(leaves + 1), flops=0, limit=48,
    )
    picked_coef = call(
        pick_kernel, "pick", panel(leaves), [VMEM] * 2, (level, layer)
    )
    passed = send(picked_coef, lambda d: d ^ 1)
    far = call(
        far_kernel, "far", panel(leaves, jnp.float32), [SMEM, VMEM] + [ANY] * 4,
        (far_list, far_coupling, level, layer, share_other, passed),
        scratch=[
            pltpu.VMEM((4 * leaves * rank, width), jnp.bfloat16),
            pltpu.SemaphoreType.DMA((4,)),
        ],
        flops=2 * leaves * far_slots * rank * rank * width,
        moved=2 * leaves * far_slots * rank * rank, limit=10,
    )
    handed = call(hand_kernel, "hand", panel(GROUP // 4), [VMEM, ANY], (beside, near))
    their_beside = send(handed, lambda d: d ^ 1)
    return call(
        down_kernel, "down", jax.ShapeDtypeStruct(source.shape, jnp.bfloat16),
        [SMEM] + [VMEM] * 9,
        (
            coarse_list, transfer, coarse_coupling, row_basis, near, far,
            column, handed, their_column, their_beside,
        ),
        flops=8 * leaves * rank * rank * width,
        moved=4 * leaves * rows * width, limit=8,
    )


def solution(mesh):
    placed = (
        P(("clip", "row"), None),
        P(("clip", "row"), None, None, None),
        P(("clip", "row"), None),
        P(("clip", "row")),
        P(("clip", "row"), None, None),
        P(("clip", "row"), None, None),
        P(("clip", "row"), None, None),
        P(("clip", "row"), None),
        P(("clip", "row"), None, None, None),
        P(("clip", "row"), None),
        P(("clip", "row"), None, None, None),
    )
    return jax.shard_map(
        body, mesh=mesh, in_specs=placed, out_specs=P(("clip", "row"), None), check_vma=False
    )
```

```python
import jax
import jax.numpy as jnp
from jax import lax
from jax.experimental import pallas as pl
from jax.experimental.pallas import tpu as pltpu
from jax.sharding import PartitionSpec as P

GROUP = 16
CHUNK = 4
MIB = 2**20

VMEM = pl.BlockSpec(memory_space=pltpu.VMEM)
SMEM = pl.BlockSpec(memory_space=pltpu.SMEM)
ANY = pl.BlockSpec(memory_space=pl.ANY)


def dot(a, b):
    return jnp.dot(a, b, preferred_element_type=jnp.float32)


def dot_t(a, b):
    return lax.dot_general(
        a, b, (((0,), (0,)), ((), ())), preferred_element_type=jnp.float32
    )


def rows_at(index, rows):
    return pl.ds(pl.multiple_of(index * rows, rows), rows)


def coef_kernel(source_ref, col_ref, share_ref, coef_ref):
    leaves, rows, rank = col_ref.shape
    for leaf in range(leaves):
        panel = source_ref[pl.ds(leaf * rows, rows), :]
        share_ref[pl.ds(leaf * rows, rows), :] = panel
        coef = dot_t(col_ref[leaf], panel).astype(jnp.bfloat16)
        coef_ref[pl.ds(leaf * rank, rank), :] = coef
        share_ref[pl.ds(leaves * rows + leaf * rank, rank), :] = coef


def parent_kernel(coef_ref, transfer_ref, parent_ref):
    leaves, rank, _ = transfer_ref.shape
    total = None
    for leaf in range(leaves):
        term = dot_t(transfer_ref[leaf], coef_ref[pl.ds(leaf * rank, rank), :])
        total = term if total is None else total + term
    parent_ref[...] = total.astype(jnp.bfloat16)


def unused_layer(place):
    layer = (place >> 2) & 3
    corner = place & 3
    below = ((layer + 3) & 3) ^ layer
    above = ((layer + 1) & 3) ^ layer
    return jnp.where(corner == 1, below, jnp.where(corner == 2, above, 0))


def column_kernel(own_ref, first_ref, second_ref, third_ref, _, column_ref, sent_ref):
    rank = own_ref.shape[0]
    for n, ref in enumerate((own_ref, first_ref, second_ref, third_ref)):
        column_ref[pl.ds(n * rank, rank), :] = ref[...]
    unused = unused_layer(lax.axis_index("row") ^ 2)
    for n in range(GROUP // 4 - 1):
        index = jnp.where(n < unused, n, n + 1)
        sent_ref[pl.ds(n * rank, rank), :] = column_ref[rows_at(index, rank), :]


def pick_kernel(level_ref, layer_ref, out_ref):
    corner = lax.axis_index("row") & 3
    level = (corner == 0) | (corner == 3)
    out_ref[...] = jnp.where(level, level_ref[...], layer_ref[...])


def hand_kernel(in_ref, *refs):
    out_ref = refs[-1]
    out_ref[...] = in_ref[pl.ds(0, out_ref.shape[0]), :]


def pick_slots(index_ref, blocks_hbm, blocks, sems, order_ref, low, high):
    leaves, slots, rows, _ = blocks.shape

    def picker(leaf):
        def step(slot, found):
            panel = index_ref[leaf, slot]
            kept = (panel >= low) & (panel < high)

            @pl.when(kept)
            def _():
                order_ref[leaf, found] = panel - low
                pltpu.make_async_copy(
                    blocks_hbm.at[leaf, slot], blocks.at[leaf, found], sems.at[leaf, found]
                ).start()

            return found + kept.astype(jnp.int32)

        return step

    found = [lax.fori_loop(0, slots, picker(leaf), 0) for leaf in range(leaves)]
    for leaf in range(leaves):
        for pad in range(CHUNK):
            order_ref[leaf, found[leaf] + pad] = high - low
    return found


def add_slots(total_ref, blocks_hbm, blocks, sems, order_ref, found, panels):
    leaves, slots, rows, _ = blocks.shape
    for leaf in range(leaves):
        count = found[leaf]

        def term(n):
            block = blocks[leaf, jnp.where(n < count, n, 0)]
            return dot(block, panels[rows_at(order_ref[leaf, n], rows), :])

        for first in range(0, slots, CHUNK):
            @pl.when(first < count)
            def _():
                for n in range(first, first + CHUNK):
                    @pl.when(n < count)
                    def _():
                        pltpu.make_async_copy(
                            blocks_hbm.at[leaf, 0], blocks.at[leaf, n], sems.at[leaf, n]
                        ).wait()
                even = term(first) + term(first + 2)
                odd = term(first + 1) + term(first + 3)
                total_ref[leaf] = total_ref[leaf] + (even + odd)


def near_kernel(
    index_ref, blocks_hbm, own_ref, share_ref,
    near_ref,
    blocks, panels, order, block_sems, panel_sems,
):
    leaves, _, rows, _ = blocks.shape
    size = leaves * rows
    pairs = [
        pltpu.make_async_copy(
            ref.at[pl.ds(0, size)], panels.at[pl.ds(which * size, size)], panel_sems.at[which]
        )
        for which, ref in enumerate((own_ref, share_ref))
    ]
    for copy in pairs:
        copy.start()
    found = pick_slots(index_ref, blocks_hbm, blocks, block_sems, order, 0, 2 * leaves)
    near_ref[...] = jnp.zeros(near_ref.shape, near_ref.dtype)
    panels[pl.ds(2 * size, rows), :] = jnp.zeros((rows, panels.shape[1]), panels.dtype)
    for copy in pairs:
        copy.wait()
    add_slots(near_ref, blocks_hbm, blocks, block_sems, order, found, panels)


def across_kernel(
    index_ref, blocks_hbm, near_ref, across_ref,
    total_ref,
    blocks, panels, order, block_sems, panel_sems,
):
    leaves, _, rows, _ = blocks.shape
    size = leaves * rows
    copy = pltpu.make_async_copy(across_ref, panels.at[pl.ds(0, size)], panel_sems.at[0])
    copy.start()
    found = pick_slots(
        index_ref, blocks_hbm, blocks, block_sems, order, 2 * leaves, 3 * leaves
    )
    total_ref[...] = near_ref[...]
    panels[pl.ds(size, rows), :] = jnp.zeros((rows, panels.shape[1]), panels.dtype)
    copy.wait()
    add_slots(total_ref, blocks_hbm, blocks, block_sems, order, found, panels)


def far_kernel(
    list_ref, coupling_ref, level_ref, layer_ref, share_ref, passed_ref,
    far_ref,
    coefs, sems,
):
    leaves, slots, rank, _ = coupling_ref.shape
    size = leaves * rank
    place = lax.axis_index("row")
    beyond = jnp.where((place & 2) == 0, place - 2, place + 2)
    copies = [
        pltpu.make_async_copy(
            ref.at[pl.ds(ref.shape[0] - size, size)], coefs.at[pl.ds(n * size, size)], sems.at[n]
        )
        for n, ref in enumerate((level_ref, layer_ref, share_ref, passed_ref))
    ]
    for copy in copies:
        copy.start()
    for copy in copies:
        copy.wait()

    def panel_of(leaf, slot):
        column = list_ref[leaf, slot]
        cluster = lax.div(column, leaves)
        which = jnp.where(
            cluster == (place ^ 2), 0,
            jnp.where(cluster == beyond, 1, jnp.where(cluster == (place ^ 1), 2, 3)),
        )
        return coefs[rows_at(which * leaves + column - cluster * leaves, rank), :]

    for leaf in range(leaves):
        total = None
        for slot in range(0, slots, 2):
            both = jnp.concatenate([coupling_ref[leaf, slot], coupling_ref[leaf, slot + 1]], axis=1)
            panels = jnp.concatenate([panel_of(leaf, slot), panel_of(leaf, slot + 1)], axis=0)
            term = dot(both, panels)
            total = term if total is None else total + term
        far_ref[pl.ds(leaf * rank, rank), :] = total


def down_kernel(
    list_ref, transfer_ref, coupling_ref, row_ref, near_ref, far_ref,
    column_ref, beside_ref, their_column_ref, their_beside_ref,
    out_ref,
):
    leaves, rows, rank = row_ref.shape
    local = lax.axis_index("row") & (GROUP - 1)
    unused, their_unused = unused_layer(local), unused_layer(local ^ 1)

    def panel_of(slot):
        flip = (list_ref[0, slot] & (GROUP - 1)) ^ local
        layer = flip >> 2

        def beside(ref, gap):
            index = jnp.minimum(jnp.where(layer > gap, layer - 1, layer), GROUP // 4 - 2)
            return ref[rows_at(index, rank), :]

        where = rows_at(layer, rank)
        same = (flip & 2) == 0
        mine = jnp.where(same, column_ref[where, :], beside(beside_ref, unused))
        theirs = jnp.where(
            same, their_column_ref[where, :], beside(their_beside_ref, their_unused)
        )
        return jnp.where((flip & 1) == 0, mine, theirs)

    terms = []
    for slot in range(0, list_ref.shape[1], 2):
        both = jnp.concatenate([coupling_ref[0, slot], coupling_ref[0, slot + 1]], axis=1)
        terms.append(dot(both, jnp.concatenate([panel_of(slot), panel_of(slot + 1)], axis=0)))
    while len(terms) > 1:
        terms = [first + second for first, second in zip(terms[::2], terms[1::2])]
    high = terms[0].astype(jnp.bfloat16)
    low = (terms[0] - high.astype(jnp.float32)).astype(jnp.bfloat16)
    matrix = transfer_ref[...].reshape(leaves * rank, rank)
    spread = dot(
        jnp.concatenate([matrix, matrix], axis=1), jnp.concatenate([high, low], axis=0)
    )
    down = (far_ref[...] + spread).astype(jnp.bfloat16)
    for leaf in range(leaves):
        result = near_ref[leaf] + dot(row_ref[leaf], down[leaf * rank:(leaf + 1) * rank])
        out_ref[pl.ds(leaf * rows, rows), :] = result.astype(jnp.bfloat16)


def call(kernel, name, outs, specs, args, scratch=(), flops=0, moved=0, limit=4):
    many = isinstance(outs, tuple)
    return pl.pallas_call(
        kernel,
        out_shape=outs,
        in_specs=specs,
        out_specs=(VMEM,) * len(outs) if many else VMEM,
        scratch_shapes=list(scratch),
        cost_estimate=pl.CostEstimate(flops=flops, bytes_accessed=moved, transcendentals=0),
        compiler_params=pltpu.CompilerParams(vmem_limit_bytes=limit * MIB),
        name=name,
    )(*args)


def body(
    source,
    near_blocks,
    near_list,
    near_count,
    col_basis,
    row_basis,
    transfer,
    far_list,
    far_coupling,
    coarse_list,
    coarse_coupling,
):
    leaves, slots, rows, _ = near_blocks.shape
    rank = col_basis.shape[2]
    width = source.shape[1]
    count = lax.axis_size("row")
    far_slots = far_coupling.shape[1]

    def send(value, target):
        pairs = [(d, target(d)) for d in range(count) if 0 <= target(d) < count]
        return lax.ppermute(value, "row", pairs)

    def panel(blocks, dtype=jnp.bfloat16):
        return jax.ShapeDtypeStruct((blocks * rank, width), dtype)

    share, coef = call(
        coef_kernel, "coef",
        (jax.ShapeDtypeStruct((leaves * (rows + rank), width), jnp.bfloat16), panel(leaves)),
        [VMEM] * 2, (source, col_basis), flops=2 * leaves * rank * width * rows,
        moved=2 * leaves * rows * (width + rank), limit=8,
    )
    parent = call(parent_kernel, "parent", panel(1), [VMEM] * 2, (coef, transfer))
    layers = [send(parent, lambda d, bit=bit: d ^ bit) for bit in (4, 8, 12)]
    share_other = send(share, lambda d: d ^ 1)
    level = send(coef, lambda d: d ^ 2)
    panels = call(
        hand_kernel, "panels", jax.ShapeDtypeStruct(source.shape, jnp.bfloat16), [VMEM] + [ANY] * 1,
        (share, share_other),
    )
    across = send(panels, lambda d: d + 1 if d & 1 else d - 1)

    place = lax.axis_index("row")
    live = lax.broadcasted_iota(jnp.int32, (leaves, slots), 1) < near_count[:, None]
    which = jnp.minimum((near_list // leaves) ^ place, 2)
    index = jnp.where(live, which * leaves + near_list % leaves, 3 * leaves)
    def slots_scratch(panels):
        return [
            pltpu.VMEM(near_blocks.shape, jnp.bfloat16),
            pltpu.VMEM((panels * rows, width), jnp.bfloat16),
            pltpu.SMEM((leaves, slots + CHUNK), jnp.int32),
            pltpu.SemaphoreType.DMA((leaves, slots)),
            pltpu.SemaphoreType.DMA((2,)),
        ]

    shape = jax.ShapeDtypeStruct((leaves, rows, width), jnp.float32)
    near = call(
        near_kernel, "near", shape, [SMEM] + [ANY] * 3,
        (index, near_blocks, share, share_other),
        scratch=slots_scratch(2 * leaves + 1), flops=2*10**9, limit=48,
    )
    layer = send(level, lambda d: d - 4 if d & 2 else d + 4)
    column, sent = call(
        column_kernel, "column", (panel(GROUP // 4), panel(GROUP // 4 - 1)),
        [VMEM] * 4 + [ANY], (parent, *layers, near),
    )
    beside = send(sent, lambda d: d ^ 2)
    their_column = send(column, lambda d: d ^ 1)
    near = call(
        across_kernel, "across", shape, [SMEM, ANY, VMEM, ANY],
        (index, near_blocks, near, across),
        scratch=slots_scratch(leaves + 1), flops=0, limit=48,
    )
    picked_coef = call(
        pick_kernel, "pick", panel(leaves), [VMEM] * 2, (level, layer)
    )
    passed = send(picked_coef, lambda d: d ^ 1)
    far = call(
        far_kernel, "far", panel(leaves, jnp.float32), [SMEM, VMEM] + [ANY] * 4,
        (far_list, far_coupling, level, layer, share_other, passed),
        scratch=[
            pltpu.VMEM((4 * leaves * rank, width), jnp.bfloat16),
            pltpu.SemaphoreType.DMA((4,)),
        ],
        flops=2 * leaves * far_slots * rank * rank * width,
        moved=2 * leaves * far_slots * rank * rank, limit=10,
    )
    handed = call(hand_kernel, "hand", panel(GROUP // 4 - 1), [VMEM, ANY], (beside, near))
    their_beside = send(handed, lambda d: d ^ 1)
    return call(
        down_kernel, "down", jax.ShapeDtypeStruct(source.shape, jnp.bfloat16),
        [SMEM] + [VMEM] * 9,
        (
            coarse_list, transfer, coarse_coupling, row_basis, near, far,
            column, handed, their_column, their_beside,
        ),
        flops=8 * leaves * rank * rank * width,
        moved=4 * leaves * rows * width, limit=8,
    )


def solution(mesh):
    placed = (
        P(("clip", "row"), None),
        P(("clip", "row"), None, None, None),
        P(("clip", "row"), None),
        P(("clip", "row")),
        P(("clip", "row"), None, None),
        P(("clip", "row"), None, None),
        P(("clip", "row"), None, None),
        P(("clip", "row"), None),
        P(("clip", "row"), None, None, None),
        P(("clip", "row"), None),
        P(("clip", "row"), None, None, None),
    )
    return jax.shard_map(
        body, mesh=mesh, in_specs=placed, out_specs=P(("clip", "row"), None), check_vma=False
    )
```

```python
import jax
import jax.numpy as jnp
from jax import lax
from jax.experimental import pallas as pl
from jax.experimental.pallas import tpu as pltpu
from jax.sharding import PartitionSpec as P

GROUP = 16
CHUNK = 2
MIB = 2**20

VMEM = pl.BlockSpec(memory_space=pltpu.VMEM)
SMEM = pl.BlockSpec(memory_space=pltpu.SMEM)
ANY = pl.BlockSpec(memory_space=pl.ANY)


def dot(a, b):
    return jnp.dot(a, b, preferred_element_type=jnp.float32)


def dot_t(a, b):
    return lax.dot_general(
        a, b, (((0,), (0,)), ((), ())), preferred_element_type=jnp.float32
    )


def rows_at(index, rows):
    return pl.ds(pl.multiple_of(index * rows, rows), rows)


def coef_kernel(source_ref, col_ref, share_ref, coef_ref):
    leaves, rows, rank = col_ref.shape
    for leaf in range(leaves):
        panel = source_ref[pl.ds(leaf * rows, rows), :]
        share_ref[pl.ds(leaf * rows, rows), :] = panel
        coef = dot_t(col_ref[leaf], panel).astype(jnp.bfloat16)
        coef_ref[pl.ds(leaf * rank, rank), :] = coef
        share_ref[pl.ds(leaves * rows + leaf * rank, rank), :] = coef


def parent_kernel(coef_ref, transfer_ref, parent_ref):
    leaves, rank, _ = transfer_ref.shape
    total = None
    for leaf in range(leaves):
        term = dot_t(transfer_ref[leaf], coef_ref[pl.ds(leaf * rank, rank), :])
        total = term if total is None else total + term
    parent_ref[...] = total.astype(jnp.bfloat16)


def unused_layer(place):
    layer = (place >> 2) & 3
    corner = place & 3
    below = ((layer + 3) & 3) ^ layer
    above = ((layer + 1) & 3) ^ layer
    return jnp.where(corner == 1, below, jnp.where(corner == 2, above, 0))


def column_kernel(own_ref, first_ref, second_ref, third_ref, _, column_ref, sent_ref):
    rank = own_ref.shape[0]
    for n, ref in enumerate((own_ref, first_ref, second_ref, third_ref)):
        column_ref[pl.ds(n * rank, rank), :] = ref[...]
    unused = unused_layer(lax.axis_index("row") ^ 2)
    for n in range(GROUP // 4 - 1):
        index = jnp.where(n < unused, n, n + 1)
        sent_ref[pl.ds(n * rank, rank), :] = column_ref[rows_at(index, rank), :]


def pick_kernel(level_ref, layer_ref, out_ref):
    corner = lax.axis_index("row") & 3
    level = (corner == 0) | (corner == 3)
    out_ref[...] = jnp.where(level, level_ref[...], layer_ref[...])


def hand_kernel(in_ref, *refs):
    out_ref = refs[-1]
    out_ref[...] = in_ref[pl.ds(0, out_ref.shape[0]), :]


def pick_slots(index_ref, blocks_hbm, blocks, sems, order_ref, low, high):
    leaves, slots, rows, _ = blocks.shape

    def picker(leaf):
        def step(slot, found):
            panel = index_ref[leaf, slot]
            kept = (panel >= low) & (panel < high)

            @pl.when(kept)
            def _():
                order_ref[leaf, found] = panel - low
                pltpu.make_async_copy(
                    blocks_hbm.at[leaf, slot], blocks.at[leaf, found], sems.at[leaf, found]
                ).start()

            return found + kept.astype(jnp.int32)

        return step

    found = [lax.fori_loop(0, slots, picker(leaf), 0) for leaf in range(leaves)]
    for leaf in range(leaves):
        for pad in range(CHUNK):
            order_ref[leaf, found[leaf] + pad] = high - low
    return found


def add_slots(total_ref, blocks_hbm, blocks, sems, order_ref, found, panels):
    leaves, slots, rows, _ = blocks.shape
    for leaf in range(leaves):
        count = found[leaf]

        def term(n):
            block = blocks[leaf, jnp.where(n < count, n, 0)]
            return dot(block, panels[rows_at(order_ref[leaf, n], rows), :])

        for first in range(0, slots, CHUNK):
            @pl.when(first < count)
            def _():
                for n in range(first, first + CHUNK):
                    @pl.when(n < count)
                    def _():
                        pltpu.make_async_copy(
                            blocks_hbm.at[leaf, 0], blocks.at[leaf, n], sems.at[leaf, n]
                        ).wait()
                total_ref[leaf] = total_ref[leaf] + (term(first) + term(first + 1))


def near_kernel(
    index_ref, blocks_hbm, own_ref, share_ref,
    near_ref,
    blocks, panels, order, block_sems, panel_sems,
):
    leaves, _, rows, _ = blocks.shape
    size = leaves * rows
    pairs = [
        pltpu.make_async_copy(
            ref.at[pl.ds(0, size)], panels.at[pl.ds(which * size, size)], panel_sems.at[which]
        )
        for which, ref in enumerate((own_ref, share_ref))
    ]
    for copy in pairs:
        copy.start()
    found = pick_slots(index_ref, blocks_hbm, blocks, block_sems, order, 0, 2 * leaves)
    near_ref[...] = jnp.zeros(near_ref.shape, near_ref.dtype)
    panels[pl.ds(2 * size, rows), :] = jnp.zeros((rows, panels.shape[1]), panels.dtype)
    for copy in pairs:
        copy.wait()
    add_slots(near_ref, blocks_hbm, blocks, block_sems, order, found, panels)


def across_kernel(
    index_ref, blocks_hbm, near_ref, across_ref,
    total_ref,
    blocks, panels, order, block_sems, panel_sems,
):
    leaves, _, rows, _ = blocks.shape
    size = leaves * rows
    copy = pltpu.make_async_copy(across_ref, panels.at[pl.ds(0, size)], panel_sems.at[0])
    copy.start()
    found = pick_slots(
        index_ref, blocks_hbm, blocks, block_sems, order, 2 * leaves, 3 * leaves
    )
    total_ref[...] = near_ref[...]
    panels[pl.ds(size, rows), :] = jnp.zeros((rows, panels.shape[1]), panels.dtype)
    copy.wait()
    add_slots(total_ref, blocks_hbm, blocks, block_sems, order, found, panels)


def far_kernel(
    list_ref, coupling_ref, level_ref, layer_ref, share_ref, passed_ref,
    far_ref,
    coefs, sems,
):
    leaves, slots, rank, _ = coupling_ref.shape
    size = leaves * rank
    place = lax.axis_index("row")
    beyond = jnp.where((place & 2) == 0, place - 2, place + 2)
    copies = [
        pltpu.make_async_copy(
            ref.at[pl.ds(ref.shape[0] - size, size)], coefs.at[pl.ds(n * size, size)], sems.at[n]
        )
        for n, ref in enumerate((level_ref, layer_ref, share_ref, passed_ref))
    ]
    for copy in copies:
        copy.start()
    for copy in copies:
        copy.wait()

    def panel_of(leaf, slot):
        column = list_ref[leaf, slot]
        cluster = lax.div(column, leaves)
        which = jnp.where(
            cluster == (place ^ 2), 0,
            jnp.where(cluster == beyond, 1, jnp.where(cluster == (place ^ 1), 2, 3)),
        )
        return coefs[rows_at(which * leaves + column - cluster * leaves, rank), :]

    for leaf in range(leaves):
        total = None
        for slot in range(0, slots, 2):
            both = jnp.concatenate([coupling_ref[leaf, slot], coupling_ref[leaf, slot + 1]], axis=1)
            panels = jnp.concatenate([panel_of(leaf, slot), panel_of(leaf, slot + 1)], axis=0)
            term = dot(both, panels)
            total = term if total is None else total + term
        far_ref[pl.ds(leaf * rank, rank), :] = total


def down_kernel(
    list_ref, transfer_ref, coupling_ref, row_ref, near_ref, far_ref,
    column_ref, beside_ref, their_column_ref, their_beside_ref,
    out_hbm,
    out, sems,
):
    leaves, rows, rank = row_ref.shape
    local = lax.axis_index("row") & (GROUP - 1)
    unused, their_unused = unused_layer(local), unused_layer(local ^ 1)

    def panel_of(slot):
        flip = (list_ref[0, slot] & (GROUP - 1)) ^ local
        layer = flip >> 2

        def beside(ref, gap):
            index = jnp.minimum(jnp.where(layer > gap, layer - 1, layer), GROUP // 4 - 2)
            return ref[rows_at(index, rank), :]

        where = rows_at(layer, rank)
        same = (flip & 2) == 0
        mine = jnp.where(same, column_ref[where, :], beside(beside_ref, unused))
        theirs = jnp.where(
            same, their_column_ref[where, :], beside(their_beside_ref, their_unused)
        )
        return jnp.where((flip & 1) == 0, mine, theirs)

    terms = []
    for slot in range(0, list_ref.shape[1], 2):
        both = jnp.concatenate([coupling_ref[0, slot], coupling_ref[0, slot + 1]], axis=1)
        terms.append(dot(both, jnp.concatenate([panel_of(slot), panel_of(slot + 1)], axis=0)))
    while len(terms) > 1:
        terms = [first + second for first, second in zip(terms[::2], terms[1::2])]
    high = terms[0].astype(jnp.bfloat16)
    low = (terms[0] - high.astype(jnp.float32)).astype(jnp.bfloat16)
    matrix = transfer_ref[...].reshape(leaves * rank, rank)
    spread = dot(
        jnp.concatenate([matrix, matrix], axis=1), jnp.concatenate([high, low], axis=0)
    )
    down = (far_ref[...] + spread).astype(jnp.bfloat16)
    copies = []
    for leaf in range(leaves):
        result = near_ref[leaf] + dot(row_ref[leaf], down[leaf * rank:(leaf + 1) * rank])
        here = pl.ds(leaf * rows, rows)
        out[here, :] = result.astype(jnp.bfloat16)
        copies.append(pltpu.make_async_copy(out.at[here], out_hbm.at[here], sems.at[leaf]))
        copies[-1].start()
    for copy in copies:
        copy.wait()


def call(kernel, name, outs, specs, args, scratch=(), flops=0, moved=0, limit=4, to=VMEM):
    many = isinstance(outs, tuple)
    return pl.pallas_call(
        kernel,
        out_shape=outs,
        in_specs=specs,
        out_specs=(to,) * len(outs) if many else to,
        scratch_shapes=list(scratch),
        cost_estimate=pl.CostEstimate(flops=flops, bytes_accessed=moved, transcendentals=0),
        compiler_params=pltpu.CompilerParams(vmem_limit_bytes=limit * MIB),
        name=name,
    )(*args)


def body(
    source,
    near_blocks,
    near_list,
    near_count,
    col_basis,
    row_basis,
    transfer,
    far_list,
    far_coupling,
    coarse_list,
    coarse_coupling,
):
    leaves, slots, rows, _ = near_blocks.shape
    rank = col_basis.shape[2]
    width = source.shape[1]
    count = lax.axis_size("row")
    far_slots = far_coupling.shape[1]

    def send(value, target):
        pairs = [(d, target(d)) for d in range(count) if 0 <= target(d) < count]
        return lax.ppermute(value, "row", pairs)

    def panel(blocks, dtype=jnp.bfloat16):
        return jax.ShapeDtypeStruct((blocks * rank, width), dtype)

    share, coef = call(
        coef_kernel, "coef",
        (jax.ShapeDtypeStruct((leaves * (rows + rank), width), jnp.bfloat16), panel(leaves)),
        [VMEM] * 2, (source, col_basis), flops=2 * leaves * rank * width * rows,
        moved=2 * leaves * rows * (width + rank), limit=8,
    )
    parent = call(parent_kernel, "parent", panel(1), [VMEM] * 2, (coef, transfer))
    layers = [send(parent, lambda d, bit=bit: d ^ bit) for bit in (4, 8, 12)]
    share_other = send(share, lambda d: d ^ 1)
    level = send(coef, lambda d: d ^ 2)
    panels = call(
        hand_kernel, "panels", jax.ShapeDtypeStruct(source.shape, jnp.bfloat16), [VMEM] + [ANY] * 1,
        (share, share_other),
    )
    across = send(panels, lambda d: d + 1 if d & 1 else d - 1)

    place = lax.axis_index("row")
    live = lax.broadcasted_iota(jnp.int32, (leaves, slots), 1) < near_count[:, None]
    which = jnp.minimum((near_list // leaves) ^ place, 2)
    index = jnp.where(live, which * leaves + near_list % leaves, 3 * leaves)
    def slots_scratch(panels):
        return [
            pltpu.VMEM(near_blocks.shape, jnp.bfloat16),
            pltpu.VMEM((panels * rows, width), jnp.bfloat16),
            pltpu.SMEM((leaves, slots + CHUNK), jnp.int32),
            pltpu.SemaphoreType.DMA((leaves, slots)),
            pltpu.SemaphoreType.DMA((2,)),
        ]

    shape = jax.ShapeDtypeStruct((leaves, rows, width), jnp.float32)
    near = call(
        near_kernel, "near", shape, [SMEM] + [ANY] * 3,
        (index, near_blocks, share, share_other),
        scratch=slots_scratch(2 * leaves + 1), flops=2*10**9, limit=48,
    )
    layer = send(level, lambda d: d - 4 if d & 2 else d + 4)
    column, sent = call(
        column_kernel, "column", (panel(GROUP // 4), panel(GROUP // 4 - 1)),
        [VMEM] * 4 + [ANY], (parent, *layers, near),
    )
    beside = send(sent, lambda d: d ^ 2)
    their_column = send(column, lambda d: d ^ 1)
    near = call(
        across_kernel, "across", shape, [SMEM, ANY, VMEM, ANY],
        (index, near_blocks, near, across),
        scratch=slots_scratch(leaves + 1), flops=0, limit=48,
    )
    picked_coef = call(
        pick_kernel, "pick", panel(leaves), [VMEM] * 2, (level, layer)
    )
    passed = send(picked_coef, lambda d: d ^ 1)
    far = call(
        far_kernel, "far", panel(leaves, jnp.float32), [SMEM, VMEM] + [ANY] * 4,
        (far_list, far_coupling, level, layer, share_other, passed),
        scratch=[
            pltpu.VMEM((4 * leaves * rank, width), jnp.bfloat16),
            pltpu.SemaphoreType.DMA((4,)),
        ],
        flops=2 * leaves * far_slots * rank * rank * width,
        moved=2 * leaves * far_slots * rank * rank, limit=10,
    )
    handed = call(hand_kernel, "hand", panel(GROUP // 4 - 1), [VMEM, ANY], (beside, near))
    their_beside = send(handed, lambda d: d ^ 1)
    return call(
        down_kernel, "down", jax.ShapeDtypeStruct(source.shape, jnp.bfloat16),
        [SMEM] + [VMEM] * 9,
        (
            coarse_list, transfer, coarse_coupling, row_basis, near, far,
            column, handed, their_column, their_beside,
        ),
        flops=8 * leaves * rank * rank * width,
        scratch=[
            pltpu.VMEM(source.shape, jnp.bfloat16),
            pltpu.SemaphoreType.DMA((leaves,)),
        ],
        moved=4 * leaves * rows * width, limit=8, to=ANY,
    )


def solution(mesh):
    placed = (
        P(("clip", "row"), None),
        P(("clip", "row"), None, None, None),
        P(("clip", "row"), None),
        P(("clip", "row")),
        P(("clip", "row"), None, None),
        P(("clip", "row"), None, None),
        P(("clip", "row"), None, None),
        P(("clip", "row"), None),
        P(("clip", "row"), None, None, None),
        P(("clip", "row"), None),
        P(("clip", "row"), None, None, None),
    )
    return jax.shard_map(
        body, mesh=mesh, in_specs=placed, out_specs=P(("clip", "row"), None), check_vma=False
    )
```

```python
import jax
import jax.numpy as jnp
from jax import lax
from jax.experimental import pallas as pl
from jax.experimental.pallas import tpu as pltpu
from jax.sharding import PartitionSpec as P

GROUP = 16
CHUNK = 2
MIB = 2**20

VMEM = pl.BlockSpec(memory_space=pltpu.VMEM)
SMEM = pl.BlockSpec(memory_space=pltpu.SMEM)
ANY = pl.BlockSpec(memory_space=pl.ANY)


def dot(a, b):
    return jnp.dot(a, b, preferred_element_type=jnp.float32)


def dot_t(a, b):
    return lax.dot_general(
        a, b, (((0,), (0,)), ((), ())), preferred_element_type=jnp.float32
    )


def rows_at(index, rows):
    return pl.ds(pl.multiple_of(index * rows, rows), rows)


def coef_kernel(source_ref, col_ref, coef_ref):
    leaves, rows, rank = col_ref.shape
    for leaf in range(leaves):
        panel = source_ref[pl.ds(leaf * rows, rows), :]
        coef_ref[pl.ds(leaf * rank, rank), :] = dot_t(col_ref[leaf], panel).astype(jnp.bfloat16)


def parent_kernel(coef_ref, transfer_ref, parent_ref):
    leaves, rank, _ = transfer_ref.shape
    total = None
    for leaf in range(leaves):
        term = dot_t(transfer_ref[leaf], coef_ref[pl.ds(leaf * rank, rank), :])
        total = term if total is None else total + term
    parent_ref[...] = total.astype(jnp.bfloat16)


def unused_layer(place):
    layer = (place >> 2) & 3
    corner = place & 3
    below = ((layer + 3) & 3) ^ layer
    above = ((layer + 1) & 3) ^ layer
    return jnp.where(corner == 1, below, jnp.where(corner == 2, above, 0))


def column_kernel(own_ref, first_ref, second_ref, third_ref, coef_ref, _, column_ref, sent_ref):
    rank = own_ref.shape[0]
    for n, ref in enumerate((own_ref, first_ref, second_ref, third_ref)):
        column_ref[pl.ds(n * rank, rank), :] = ref[...]
    column_ref[pl.ds(4 * rank, coef_ref.shape[0]), :] = coef_ref[...]
    unused = unused_layer(lax.axis_index("row") ^ 2)
    for n in range(GROUP // 4 - 1):
        index = jnp.where(n < unused, n, n + 1)
        sent_ref[pl.ds(n * rank, rank), :] = column_ref[rows_at(index, rank), :]


def pick_kernel(level_ref, layer_ref, out_ref):
    corner = lax.axis_index("row") & 3
    level = (corner == 0) | (corner == 3)
    out_ref[...] = jnp.where(level, level_ref[...], layer_ref[...])


def hand_kernel(in_ref, *refs):
    out_ref = refs[-1]
    out_ref[...] = in_ref[pl.ds(0, out_ref.shape[0]), :]


def pick_slots(index_ref, blocks_hbm, blocks, sems, order_ref, low, high):
    leaves, slots, rows, _ = blocks.shape

    def picker(leaf):
        def step(slot, found):
            panel = index_ref[leaf, slot]
            kept = (panel >= low) & (panel < high)

            @pl.when(kept)
            def _():
                order_ref[leaf, found] = panel - low
                pltpu.make_async_copy(
                    blocks_hbm.at[leaf, slot], blocks.at[leaf, found], sems.at[leaf, found]
                ).start()

            return found + kept.astype(jnp.int32)

        return step

    found = [lax.fori_loop(0, slots, picker(leaf), 0) for leaf in range(leaves)]
    for leaf in range(leaves):
        for pad in range(CHUNK):
            order_ref[leaf, found[leaf] + pad] = high - low
    return found


def add_slots(total_ref, blocks_hbm, blocks, sems, order_ref, found, panels):
    leaves, slots, rows, _ = blocks.shape
    for leaf in range(leaves):
        count = found[leaf]

        def term(n):
            block = blocks[leaf, jnp.where(n < count, n, 0)]
            return dot(block, panels[rows_at(order_ref[leaf, n], rows), :])

        for first in range(0, slots, CHUNK):
            @pl.when(first < count)
            def _():
                for n in range(first, first + CHUNK):
                    @pl.when(n < count)
                    def _():
                        pltpu.make_async_copy(
                            blocks_hbm.at[leaf, 0], blocks.at[leaf, n], sems.at[leaf, n]
                        ).wait()
                total_ref[leaf] = total_ref[leaf] + (term(first) + term(first + 1))


def near_kernel(
    index_ref, blocks_hbm, own_ref, share_ref,
    near_ref,
    blocks, panels, order, block_sems, panel_sems,
):
    leaves, _, rows, _ = blocks.shape
    size = leaves * rows
    pairs = [
        pltpu.make_async_copy(
            ref.at[pl.ds(0, size)], panels.at[pl.ds(which * size, size)], panel_sems.at[which]
        )
        for which, ref in enumerate((own_ref, share_ref))
    ]
    for copy in pairs:
        copy.start()
    found = pick_slots(index_ref, blocks_hbm, blocks, block_sems, order, 0, 2 * leaves)
    near_ref[...] = jnp.zeros(near_ref.shape, near_ref.dtype)
    panels[pl.ds(2 * size, rows), :] = jnp.zeros((rows, panels.shape[1]), panels.dtype)
    for copy in pairs:
        copy.wait()
    add_slots(near_ref, blocks_hbm, blocks, block_sems, order, found, panels)


def across_kernel(
    index_ref, blocks_hbm, near_ref, across_ref,
    total_ref,
    blocks, panels, order, block_sems, panel_sems,
):
    leaves, _, rows, _ = blocks.shape
    size = leaves * rows
    copy = pltpu.make_async_copy(across_ref, panels.at[pl.ds(0, size)], panel_sems.at[0])
    copy.start()
    found = pick_slots(
        index_ref, blocks_hbm, blocks, block_sems, order, 2 * leaves, 3 * leaves
    )
    total_ref[...] = near_ref[...]
    panels[pl.ds(size, rows), :] = jnp.zeros((rows, panels.shape[1]), panels.dtype)
    copy.wait()
    add_slots(total_ref, blocks_hbm, blocks, block_sems, order, found, panels)


def far_kernel(
    list_ref, coupling_ref, level_ref, layer_ref, share_ref, passed_ref,
    far_ref,
    coefs, sems,
):
    leaves, slots, rank, _ = coupling_ref.shape
    size = leaves * rank
    place = lax.axis_index("row")
    beyond = jnp.where((place & 2) == 0, place - 2, place + 2)
    copies = [
        pltpu.make_async_copy(
            ref.at[pl.ds(ref.shape[0] - size, size)], coefs.at[pl.ds(n * size, size)], sems.at[n]
        )
        for n, ref in enumerate((level_ref, layer_ref, share_ref, passed_ref))
    ]
    for copy in copies:
        copy.start()
    for copy in copies:
        copy.wait()

    def panel_of(leaf, slot):
        column = list_ref[leaf, slot]
        cluster = lax.div(column, leaves)
        which = jnp.where(
            cluster == (place ^ 2), 0,
            jnp.where(cluster == beyond, 1, jnp.where(cluster == (place ^ 1), 2, 3)),
        )
        return coefs[rows_at(which * leaves + column - cluster * leaves, rank), :]

    for leaf in range(leaves):
        total = None
        for slot in range(0, slots, 2):
            both = jnp.concatenate([coupling_ref[leaf, slot], coupling_ref[leaf, slot + 1]], axis=1)
            panels = jnp.concatenate([panel_of(leaf, slot), panel_of(leaf, slot + 1)], axis=0)
            term = dot(both, panels)
            total = term if total is None else total + term
        far_ref[pl.ds(leaf * rank, rank), :] = total


def down_kernel(
    list_ref, transfer_ref, coupling_ref, row_ref, near_ref, far_ref,
    column_ref, beside_ref, their_column_ref, their_beside_ref,
    out_hbm,
    out, sems,
):
    leaves, rows, rank = row_ref.shape
    local = lax.axis_index("row") & (GROUP - 1)
    unused, their_unused = unused_layer(local), unused_layer(local ^ 1)

    def panel_of(slot):
        flip = (list_ref[0, slot] & (GROUP - 1)) ^ local
        layer = flip >> 2

        def beside(ref, gap):
            index = jnp.minimum(jnp.where(layer > gap, layer - 1, layer), GROUP // 4 - 2)
            return ref[rows_at(index, rank), :]

        where = rows_at(layer, rank)
        same = (flip & 2) == 0
        mine = jnp.where(same, column_ref[where, :], beside(beside_ref, unused))
        theirs = jnp.where(
            same, their_column_ref[where, :], beside(their_beside_ref, their_unused)
        )
        return jnp.where((flip & 1) == 0, mine, theirs)

    terms = []
    for slot in range(0, list_ref.shape[1], 2):
        both = jnp.concatenate([coupling_ref[0, slot], coupling_ref[0, slot + 1]], axis=1)
        terms.append(dot(both, jnp.concatenate([panel_of(slot), panel_of(slot + 1)], axis=0)))
    while len(terms) > 1:
        terms = [first + second for first, second in zip(terms[::2], terms[1::2])]
    high = terms[0].astype(jnp.bfloat16)
    low = (terms[0] - high.astype(jnp.float32)).astype(jnp.bfloat16)
    matrix = transfer_ref[...].reshape(leaves * rank, rank)
    spread = dot(
        jnp.concatenate([matrix, matrix], axis=1), jnp.concatenate([high, low], axis=0)
    )
    down = (far_ref[...] + spread).astype(jnp.bfloat16)
    copies = []
    for leaf in range(leaves):
        result = near_ref[leaf] + dot(row_ref[leaf], down[leaf * rank:(leaf + 1) * rank])
        here = pl.ds(leaf * rows, rows)
        out[here, :] = result.astype(jnp.bfloat16)
        copies.append(pltpu.make_async_copy(out.at[here], out_hbm.at[here], sems.at[leaf]))
        copies[-1].start()
    for copy in copies:
        copy.wait()


def call(kernel, name, outs, specs, args, scratch=(), flops=0, moved=0, limit=4, to=VMEM):
    many = isinstance(outs, tuple)
    return pl.pallas_call(
        kernel,
        out_shape=outs,
        in_specs=specs,
        out_specs=(to,) * len(outs) if many else to,
        scratch_shapes=list(scratch),
        cost_estimate=pl.CostEstimate(flops=flops, bytes_accessed=moved, transcendentals=0),
        compiler_params=pltpu.CompilerParams(vmem_limit_bytes=limit * MIB),
        name=name,
    )(*args)


def body(
    source,
    near_blocks,
    near_list,
    near_count,
    col_basis,
    row_basis,
    transfer,
    far_list,
    far_coupling,
    coarse_list,
    coarse_coupling,
):
    leaves, slots, rows, _ = near_blocks.shape
    rank = col_basis.shape[2]
    width = source.shape[1]
    count = lax.axis_size("row")
    far_slots = far_coupling.shape[1]

    def send(value, target):
        pairs = [(d, target(d)) for d in range(count) if 0 <= target(d) < count]
        return lax.ppermute(value, "row", pairs)

    def panel(blocks, dtype=jnp.bfloat16):
        return jax.ShapeDtypeStruct((blocks * rank, width), dtype)

    coef = call(
        coef_kernel, "coef", panel(leaves), [VMEM] * 2, (source, col_basis),
        flops=2 * leaves * rank * width * rows,
        moved=2 * leaves * rows * (width + rank), limit=8,
    )
    parent = call(parent_kernel, "parent", panel(1), [VMEM] * 2, (coef, transfer))
    layers = [send(parent, lambda d, bit=bit: d ^ bit) for bit in (4, 8, 12)]
    source_other = send(source, lambda d: d ^ 1)
    level = send(coef, lambda d: d ^ 2)
    panels = call(
        hand_kernel, "panels", jax.ShapeDtypeStruct(source.shape, jnp.bfloat16), [VMEM] + [ANY] * 1,
        (source, source_other),
    )
    across = send(panels, lambda d: d + 1 if d & 1 else d - 1)

    place = lax.axis_index("row")
    live = lax.broadcasted_iota(jnp.int32, (leaves, slots), 1) < near_count[:, None]
    which = jnp.minimum((near_list // leaves) ^ place, 2)
    index = jnp.where(live, which * leaves + near_list % leaves, 3 * leaves)
    def slots_scratch(panels):
        return [
            pltpu.VMEM(near_blocks.shape, jnp.bfloat16),
            pltpu.VMEM((panels * rows, width), jnp.bfloat16),
            pltpu.SMEM((leaves, slots + CHUNK), jnp.int32),
            pltpu.SemaphoreType.DMA((leaves, slots)),
            pltpu.SemaphoreType.DMA((2,)),
        ]

    shape = jax.ShapeDtypeStruct((leaves, rows, width), jnp.float32)
    near = call(
        near_kernel, "near", shape, [SMEM] + [ANY] * 3,
        (index, near_blocks, panels, source_other),
        scratch=slots_scratch(2 * leaves + 1), flops=10**9, limit=48,
    )
    layer = send(level, lambda d: d - 4 if d & 2 else d + 4)
    column, sent = call(
        column_kernel, "column", (panel(GROUP // 4 + leaves), panel(GROUP // 4 - 1)),
        [VMEM] * 5 + [ANY], (parent, *layers, coef, near),
    )
    beside = send(sent, lambda d: d ^ 2)
    their_column = send(column, lambda d: d ^ 1)
    near = call(
        across_kernel, "across", shape, [SMEM, ANY, VMEM, ANY],
        (index, near_blocks, near, across),
        scratch=slots_scratch(leaves + 1), flops=0, limit=48,
    )
    picked_coef = call(
        pick_kernel, "pick", panel(leaves), [VMEM] * 2, (level, layer)
    )
    passed = send(picked_coef, lambda d: d ^ 1)
    far = call(
        far_kernel, "far", panel(leaves, jnp.float32), [SMEM, VMEM] + [ANY] * 4,
        (far_list, far_coupling, level, layer, their_column, passed),
        scratch=[
            pltpu.VMEM((4 * leaves * rank, width), jnp.bfloat16),
            pltpu.SemaphoreType.DMA((4,)),
        ],
        flops=2 * leaves * far_slots * rank * rank * width,
        moved=2 * leaves * far_slots * rank * rank, limit=10,
    )
    handed = call(hand_kernel, "hand", panel(GROUP // 4 - 1), [VMEM, ANY], (beside, near))
    their_beside = send(handed, lambda d: d ^ 1)
    return call(
        down_kernel, "down", jax.ShapeDtypeStruct(source.shape, jnp.bfloat16),
        [SMEM] + [VMEM] * 9,
        (
            coarse_list, transfer, coarse_coupling, row_basis, near, far,
            column, handed, their_column, their_beside,
        ),
        flops=8 * leaves * rank * rank * width,
        scratch=[
            pltpu.VMEM(source.shape, jnp.bfloat16),
            pltpu.SemaphoreType.DMA((leaves,)),
        ],
        moved=4 * leaves * rows * width, limit=8, to=ANY,
    )


def solution(mesh):
    placed = (
        P(("clip", "row"), None),
        P(("clip", "row"), None, None, None),
        P(("clip", "row"), None),
        P(("clip", "row")),
        P(("clip", "row"), None, None),
        P(("clip", "row"), None, None),
        P(("clip", "row"), None, None),
        P(("clip", "row"), None),
        P(("clip", "row"), None, None, None),
        P(("clip", "row"), None),
        P(("clip", "row"), None, None, None),
    )
    return jax.shard_map(
        body, mesh=mesh, in_specs=placed, out_specs=P(("clip", "row"), None), check_vma=False
    )
```

```python
import jax
import jax.numpy as jnp
from jax import lax
from jax.experimental import pallas as pl
from jax.experimental.pallas import tpu as pltpu
from jax.sharding import PartitionSpec as P

GROUP = 16
CHUNK = 2
MIB = 2**20

VMEM = pl.BlockSpec(memory_space=pltpu.VMEM)
SMEM = pl.BlockSpec(memory_space=pltpu.SMEM)
ANY = pl.BlockSpec(memory_space=pl.ANY)


def dot(a, b):
    return jnp.dot(a, b, preferred_element_type=jnp.float32)


def dot_t(a, b):
    return lax.dot_general(
        a, b, (((0,), (0,)), ((), ())), preferred_element_type=jnp.float32
    )


def rows_at(index, rows):
    return pl.ds(pl.multiple_of(index * rows, rows), rows)


def coef_kernel(source_ref, col_ref, own_ref, coef_ref):
    leaves, rows, rank = col_ref.shape
    for leaf in range(leaves):
        panel = source_ref[pl.ds(leaf * rows, rows), :]
        own_ref[pl.ds(leaf * rows, rows), :] = panel
        coef_ref[pl.ds(leaf * rank, rank), :] = dot_t(col_ref[leaf], panel).astype(jnp.bfloat16)


def parent_kernel(coef_ref, transfer_ref, parent_ref):
    leaves, rank, _ = transfer_ref.shape
    total = None
    for leaf in range(leaves):
        term = dot_t(transfer_ref[leaf], coef_ref[pl.ds(leaf * rank, rank), :])
        total = term if total is None else total + term
    parent_ref[...] = total.astype(jnp.bfloat16)


def unused_layer(place):
    layer = (place >> 2) & 3
    corner = place & 3
    below = ((layer + 3) & 3) ^ layer
    above = ((layer + 1) & 3) ^ layer
    return jnp.where(corner == 1, below, jnp.where(corner == 2, above, 0))


def column_kernel(own_ref, first_ref, second_ref, third_ref, coef_ref, _, column_ref, sent_ref):
    rank = own_ref.shape[0]
    for n, ref in enumerate((own_ref, first_ref, second_ref, third_ref)):
        column_ref[pl.ds(n * rank, rank), :] = ref[...]
    column_ref[pl.ds(4 * rank, coef_ref.shape[0]), :] = coef_ref[...]
    unused = unused_layer(lax.axis_index("row") ^ 2)
    for n in range(GROUP // 4 - 1):
        index = jnp.where(n < unused, n, n + 1)
        sent_ref[pl.ds(n * rank, rank), :] = column_ref[rows_at(index, rank), :]


def pick_kernel(level_ref, layer_ref, out_ref):
    corner = lax.axis_index("row") & 3
    level = (corner == 0) | (corner == 3)
    out_ref[...] = jnp.where(level, level_ref[...], layer_ref[...])


def hand_kernel(in_ref, *refs):
    out_ref = refs[-1]
    out_ref[...] = in_ref[pl.ds(0, out_ref.shape[0]), :]


def pick_slots(index_ref, blocks_hbm, blocks, sems, order_ref, low, high):
    leaves, slots, rows, _ = blocks.shape

    def picker(leaf):
        def step(slot, found):
            panel = index_ref[leaf, slot]
            kept = (panel >= low) & (panel < high)

            @pl.when(kept)
            def _():
                order_ref[leaf, found] = panel - low
                pltpu.make_async_copy(
                    blocks_hbm.at[leaf, slot], blocks.at[leaf, found], sems.at[leaf, found]
                ).start()

            return found + kept.astype(jnp.int32)

        return step

    found = [lax.fori_loop(0, slots, picker(leaf), 0) for leaf in range(leaves)]
    for leaf in range(leaves):
        for pad in range(CHUNK):
            order_ref[leaf, found[leaf] + pad] = high - low
    return found


def add_slots(total_ref, blocks_hbm, blocks, sems, order_ref, found, panels):
    leaves, slots, rows, _ = blocks.shape
    for leaf in range(leaves):
        count = found[leaf]

        def term(n):
            block = blocks[leaf, jnp.where(n < count, n, 0)]
            return dot(block, panels[rows_at(order_ref[leaf, n], rows), :])

        for first in range(0, slots, CHUNK):
            @pl.when(first < count)
            def _():
                for n in range(first, first + CHUNK):
                    @pl.when(n < count)
                    def _():
                        pltpu.make_async_copy(
                            blocks_hbm.at[leaf, 0], blocks.at[leaf, n], sems.at[leaf, n]
                        ).wait()
                total_ref[leaf] = total_ref[leaf] + (term(first) + term(first + 1))


def near_kernel(
    index_ref, blocks_hbm, own_ref, share_ref,
    near_ref,
    blocks, panels, order, block_sems, panel_sems,
):
    leaves, _, rows, _ = blocks.shape
    size = leaves * rows
    pairs = [
        pltpu.make_async_copy(
            ref.at[pl.ds(0, size)], panels.at[pl.ds(which * size, size)], panel_sems.at[which]
        )
        for which, ref in enumerate((own_ref, share_ref))
    ]
    for copy in pairs:
        copy.start()
    found = pick_slots(index_ref, blocks_hbm, blocks, block_sems, order, 0, 2 * leaves)
    near_ref[...] = jnp.zeros(near_ref.shape, near_ref.dtype)
    panels[pl.ds(2 * size, rows), :] = jnp.zeros((rows, panels.shape[1]), panels.dtype)
    for copy in pairs:
        copy.wait()
    add_slots(near_ref, blocks_hbm, blocks, block_sems, order, found, panels)


def across_kernel(
    index_ref, blocks_hbm, near_ref, across_ref,
    total_ref,
    blocks, panels, order, block_sems, panel_sems,
):
    leaves, _, rows, _ = blocks.shape
    size = leaves * rows
    copy = pltpu.make_async_copy(across_ref, panels.at[pl.ds(0, size)], panel_sems.at[0])
    copy.start()
    found = pick_slots(
        index_ref, blocks_hbm, blocks, block_sems, order, 2 * leaves, 3 * leaves
    )
    total_ref[...] = near_ref[...]
    panels[pl.ds(size, rows), :] = jnp.zeros((rows, panels.shape[1]), panels.dtype)
    copy.wait()
    add_slots(total_ref, blocks_hbm, blocks, block_sems, order, found, panels)


def far_kernel(
    list_ref, coupling_ref, level_ref, layer_ref, share_ref, passed_ref,
    far_ref,
    coefs, sems,
):
    leaves, slots, rank, _ = coupling_ref.shape
    size = leaves * rank
    place = lax.axis_index("row")
    beyond = jnp.where((place & 2) == 0, place - 2, place + 2)
    copies = [
        pltpu.make_async_copy(
            ref.at[pl.ds(ref.shape[0] - size, size)], coefs.at[pl.ds(n * size, size)], sems.at[n]
        )
        for n, ref in enumerate((level_ref, layer_ref, share_ref, passed_ref))
    ]
    for copy in copies:
        copy.start()
    for copy in copies:
        copy.wait()

    def panel_of(leaf, slot):
        column = list_ref[leaf, slot]
        cluster = lax.div(column, leaves)
        which = jnp.where(
            cluster == (place ^ 2), 0,
            jnp.where(cluster == beyond, 1, jnp.where(cluster == (place ^ 1), 2, 3)),
        )
        return coefs[rows_at(which * leaves + column - cluster * leaves, rank), :]

    for leaf in range(leaves):
        total = None
        for slot in range(0, slots, 2):
            both = jnp.concatenate([coupling_ref[leaf, slot], coupling_ref[leaf, slot + 1]], axis=1)
            panels = jnp.concatenate([panel_of(leaf, slot), panel_of(leaf, slot + 1)], axis=0)
            term = dot(both, panels)
            total = term if total is None else total + term
        far_ref[pl.ds(leaf * rank, rank), :] = total


def down_kernel(
    list_ref, transfer_ref, coupling_ref, row_ref, near_ref, far_ref,
    column_ref, beside_ref, their_column_ref, their_beside_ref,
    out_hbm,
    out, sems,
):
    leaves, rows, rank = row_ref.shape
    local = lax.axis_index("row") & (GROUP - 1)
    unused, their_unused = unused_layer(local), unused_layer(local ^ 1)

    def panel_of(slot):
        flip = (list_ref[0, slot] & (GROUP - 1)) ^ local
        layer = flip >> 2

        def beside(ref, gap):
            index = jnp.minimum(jnp.where(layer > gap, layer - 1, layer), GROUP // 4 - 2)
            return ref[rows_at(index, rank), :]

        where = rows_at(layer, rank)
        same = (flip & 2) == 0
        mine = jnp.where(same, column_ref[where, :], beside(beside_ref, unused))
        theirs = jnp.where(
            same, their_column_ref[where, :], beside(their_beside_ref, their_unused)
        )
        return jnp.where((flip & 1) == 0, mine, theirs)

    terms = []
    for slot in range(0, list_ref.shape[1], 2):
        both = jnp.concatenate([coupling_ref[0, slot], coupling_ref[0, slot + 1]], axis=1)
        terms.append(dot(both, jnp.concatenate([panel_of(slot), panel_of(slot + 1)], axis=0)))
    while len(terms) > 1:
        terms = [first + second for first, second in zip(terms[::2], terms[1::2])]
    high = terms[0].astype(jnp.bfloat16)
    low = (terms[0] - high.astype(jnp.float32)).astype(jnp.bfloat16)
    matrix = transfer_ref[...].reshape(leaves * rank, rank)
    spread = dot(
        jnp.concatenate([matrix, matrix], axis=1), jnp.concatenate([high, low], axis=0)
    )
    down = (far_ref[...] + spread).astype(jnp.bfloat16)
    copies = []
    for leaf in range(leaves):
        result = near_ref[leaf] + dot(row_ref[leaf], down[leaf * rank:(leaf + 1) * rank])
        here = pl.ds(leaf * rows, rows)
        out[here, :] = result.astype(jnp.bfloat16)
        copies.append(pltpu.make_async_copy(out.at[here], out_hbm.at[here], sems.at[leaf]))
        copies[-1].start()
    for copy in copies:
        copy.wait()


def call(kernel, name, outs, specs, args, scratch=(), flops=0, moved=0, limit=4, to=VMEM):
    many = isinstance(outs, tuple)
    return pl.pallas_call(
        kernel,
        out_shape=outs,
        in_specs=specs,
        out_specs=(to,) * len(outs) if many else to,
        scratch_shapes=list(scratch),
        cost_estimate=pl.CostEstimate(flops=flops, bytes_accessed=moved, transcendentals=0),
        compiler_params=pltpu.CompilerParams(vmem_limit_bytes=limit * MIB),
        name=name,
    )(*args)


def body(
    source,
    near_blocks,
    near_list,
    near_count,
    col_basis,
    row_basis,
    transfer,
    far_list,
    far_coupling,
    coarse_list,
    coarse_coupling,
):
    leaves, slots, rows, _ = near_blocks.shape
    rank = col_basis.shape[2]
    width = source.shape[1]
    count = lax.axis_size("row")
    far_slots = far_coupling.shape[1]

    def send(value, target):
        pairs = [(d, target(d)) for d in range(count) if 0 <= target(d) < count]
        return lax.ppermute(value, "row", pairs)

    def panel(blocks, dtype=jnp.bfloat16):
        return jax.ShapeDtypeStruct((blocks * rank, width), dtype)

    own, coef = call(
        coef_kernel, "coef",
        (jax.ShapeDtypeStruct(source.shape, jnp.bfloat16), panel(leaves)),
        [VMEM] * 2, (source, col_basis),
        flops=2 * leaves * rank * width * rows,
        moved=2 * leaves * rows * (width + rank), limit=8,
    )
    parent = call(parent_kernel, "parent", panel(1), [VMEM] * 2, (coef, transfer))
    layers = [send(parent, lambda d, bit=bit: d ^ bit) for bit in (4, 8, 12)]
    source_other = send(source, lambda d: d ^ 1)
    level = send(coef, lambda d: d ^ 2)
    panels = call(
        hand_kernel, "panels", jax.ShapeDtypeStruct(source.shape, jnp.bfloat16), [VMEM] + [ANY] * 1,
        (own, source_other),
    )
    across = send(panels, lambda d: d + 1 if d & 1 else d - 1)

    place = lax.axis_index("row")
    live = lax.broadcasted_iota(jnp.int32, (leaves, slots), 1) < near_count[:, None]
    which = jnp.minimum((near_list // leaves) ^ place, 2)
    index = jnp.where(live, which * leaves + near_list % leaves, 3 * leaves)
    def slots_scratch(panels):
        return [
            pltpu.VMEM(near_blocks.shape, jnp.bfloat16),
            pltpu.VMEM((panels * rows, width), jnp.bfloat16),
            pltpu.SMEM((leaves, slots + CHUNK), jnp.int32),
            pltpu.SemaphoreType.DMA((leaves, slots)),
            pltpu.SemaphoreType.DMA((2,)),
        ]

    shape = jax.ShapeDtypeStruct((leaves, rows, width), jnp.float32)
    near = call(
        near_kernel, "near", shape, [SMEM] + [ANY] * 3,
        (index, near_blocks, panels, source_other),
        scratch=slots_scratch(2 * leaves + 1), flops=10**9, limit=48,
    )
    layer = send(level, lambda d: d - 4 if d & 2 else d + 4)
    column, sent = call(
        column_kernel, "column", (panel(GROUP // 4 + leaves), panel(GROUP // 4 - 1)),
        [VMEM] * 5 + [ANY], (parent, *layers, coef, near),
    )
    beside = send(sent, lambda d: d ^ 2)
    their_column = send(column, lambda d: d ^ 1)
    near = call(
        across_kernel, "across", shape, [SMEM, ANY, VMEM, ANY],
        (index, near_blocks, near, across),
        scratch=slots_scratch(leaves + 1), flops=0, limit=48,
    )
    picked_coef = call(
        pick_kernel, "pick", panel(leaves), [VMEM] * 2, (level, layer)
    )
    passed = send(picked_coef, lambda d: d ^ 1)
    far = call(
        far_kernel, "far", panel(leaves, jnp.float32), [SMEM, VMEM] + [ANY] * 4,
        (far_list, far_coupling, level, layer, their_column, passed),
        scratch=[
            pltpu.VMEM((4 * leaves * rank, width), jnp.bfloat16),
            pltpu.SemaphoreType.DMA((4,)),
        ],
        flops=2 * leaves * far_slots * rank * rank * width,
        moved=2 * leaves * far_slots * rank * rank, limit=10,
    )
    handed = call(hand_kernel, "hand", panel(GROUP // 4 - 1), [VMEM, ANY], (beside, near))
    their_beside = send(handed, lambda d: d ^ 1)
    return call(
        down_kernel, "down", jax.ShapeDtypeStruct(source.shape, jnp.bfloat16),
        [SMEM] + [VMEM] * 9,
        (
            coarse_list, transfer, coarse_coupling, row_basis, near, far,
            column, handed, their_column, their_beside,
        ),
        flops=8 * leaves * rank * rank * width,
        scratch=[
            pltpu.VMEM(source.shape, jnp.bfloat16),
            pltpu.SemaphoreType.DMA((leaves,)),
        ],
        moved=4 * leaves * rows * width, limit=8, to=ANY,
    )


def solution(mesh):
    placed = (
        P(("clip", "row"), None),
        P(("clip", "row"), None, None, None),
        P(("clip", "row"), None),
        P(("clip", "row")),
        P(("clip", "row"), None, None),
        P(("clip", "row"), None, None),
        P(("clip", "row"), None, None),
        P(("clip", "row"), None),
        P(("clip", "row"), None, None, None),
        P(("clip", "row"), None),
        P(("clip", "row"), None, None, None),
    )
    return jax.shard_map(
        body, mesh=mesh, in_specs=placed, out_specs=P(("clip", "row"), None), check_vma=False
    )
```

```python
import jax
import jax.numpy as jnp
from jax import lax
from jax.experimental import pallas as pl
from jax.experimental.pallas import tpu as pltpu
from jax.sharding import PartitionSpec as P

GROUP = 16
CHUNK = 2
MIB = 2**20

VMEM = pl.BlockSpec(memory_space=pltpu.VMEM)
SMEM = pl.BlockSpec(memory_space=pltpu.SMEM)
ANY = pl.BlockSpec(memory_space=pl.ANY)


def dot(a, b):
    return jnp.dot(a, b, preferred_element_type=jnp.float32)


def dot_t(a, b):
    return lax.dot_general(
        a, b, (((0,), (0,)), ((), ())), preferred_element_type=jnp.float32
    )


def rows_at(index, rows):
    return pl.ds(pl.multiple_of(index * rows, rows), rows)


def coef_kernel(source_ref, col_ref, share_ref, coef_ref):
    leaves, rows, rank = col_ref.shape
    for leaf in range(leaves):
        panel = source_ref[pl.ds(leaf * rows, rows), :]
        share_ref[pl.ds(leaf * rows, rows), :] = panel
        coef = dot_t(col_ref[leaf], panel).astype(jnp.bfloat16)
        coef_ref[pl.ds(leaf * rank, rank), :] = coef
        share_ref[pl.ds(leaves * rows + leaf * rank, rank), :] = coef


def parent_kernel(coef_ref, transfer_ref, parent_ref):
    leaves, rank, _ = transfer_ref.shape
    total = None
    for leaf in range(leaves):
        term = dot_t(transfer_ref[leaf], coef_ref[pl.ds(leaf * rank, rank), :])
        total = term if total is None else total + term
    parent_ref[...] = total.astype(jnp.bfloat16)


def unused_layer(place):
    layer = (place >> 2) & 3
    corner = place & 3
    below = ((layer + 3) & 3) ^ layer
    above = ((layer + 1) & 3) ^ layer
    return jnp.where(corner == 1, below, jnp.where(corner == 2, above, 0))


def column_kernel(own_ref, first_ref, second_ref, third_ref, _, column_ref, sent_ref):
    rank = own_ref.shape[0]
    for n, ref in enumerate((own_ref, first_ref, second_ref, third_ref)):
        column_ref[pl.ds(n * rank, rank), :] = ref[...]
    unused = unused_layer(lax.axis_index("row") ^ 2)
    for n in range(GROUP // 4 - 1):
        index = jnp.where(n < unused, n, n + 1)
        sent_ref[pl.ds(n * rank, rank), :] = column_ref[rows_at(index, rank), :]


def pick_kernel(level_ref, layer_ref, out_ref):
    corner = lax.axis_index("row") & 3
    level = (corner == 0) | (corner == 3)
    out_ref[...] = jnp.where(level, level_ref[...], layer_ref[...])


def hand_kernel(in_ref, *refs):
    out_ref = refs[-1]
    out_ref[...] = in_ref[pl.ds(0, out_ref.shape[0]), :]


def pick_slots(index_ref, blocks_hbm, blocks, sems, order_ref, low, high):
    leaves, slots, rows, _ = blocks.shape

    def picker(leaf):
        def step(slot, found):
            panel = index_ref[leaf, slot]
            kept = (panel >= low) & (panel < high)

            @pl.when(kept)
            def _():
                order_ref[leaf, found] = panel - low
                pltpu.make_async_copy(
                    blocks_hbm.at[leaf, slot], blocks.at[leaf, found], sems.at[leaf, found]
                ).start()

            return found + kept.astype(jnp.int32)

        return step

    found = [lax.fori_loop(0, slots, picker(leaf), 0) for leaf in range(leaves)]
    for leaf in range(leaves):
        for pad in range(CHUNK):
            order_ref[leaf, found[leaf] + pad] = high - low
    return found


def add_slots(total_ref, blocks_hbm, blocks, sems, order_ref, found, panels):
    leaves, slots, rows, _ = blocks.shape
    for leaf in range(leaves):
        count = found[leaf]

        def term(n):
            block = blocks[leaf, jnp.where(n < count, n, 0)]
            return dot(block, panels[rows_at(order_ref[leaf, n], rows), :])

        for first in range(0, slots, CHUNK):
            @pl.when(first < count)
            def _():
                for n in range(first, first + CHUNK):
                    @pl.when(n < count)
                    def _():
                        pltpu.make_async_copy(
                            blocks_hbm.at[leaf, 0], blocks.at[leaf, n], sems.at[leaf, n]
                        ).wait()
                total_ref[leaf] = total_ref[leaf] + (term(first) + term(first + 1))


def near_kernel(
    index_ref, blocks_hbm, own_ref, share_ref,
    near_ref,
    blocks, panels, order, block_sems, panel_sems,
):
    leaves, _, rows, _ = blocks.shape
    size = leaves * rows
    pairs = [
        pltpu.make_async_copy(
            ref.at[pl.ds(0, size)], panels.at[pl.ds(which * size, size)], panel_sems.at[which]
        )
        for which, ref in enumerate((own_ref, share_ref))
    ]
    for copy in pairs:
        copy.start()
    found = pick_slots(index_ref, blocks_hbm, blocks, block_sems, order, 0, 2 * leaves)
    near_ref[...] = jnp.zeros(near_ref.shape, near_ref.dtype)
    panels[pl.ds(2 * size, rows), :] = jnp.zeros((rows, panels.shape[1]), panels.dtype)
    for copy in pairs:
        copy.wait()
    add_slots(near_ref, blocks_hbm, blocks, block_sems, order, found, panels)


def across_kernel(
    index_ref, blocks_hbm, near_ref, across_ref,
    total_ref,
    blocks, panels, order, block_sems, panel_sems,
):
    leaves, _, rows, _ = blocks.shape
    size = leaves * rows
    copy = pltpu.make_async_copy(across_ref, panels.at[pl.ds(0, size)], panel_sems.at[0])
    copy.start()
    found = pick_slots(
        index_ref, blocks_hbm, blocks, block_sems, order, 2 * leaves, 3 * leaves
    )
    total_ref[...] = near_ref[...]
    panels[pl.ds(size, rows), :] = jnp.zeros((rows, panels.shape[1]), panels.dtype)
    copy.wait()
    add_slots(total_ref, blocks_hbm, blocks, block_sems, order, found, panels)


def far_kernel(
    list_ref, coarse_list_ref, coupling_ref, coarse_coupling_ref,
    level_ref, layer_ref, share_ref, passed_ref, column_ref, beside_ref, their_column_ref,
    far_ref, coarse_ref, weight_ref,
    coefs, sems,
):
    leaves, slots, rank, _ = coupling_ref.shape
    size = leaves * rank
    place = lax.axis_index("row")
    beyond = jnp.where((place & 2) == 0, place - 2, place + 2)
    copies = [
        pltpu.make_async_copy(
            ref.at[pl.ds(ref.shape[0] - size, size)], coefs.at[pl.ds(n * size, size)], sems.at[n]
        )
        for n, ref in enumerate((level_ref, layer_ref, share_ref, passed_ref))
    ]
    for copy in copies:
        copy.start()
    local = place & (GROUP - 1)
    unused, their_unused = unused_layer(local), unused_layer(local ^ 1)
    weights = [jnp.zeros((rank, rank), jnp.float32)] * (GROUP // 4 - 1)
    terms = []
    for slot in range(coarse_list_ref.shape[1]):
        flip = (coarse_list_ref[0, slot] & (GROUP - 1)) ^ local
        layer = flip >> 2
        late = (flip & 3) == 3

        def gap(skipped):
            return jnp.minimum(jnp.where(layer > skipped, layer - 1, layer), GROUP // 4 - 2)

        here = rows_at(layer, rank)
        mine = jnp.where(
            (flip & 2) == 0, column_ref[here, :], beside_ref[rows_at(gap(unused), rank), :]
        )
        panel = jnp.where((flip & 1) == 0, mine, their_column_ref[here, :])
        block = coarse_coupling_ref[0, slot]
        terms.append(dot(block, jnp.where(late, jnp.zeros_like(panel), panel)))
        wide = block.astype(jnp.float32)
        weights = [
            total + jnp.where(late & (gap(their_unused) == n), wide, jnp.zeros_like(wide))
            for n, total in enumerate(weights)
        ]
    while len(terms) > 1:
        terms = [first + second for first, second in zip(terms[::2], terms[1::2])]
    coarse_ref[...] = terms[0]
    for n, total in enumerate(weights):
        high = total.astype(jnp.bfloat16)
        weight_ref[:, pl.ds(2 * n * rank, rank)] = high
        weight_ref[:, pl.ds((2 * n + 1) * rank, rank)] = (
            total - high.astype(jnp.float32)
        ).astype(jnp.bfloat16)
    for copy in copies:
        copy.wait()

    def panel_of(leaf, slot):
        column = list_ref[leaf, slot]
        cluster = lax.div(column, leaves)
        which = jnp.where(
            cluster == (place ^ 2), 0,
            jnp.where(cluster == beyond, 1, jnp.where(cluster == (place ^ 1), 2, 3)),
        )
        return coefs[rows_at(which * leaves + column - cluster * leaves, rank), :]

    for leaf in range(leaves):
        total = None
        for slot in range(0, slots, 2):
            both = jnp.concatenate([coupling_ref[leaf, slot], coupling_ref[leaf, slot + 1]], axis=1)
            panels = jnp.concatenate([panel_of(leaf, slot), panel_of(leaf, slot + 1)], axis=0)
            term = dot(both, panels)
            total = term if total is None else total + term
        far_ref[pl.ds(leaf * rank, rank), :] = total


def down_kernel(
    transfer_ref, row_ref, near_ref, far_ref, coarse_ref, weight_ref, their_beside_ref,
    out_hbm,
    out, sems,
):
    leaves, rows, rank = row_ref.shape
    panels = [their_beside_ref[pl.ds(n * rank, rank), :] for n in range(GROUP // 4 - 1)]
    stack = jnp.concatenate([panel for panel in panels for _ in range(2)], axis=0)
    coarse = coarse_ref[...] + dot(weight_ref[...], stack)
    high = coarse.astype(jnp.bfloat16)
    low = (coarse - high.astype(jnp.float32)).astype(jnp.bfloat16)
    matrix = transfer_ref[...].reshape(leaves * rank, rank)
    spread = dot(
        jnp.concatenate([matrix, matrix], axis=1), jnp.concatenate([high, low], axis=0)
    )
    down = (far_ref[...] + spread).astype(jnp.bfloat16)
    copies = []
    for leaf in range(leaves):
        result = near_ref[leaf] + dot(row_ref[leaf], down[leaf * rank:(leaf + 1) * rank])
        here = pl.ds(leaf * rows, rows)
        out[here, :] = result.astype(jnp.bfloat16)
        copies.append(pltpu.make_async_copy(out.at[here], out_hbm.at[here], sems.at[leaf]))
        copies[-1].start()
    for copy in copies:
        copy.wait()


def call(kernel, name, outs, specs, args, scratch=(), flops=0, moved=0, limit=4, to=VMEM):
    many = isinstance(outs, tuple)
    return pl.pallas_call(
        kernel,
        out_shape=outs,
        in_specs=specs,
        out_specs=(to,) * len(outs) if many else to,
        scratch_shapes=list(scratch),
        cost_estimate=pl.CostEstimate(flops=flops, bytes_accessed=moved, transcendentals=0),
        compiler_params=pltpu.CompilerParams(vmem_limit_bytes=limit * MIB),
        name=name,
    )(*args)


def body(
    source,
    near_blocks,
    near_list,
    near_count,
    col_basis,
    row_basis,
    transfer,
    far_list,
    far_coupling,
    coarse_list,
    coarse_coupling,
):
    leaves, slots, rows, _ = near_blocks.shape
    rank = col_basis.shape[2]
    width = source.shape[1]
    count = lax.axis_size("row")
    far_slots = far_coupling.shape[1]

    def send(value, target):
        pairs = [(d, target(d)) for d in range(count) if 0 <= target(d) < count]
        return lax.ppermute(value, "row", pairs)

    def panel(blocks, dtype=jnp.bfloat16):
        return jax.ShapeDtypeStruct((blocks * rank, width), dtype)

    share, coef = call(
        coef_kernel, "coef",
        (jax.ShapeDtypeStruct((leaves * (rows + rank), width), jnp.bfloat16), panel(leaves)),
        [VMEM] * 2, (source, col_basis), flops=2 * leaves * rank * width * rows,
        moved=2 * leaves * rows * (width + rank), limit=8,
    )
    parent = call(parent_kernel, "parent", panel(1), [VMEM] * 2, (coef, transfer))
    layers = [send(parent, lambda d, bit=bit: d ^ bit) for bit in (4, 8, 12)]
    share_other = send(share, lambda d: d ^ 1)
    level = send(coef, lambda d: d ^ 2)
    panels = call(
        hand_kernel, "panels", jax.ShapeDtypeStruct(source.shape, jnp.bfloat16), [VMEM] + [ANY] * 1,
        (share, share_other),
    )
    across = send(panels, lambda d: d + 1 if d & 1 else d - 1)

    place = lax.axis_index("row")
    live = lax.broadcasted_iota(jnp.int32, (leaves, slots), 1) < near_count[:, None]
    which = jnp.minimum((near_list // leaves) ^ place, 2)
    index = jnp.where(live, which * leaves + near_list % leaves, 3 * leaves)
    def slots_scratch(panels):
        return [
            pltpu.VMEM(near_blocks.shape, jnp.bfloat16),
            pltpu.VMEM((panels * rows, width), jnp.bfloat16),
            pltpu.SMEM((leaves, slots + CHUNK), jnp.int32),
            pltpu.SemaphoreType.DMA((leaves, slots)),
            pltpu.SemaphoreType.DMA((2,)),
        ]

    shape = jax.ShapeDtypeStruct((leaves, rows, width), jnp.float32)
    near = call(
        near_kernel, "near", shape, [SMEM] + [ANY] * 3,
        (index, near_blocks, share, share_other),
        scratch=slots_scratch(2 * leaves + 1), flops=2*10**9, limit=48,
    )
    layer = send(level, lambda d: d - 4 if d & 2 else d + 4)
    column, sent = call(
        column_kernel, "column", (panel(GROUP // 4), panel(GROUP // 4 - 1)),
        [VMEM] * 4 + [ANY], (parent, *layers, near),
    )
    beside = send(sent, lambda d: d ^ 2)
    their_column = send(column, lambda d: d ^ 1)
    near = call(
        across_kernel, "across", shape, [SMEM, ANY, VMEM, ANY],
        (index, near_blocks, near, across),
        scratch=slots_scratch(leaves + 1), flops=0, limit=48,
    )
    picked_coef = call(
        pick_kernel, "pick", panel(leaves), [VMEM] * 2, (level, layer)
    )
    passed = send(picked_coef, lambda d: d ^ 1)
    handed = call(hand_kernel, "hand", panel(GROUP // 4 - 1), [VMEM, ANY], (beside, near))
    their_beside = send(handed, lambda d: d ^ 1)
    far, coarse, weight = call(
        far_kernel, "far",
        (
            panel(leaves, jnp.float32), panel(1, jnp.float32),
            jax.ShapeDtypeStruct((rank, 2 * (GROUP // 4 - 1) * rank), jnp.bfloat16),
        ),
        [SMEM] * 2 + [VMEM] * 2 + [ANY] * 4 + [VMEM] * 3,
        (
            far_list, coarse_list, far_coupling, coarse_coupling, level, layer, share_other,
            passed, column, handed, their_column,
        ),
        scratch=[
            pltpu.VMEM((4 * leaves * rank, width), jnp.bfloat16),
            pltpu.SemaphoreType.DMA((4,)),
        ],
        flops=2 * leaves * far_slots * rank * rank * width,
        moved=2 * leaves * far_slots * rank * rank, limit=10,
    )
    return call(
        down_kernel, "down", jax.ShapeDtypeStruct(source.shape, jnp.bfloat16),
        [VMEM] * 7, (transfer, row_basis, near, far, coarse, weight, their_beside),
        flops=8 * leaves * rank * rank * width,
        scratch=[
            pltpu.VMEM(source.shape, jnp.bfloat16),
            pltpu.SemaphoreType.DMA((leaves,)),
        ],
        moved=4 * leaves * rows * width, limit=8, to=ANY,
    )


def solution(mesh):
    placed = (
        P(("clip", "row"), None),
        P(("clip", "row"), None, None, None),
        P(("clip", "row"), None),
        P(("clip", "row")),
        P(("clip", "row"), None, None),
        P(("clip", "row"), None, None),
        P(("clip", "row"), None, None),
        P(("clip", "row"), None),
        P(("clip", "row"), None, None, None),
        P(("clip", "row"), None),
        P(("clip", "row"), None, None, None),
    )
    return jax.shard_map(
        body, mesh=mesh, in_specs=placed, out_specs=P(("clip", "row"), None), check_vma=False
    )
```

```python
import jax
import jax.numpy as jnp
from jax import lax
from jax.experimental import pallas as pl
from jax.experimental.pallas import tpu as pltpu
from jax.sharding import PartitionSpec as P

GROUP = 16
CHUNK = 2
MIB = 2**20

VMEM = pl.BlockSpec(memory_space=pltpu.VMEM)
SMEM = pl.BlockSpec(memory_space=pltpu.SMEM)
ANY = pl.BlockSpec(memory_space=pl.ANY)


def dot(a, b):
    return jnp.dot(a, b, preferred_element_type=jnp.float32)


def dot_t(a, b):
    return lax.dot_general(
        a, b, (((0,), (0,)), ((), ())), preferred_element_type=jnp.float32
    )


def rows_at(index, rows):
    return pl.ds(pl.multiple_of(index * rows, rows), rows)


def coef_kernel(source_ref, col_ref, own_ref, coef_ref):
    leaves, rows, rank = col_ref.shape
    for leaf in range(leaves):
        panel = source_ref[pl.ds(leaf * rows, rows), :]
        own_ref[pl.ds(leaf * rows, rows), :] = panel
        coef_ref[pl.ds(leaf * rank, rank), :] = dot_t(col_ref[leaf], panel).astype(jnp.bfloat16)


def parent_kernel(coef_ref, transfer_ref, parent_ref):
    leaves, rank, _ = transfer_ref.shape
    total = None
    for leaf in range(leaves):
        term = dot_t(transfer_ref[leaf], coef_ref[pl.ds(leaf * rank, rank), :])
        total = term if total is None else total + term
    parent_ref[...] = total.astype(jnp.bfloat16)


def unused_layer(place):
    layer = (place >> 2) & 3
    corner = place & 3
    below = ((layer + 3) & 3) ^ layer
    above = ((layer + 1) & 3) ^ layer
    return jnp.where(corner == 1, below, jnp.where(corner == 2, above, 0))


def column_kernel(own_ref, first_ref, second_ref, third_ref, coef_ref, _, column_ref, sent_ref):
    rank = own_ref.shape[0]
    for n, ref in enumerate((own_ref, first_ref, second_ref, third_ref)):
        column_ref[pl.ds(n * rank, rank), :] = ref[...]
    column_ref[pl.ds(4 * rank, coef_ref.shape[0]), :] = coef_ref[...]
    unused = unused_layer(lax.axis_index("row") ^ 2)
    for n in range(GROUP // 4 - 1):
        index = jnp.where(n < unused, n, n + 1)
        sent_ref[pl.ds(n * rank, rank), :] = column_ref[rows_at(index, rank), :]


def pick_kernel(level_ref, layer_ref, out_ref):
    corner = lax.axis_index("row") & 3
    level = (corner == 0) | (corner == 3)
    out_ref[...] = jnp.where(level, level_ref[...], layer_ref[...])


def hand_kernel(in_ref, *refs):
    out_ref = refs[-1]
    out_ref[...] = in_ref[pl.ds(0, out_ref.shape[0]), :]


def pick_slots(index_ref, blocks_hbm, blocks, sems, order_ref, low, high):
    leaves, slots, rows, _ = blocks.shape

    def picker(leaf):
        def step(slot, found):
            panel = index_ref[leaf, slot]
            kept = (panel >= low) & (panel < high)

            @pl.when(kept)
            def _():
                order_ref[leaf, found] = panel - low
                pltpu.make_async_copy(
                    blocks_hbm.at[leaf, slot], blocks.at[leaf, found], sems.at[leaf, found]
                ).start()

            return found + kept.astype(jnp.int32)

        return step

    found = [lax.fori_loop(0, slots, picker(leaf), 0) for leaf in range(leaves)]
    for leaf in range(leaves):
        for pad in range(CHUNK):
            order_ref[leaf, found[leaf] + pad] = high - low
    return found


def add_slots(total_ref, blocks_hbm, blocks, sems, order_ref, found, panels):
    leaves, slots, rows, _ = blocks.shape
    for leaf in range(leaves):
        count = found[leaf]

        def term(n):
            block = blocks[leaf, jnp.where(n < count, n, 0)]
            return dot(block, panels[rows_at(order_ref[leaf, n], rows), :])

        for first in range(0, slots, CHUNK):
            @pl.when(first < count)
            def _():
                for n in range(first, first + CHUNK):
                    @pl.when(n < count)
                    def _():
                        pltpu.make_async_copy(
                            blocks_hbm.at[leaf, 0], blocks.at[leaf, n], sems.at[leaf, n]
                        ).wait()
                total_ref[leaf] = total_ref[leaf] + (term(first) + term(first + 1))


def near_kernel(
    index_ref, blocks_hbm, own_ref, share_ref,
    near_ref,
    blocks, panels, order, block_sems, panel_sems,
):
    leaves, _, rows, _ = blocks.shape
    size = leaves * rows
    pairs = [
        pltpu.make_async_copy(
            ref.at[pl.ds(0, size)], panels.at[pl.ds(which * size, size)], panel_sems.at[which]
        )
        for which, ref in enumerate((own_ref, share_ref))
    ]
    for copy in pairs:
        copy.start()
    found = pick_slots(index_ref, blocks_hbm, blocks, block_sems, order, 0, 2 * leaves)
    near_ref[...] = jnp.zeros(near_ref.shape, near_ref.dtype)
    panels[pl.ds(2 * size, rows), :] = jnp.zeros((rows, panels.shape[1]), panels.dtype)
    for copy in pairs:
        copy.wait()
    add_slots(near_ref, blocks_hbm, blocks, block_sems, order, found, panels)


def across_kernel(
    index_ref, blocks_hbm, near_ref, across_ref,
    total_ref,
    blocks, panels, order, block_sems, panel_sems,
):
    leaves, _, rows, _ = blocks.shape
    size = leaves * rows
    copy = pltpu.make_async_copy(across_ref, panels.at[pl.ds(0, size)], panel_sems.at[0])
    copy.start()
    found = pick_slots(
        index_ref, blocks_hbm, blocks, block_sems, order, 2 * leaves, 3 * leaves
    )
    total_ref[...] = near_ref[...]
    panels[pl.ds(size, rows), :] = jnp.zeros((rows, panels.shape[1]), panels.dtype)
    copy.wait()
    add_slots(total_ref, blocks_hbm, blocks, block_sems, order, found, panels)


def far_kernel(
    list_ref, coarse_list_ref, coupling_ref, coarse_coupling_ref,
    level_ref, layer_ref, share_ref, passed_ref, column_ref, beside_ref, their_column_ref,
    far_ref, coarse_ref, weight_ref,
    coefs, sems,
):
    leaves, slots, rank, _ = coupling_ref.shape
    size = leaves * rank
    place = lax.axis_index("row")
    beyond = jnp.where((place & 2) == 0, place - 2, place + 2)
    copies = [
        pltpu.make_async_copy(
            ref.at[pl.ds(ref.shape[0] - size, size)], coefs.at[pl.ds(n * size, size)], sems.at[n]
        )
        for n, ref in enumerate((level_ref, layer_ref, share_ref, passed_ref))
    ]
    for copy in copies:
        copy.start()
    local = place & (GROUP - 1)
    unused, their_unused = unused_layer(local), unused_layer(local ^ 1)
    weights = [jnp.zeros((rank, rank), jnp.float32)] * (GROUP // 4 - 1)
    terms = []
    for slot in range(coarse_list_ref.shape[1]):
        flip = (coarse_list_ref[0, slot] & (GROUP - 1)) ^ local
        layer = flip >> 2
        late = (flip & 3) == 3

        def gap(skipped):
            return jnp.minimum(jnp.where(layer > skipped, layer - 1, layer), GROUP // 4 - 2)

        here = rows_at(layer, rank)
        mine = jnp.where(
            (flip & 2) == 0, column_ref[here, :], beside_ref[rows_at(gap(unused), rank), :]
        )
        panel = jnp.where((flip & 1) == 0, mine, their_column_ref[here, :])
        block = coarse_coupling_ref[0, slot]
        terms.append(dot(block, jnp.where(late, jnp.zeros_like(panel), panel)))
        wide = block.astype(jnp.float32)
        weights = [
            total + jnp.where(late & (gap(their_unused) == n), wide, jnp.zeros_like(wide))
            for n, total in enumerate(weights)
        ]
    while len(terms) > 1:
        terms = [first + second for first, second in zip(terms[::2], terms[1::2])]
    coarse_ref[...] = terms[0]
    for n, total in enumerate(weights):
        high = total.astype(jnp.bfloat16)
        weight_ref[:, pl.ds(2 * n * rank, rank)] = high
        weight_ref[:, pl.ds((2 * n + 1) * rank, rank)] = (
            total - high.astype(jnp.float32)
        ).astype(jnp.bfloat16)
    for copy in copies:
        copy.wait()

    def panel_of(leaf, slot):
        column = list_ref[leaf, slot]
        cluster = lax.div(column, leaves)
        which = jnp.where(
            cluster == (place ^ 2), 0,
            jnp.where(cluster == beyond, 1, jnp.where(cluster == (place ^ 1), 2, 3)),
        )
        return coefs[rows_at(which * leaves + column - cluster * leaves, rank), :]

    for leaf in range(leaves):
        total = None
        for slot in range(0, slots, 2):
            both = jnp.concatenate([coupling_ref[leaf, slot], coupling_ref[leaf, slot + 1]], axis=1)
            panels = jnp.concatenate([panel_of(leaf, slot), panel_of(leaf, slot + 1)], axis=0)
            term = dot(both, panels)
            total = term if total is None else total + term
        far_ref[pl.ds(leaf * rank, rank), :] = total


def down_kernel(
    transfer_ref, row_ref, near_ref, far_ref, coarse_ref, weight_ref, their_beside_ref,
    out_hbm,
    out, sems,
):
    leaves, rows, rank = row_ref.shape
    panels = [their_beside_ref[pl.ds(n * rank, rank), :] for n in range(GROUP // 4 - 1)]
    stack = jnp.concatenate([panel for panel in panels for _ in range(2)], axis=0)
    coarse = coarse_ref[...] + dot(weight_ref[...], stack)
    high = coarse.astype(jnp.bfloat16)
    low = (coarse - high.astype(jnp.float32)).astype(jnp.bfloat16)
    matrix = transfer_ref[...].reshape(leaves * rank, rank)
    spread = dot(
        jnp.concatenate([matrix, matrix], axis=1), jnp.concatenate([high, low], axis=0)
    )
    down = (far_ref[...] + spread).astype(jnp.bfloat16)
    copies = []
    for leaf in range(leaves):
        result = near_ref[leaf] + dot(row_ref[leaf], down[leaf * rank:(leaf + 1) * rank])
        here = pl.ds(leaf * rows, rows)
        out[here, :] = result.astype(jnp.bfloat16)
        copies.append(pltpu.make_async_copy(out.at[here], out_hbm.at[here], sems.at[leaf]))
        copies[-1].start()
    for copy in copies:
        copy.wait()


def call(kernel, name, outs, specs, args, scratch=(), flops=0, moved=0, limit=4, to=VMEM):
    many = isinstance(outs, tuple)
    return pl.pallas_call(
        kernel,
        out_shape=outs,
        in_specs=specs,
        out_specs=(to,) * len(outs) if many else to,
        scratch_shapes=list(scratch),
        cost_estimate=pl.CostEstimate(flops=flops, bytes_accessed=moved, transcendentals=0),
        compiler_params=pltpu.CompilerParams(vmem_limit_bytes=limit * MIB),
        name=name,
    )(*args)


def body(
    source,
    near_blocks,
    near_list,
    near_count,
    col_basis,
    row_basis,
    transfer,
    far_list,
    far_coupling,
    coarse_list,
    coarse_coupling,
):
    leaves, slots, rows, _ = near_blocks.shape
    rank = col_basis.shape[2]
    width = source.shape[1]
    count = lax.axis_size("row")
    far_slots = far_coupling.shape[1]

    def send(value, target):
        pairs = [(d, target(d)) for d in range(count) if 0 <= target(d) < count]
        return lax.ppermute(value, "row", pairs)

    def panel(blocks, dtype=jnp.bfloat16):
        return jax.ShapeDtypeStruct((blocks * rank, width), dtype)

    own, coef = call(
        coef_kernel, "coef",
        (jax.ShapeDtypeStruct(source.shape, jnp.bfloat16), panel(leaves)),
        [VMEM] * 2, (source, col_basis),
        flops=2 * leaves * rank * width * rows,
        moved=2 * leaves * rows * (width + rank), limit=8,
    )
    parent = call(parent_kernel, "parent", panel(1), [VMEM] * 2, (coef, transfer))
    layers = [send(parent, lambda d, bit=bit: d ^ bit) for bit in (4, 8, 12)]
    source_other = send(source, lambda d: d ^ 1)
    level = send(coef, lambda d: d ^ 2)
    panels = call(
        hand_kernel, "panels", jax.ShapeDtypeStruct(source.shape, jnp.bfloat16), [VMEM] + [ANY] * 1,
        (own, source_other),
    )
    across = send(panels, lambda d: d + 1 if d & 1 else d - 1)

    place = lax.axis_index("row")
    live = lax.broadcasted_iota(jnp.int32, (leaves, slots), 1) < near_count[:, None]
    which = jnp.minimum((near_list // leaves) ^ place, 2)
    index = jnp.where(live, which * leaves + near_list % leaves, 3 * leaves)
    def slots_scratch(panels):
        return [
            pltpu.VMEM(near_blocks.shape, jnp.bfloat16),
            pltpu.VMEM((panels * rows, width), jnp.bfloat16),
            pltpu.SMEM((leaves, slots + CHUNK), jnp.int32),
            pltpu.SemaphoreType.DMA((leaves, slots)),
            pltpu.SemaphoreType.DMA((2,)),
        ]

    shape = jax.ShapeDtypeStruct((leaves, rows, width), jnp.float32)
    near = call(
        near_kernel, "near", shape, [SMEM] + [ANY] * 3,
        (index, near_blocks, panels, source_other),
        scratch=slots_scratch(2 * leaves + 1), flops=10**9, limit=48,
    )
    layer = send(level, lambda d: d - 4 if d & 2 else d + 4)
    column, sent = call(
        column_kernel, "column", (panel(GROUP // 4 + leaves), panel(GROUP // 4 - 1)),
        [VMEM] * 5 + [ANY], (parent, *layers, coef, near),
    )
    beside = send(sent, lambda d: d ^ 2)
    their_column = send(column, lambda d: d ^ 1)
    near = call(
        across_kernel, "across", shape, [SMEM, ANY, VMEM, ANY],
        (index, near_blocks, near, across),
        scratch=slots_scratch(leaves + 1), flops=0, limit=48,
    )
    picked_coef = call(
        pick_kernel, "pick", panel(leaves), [VMEM] * 2, (level, layer)
    )
    passed = send(picked_coef, lambda d: d ^ 1)
    handed = call(hand_kernel, "hand", panel(GROUP // 4 - 1), [VMEM, ANY], (beside, near))
    their_beside = send(handed, lambda d: d ^ 1)
    far, coarse, weight = call(
        far_kernel, "far",
        (
            panel(leaves, jnp.float32), panel(1, jnp.float32),
            jax.ShapeDtypeStruct((rank, 2 * (GROUP // 4 - 1) * rank), jnp.bfloat16),
        ),
        [SMEM] * 2 + [VMEM] * 2 + [ANY] * 4 + [VMEM] * 3,
        (
            far_list, coarse_list, far_coupling, coarse_coupling, level, layer, their_column,
            passed, column, handed, their_column,
        ),
        scratch=[
            pltpu.VMEM((4 * leaves * rank, width), jnp.bfloat16),
            pltpu.SemaphoreType.DMA((4,)),
        ],
        flops=2 * leaves * far_slots * rank * rank * width,
        moved=2 * leaves * far_slots * rank * rank, limit=10,
    )
    return call(
        down_kernel, "down", jax.ShapeDtypeStruct(source.shape, jnp.bfloat16),
        [VMEM] * 7, (transfer, row_basis, near, far, coarse, weight, their_beside),
        flops=8 * leaves * rank * rank * width,
        scratch=[
            pltpu.VMEM(source.shape, jnp.bfloat16),
            pltpu.SemaphoreType.DMA((leaves,)),
        ],
        moved=4 * leaves * rows * width, limit=8, to=ANY,
    )


def solution(mesh):
    placed = (
        P(("clip", "row"), None),
        P(("clip", "row"), None, None, None),
        P(("clip", "row"), None),
        P(("clip", "row")),
        P(("clip", "row"), None, None),
        P(("clip", "row"), None, None),
        P(("clip", "row"), None, None),
        P(("clip", "row"), None),
        P(("clip", "row"), None, None, None),
        P(("clip", "row"), None),
        P(("clip", "row"), None, None, None),
    )
    return jax.shard_map(
        body, mesh=mesh, in_specs=placed, out_specs=P(("clip", "row"), None), check_vma=False
    )
```
